32 devices in a mesh: groups: 2 (over y), seq: 4 (over z), head: 2 (over x), sub: 2 (over core).
Axes of the slice: x: 2, y: 2, z: 4, core: 2. Of those that a mesh axis runs over, the one named last changes fastest.
Arguments:
- queries: bfloat16 [4096, 4096], P(('groups', 'seq'), ('head', 'sub')), parts along dimension 0, may hold values from -33 to 33
- keys: bfloat16 [4096, 4096], P(('groups', 'seq'), ('head', 'sub')), parts along dimension 0, may hold values from -6 to 6
- values: bfloat16 [4096, 4096], P(('groups', 'seq'), ('head', 'sub')), parts along dimension 0, may hold values from -6 to 6
- latent_keys: bfloat16 [1024, 4096], P('groups', ('head', 'sub')), parts along dimension 0, may hold values from -6 to 6
- latent_values: bfloat16 [1024, 4096], P('groups', ('head', 'sub')), parts along dimension 0, may hold values from -6 to 6
- pattern: int32 [16, 8], P(('groups', 'seq')), parts along dimension 0, may hold values 0 or 1
- doc_starts: int32 [64], P('groups'), parts along dimension 0, may hold values from 0 to 2047, as said below
- doc_owner: int32 [64], P('groups'), parts along dimension 0, may hold values from 0 to 3, as said below
Outputs:
- context: bfloat16 [4096, 4096], P(('groups', 'seq'), ('head', 'sub')), parts along dimension 0
- pooled: bfloat16 [8, 4, 2, 4096], P(('groups', 'seq'), None, None, ('head', 'sub')), parts along dimension 0
The draws below stay inside these ranges and needn't reach their ends.
There are 2 independent parts, one for each index of `groups`. The reference program is written for one: setup_inputs(seed, part) draws one part's arguments, and reference() takes and returns one part's arrays. A program takes and returns all parts, laid end to end along the dimension named above; each array names one. Nothing has to cross between parts.
Inputs may be any that keep to these rules, and one draw needn't show every extreme that they name: `doc_starts`: document 2i starts at i * 128, the start of the i-th piece of 128 tokens, and document 2i + 1 starts 1 to 127 tokens later. `doc_owner`: documents 2i and 2i + 1 have one owner; the 4 pieces of one shard of 512 tokens have different owners; in every draw some owner owns a piece of every shard.
All inputs are finite; a program needn't handle non-finite values. No bound on the sum of `pattern` on one device may be relied on, other than what follows from the above.
Results may differ from the reference program's by a relative error of at most 0.0085.
Values may be sent and summed in bfloat16 or wider, within the bound.
No kernel may reach another device: no remote copies, remote signals or barrier semaphores. Data moves between devices by JAX's collectives and lax.ppermute only.
A program may use at most 128 MiB of HBM per device.

```python
import math
import jax
import jax.numpy as jnp
from jax import lax

HEADS = 32
HD = 128
D = 4096
LAT = 512
LEVELS = 4
BLK = 256
PIECES = 4
TOK_DEV = 512
TOKENS = 2048
CAP = 128
NQB = 8
SLOTS = 8
DOCS = 32
N_SEQ = 4


def draw_queries(key, part):
    sampled = jnp.clip(2.5 * jax.random.normal(jax.random.fold_in(key, 1), (TOKENS, D), jnp.float32), -12.0, 12.0)
    return sampled.astype(jnp.bfloat16)


def draw_keys(key, part):
    sampled = jnp.clip(jax.random.normal(jax.random.fold_in(key, 2), (TOKENS, D), jnp.float32), -6.0, 6.0)
    return sampled.astype(jnp.bfloat16)


def draw_latent_keys(key, part):
    sampled = jnp.clip(jax.random.normal(jax.random.fold_in(key, 3), (LAT, D), jnp.float32), -6.0, 6.0)
    return sampled.astype(jnp.bfloat16)


def piece_layout(key):
    shard_count = TOKENS // TOK_DEV
    owner_index = jnp.arange(shard_count, dtype=jnp.int32)
    hot_owners = jax.random.permutation(jax.random.fold_in(key, 21), shard_count)[:2].astype(jnp.int32)
    heated = jnp.any(owner_index[:, None] == hot_owners[None, :], axis=1).astype(jnp.int32)
    base_score = jax.random.randint(jax.random.fold_in(key, 22), (shard_count, shard_count), 0, 1000)
    owner_score = (base_score + 1000 * heated[None, :]) * shard_count + owner_index[None, :]
    chosen = lax.top_k(owner_score, PIECES)[1].astype(jnp.int32)
    order_score = jax.random.randint(jax.random.fold_in(key, 23), (shard_count, PIECES), 0, 1000) * PIECES + jnp.arange(PIECES, dtype=jnp.int32)[None, :]
    order_rank = jnp.argsort(order_score, axis=1)
    chosen = jnp.take_along_axis(chosen, order_rank, axis=1)
    splits = jax.random.randint(jax.random.fold_in(key, 24), (shard_count, PIECES), 1, CAP)
    return (chosen, splits.astype(jnp.int32))


def draw_doc_starts(key, part):
    chosen, splits = piece_layout(key)
    shard_count = TOKENS // TOK_DEV
    piece_start = (jnp.arange(shard_count, dtype=jnp.int32)[:, None] * TOK_DEV + jnp.arange(PIECES, dtype=jnp.int32)[None, :] * CAP).astype(jnp.int32)
    return jnp.stack((piece_start, piece_start + splits), axis=2).reshape(-1).astype(jnp.int32)


def draw_doc_owner(key, part):
    chosen, splits = piece_layout(key)
    return jnp.stack((chosen, chosen), axis=2).reshape(-1).astype(jnp.int32)


def place_ends(values, key, least, largest):
    extent = values.shape
    place = [jax.random.randint(jax.random.fold_in(key, axis), (), 0, extent[axis]) for axis in range(len(extent))]
    values = values.at[tuple(place)].set(least)
    longest = extent.index(max(extent))
    place[longest] = (place[longest] + 1) % extent[longest]
    return values.at[tuple(place)].set(largest)


def block_scale(stream_key, shape, shards, low, top_value):
    loudness = 1.0
    for dim, blocks in shards:
        steps = jax.random.uniform(jax.random.fold_in(jax.random.fold_in(stream_key, 6), dim), (blocks,), jnp.float32, low / len(shards), top_value / len(shards))
        loudness = loudness * jnp.repeat(jnp.exp(steps), shape[dim] // blocks).reshape((-1,) + (1,) * (len(shape) - 1 - dim))
    return loudness


def gaussian(rng, shape, deviation, most, cuts=(), kind=jnp.bfloat16):
    factor_of = block_scale(rng, shape, cuts, -0.22, 0.18) if cuts else 1.0
    drawn = jax.random.normal(rng, shape, jnp.float32) * deviation * factor_of
    return jnp.minimum(jnp.maximum(drawn, -most), most).astype(kind)


def setup_inputs(seed: int = 0, part: int = 0) -> dict:
    arg_keys = jax.random.split(jax.random.key(seed), 9)
    own_keys = jax.random.split(jax.random.fold_in(arg_keys[8], part), 9)
    queries = draw_queries(jax.random.fold_in(jax.random.fold_in(arg_keys[8], part), 71), part)
    keys = draw_keys(jax.random.fold_in(jax.random.fold_in(arg_keys[8], part), 71), part)
    values = gaussian(own_keys[2], (TOKENS, D), 1.0, 6.0, ((0, 4), (1, 4)))
    latent_keys = draw_latent_keys(jax.random.fold_in(jax.random.fold_in(arg_keys[8], part), 71), part)
    latent_values = gaussian(own_keys[4], (LAT, D), 1.0, 6.0, ((1, 4),))
    pattern = place_ends((jax.random.randint(own_keys[5], (NQB, SLOTS), 0, 4) < 3).astype(jnp.int32), jax.random.fold_in(own_keys[5], 1), 0, 1)
    doc_starts = draw_doc_starts(jax.random.fold_in(jax.random.fold_in(arg_keys[8], part), 71), part)
    doc_owner = draw_doc_owner(jax.random.fold_in(jax.random.fold_in(arg_keys[8], part), 71), part)
    return {"queries": queries, "keys": keys, "values": values, "latent_keys": latent_keys, "latent_values": latent_values, "pattern": pattern, "doc_starts": doc_starts, "doc_owner": doc_owner}


def latent_rows(query_rows, latent_keys, latent_values):
    score_scale = 1.0 / math.sqrt(HD)
    row_count = query_rows.shape[0]
    query_heads = query_rows.reshape(row_count, HEADS, HD).astype(jnp.float32)
    latent_heads = latent_keys.reshape(LAT, HEADS, HD).astype(jnp.float32)
    value_heads = latent_values.reshape(LAT, HEADS, HD).astype(jnp.float32)
    scores = jnp.einsum('qhd,lhd->hql', query_heads, latent_heads, precision=lax.Precision.HIGHEST) * score_scale
    row_peak = lax.optimization_barrier(jnp.max(scores, axis=2, keepdims=True))
    exp_terms = jnp.exp(scores - row_peak)
    totals = lax.optimization_barrier(jnp.sum(exp_terms, axis=2))
    weights = lax.optimization_barrier(exp_terms.astype(jnp.bfloat16)).astype(jnp.float32)
    blended = jnp.einsum('hql,lhd->qhd', weights, value_heads, precision=lax.Precision.HIGHEST)
    blended = blended / jnp.moveaxis(totals, 0, 1)[:, :, None]
    return blended.reshape(row_count, D)

def reference(queries, keys, values, latent_keys, latent_values, pattern, doc_starts, doc_owner):
    score_scale = 1.0 / math.sqrt(HD)
    per_shard = TOK_DEV // BLK
    all_blocks = TOKENS // BLK

    def one_block(block_index):
        shard_start = (block_index // per_shard * TOK_DEV).astype(jnp.int32)
        key_parts = [lax.dynamic_slice_in_dim(keys, shard_start, TOK_DEV, 0)]
        value_parts = [lax.dynamic_slice_in_dim(values, shard_start, TOK_DEV, 0)]
        mask_parts = [jnp.ones((TOK_DEV,), dtype=bool)]
        for level_index in range(LEVELS):
            for side_index in range(2):
                offset = per_shard * 2 ** level_index * (2 * side_index - 1)
                other_block = block_index + offset
                slot_live = (other_block >= 0) & (other_block < all_blocks) & (pattern[block_index, 2 * level_index + side_index] == 1)
                row_start = (jnp.clip(other_block, 0, all_blocks - 1) * BLK).astype(jnp.int32)
                key_parts.append(lax.dynamic_slice_in_dim(keys, row_start, BLK, 0))
                value_parts.append(lax.dynamic_slice_in_dim(values, row_start, BLK, 0))
                mask_parts.append(jnp.broadcast_to(slot_live, (BLK,)))
        key_all = jnp.concatenate(key_parts, axis=0)
        value_all = jnp.concatenate(value_parts, axis=0)
        mask_all = jnp.concatenate(mask_parts, axis=0)
        query_block = lax.dynamic_slice_in_dim(queries, (block_index * BLK).astype(jnp.int32), BLK, 0)
        query_heads = query_block.reshape(BLK, HEADS, HD).astype(jnp.float32)
        key_heads = key_all.reshape(-1, HEADS, HD).astype(jnp.float32)
        value_heads = value_all.reshape(-1, HEADS, HD).astype(jnp.float32)
        scores = jnp.einsum('qhd,khd->hqk', query_heads, key_heads, precision=lax.Precision.HIGHEST) * score_scale
        scores = jnp.where(mask_all[None, None, :], scores, -jnp.inf)
        row_peak = lax.optimization_barrier(jnp.max(scores, axis=2, keepdims=True))
        exp_terms = jnp.exp(scores - row_peak)
        totals = lax.optimization_barrier(jnp.sum(exp_terms, axis=2))
        weights = lax.optimization_barrier(exp_terms.astype(jnp.bfloat16)).astype(jnp.float32)
        output_rows = jnp.einsum('hqk,khd->qhd', weights, value_heads, precision=lax.Precision.HIGHEST)
        output_rows = output_rows / jnp.moveaxis(totals, 0, 1)[:, :, None]
        return output_rows.reshape(BLK, D).astype(jnp.bfloat16)
    context = lax.map(one_block, jnp.arange(all_blocks, dtype=jnp.int32)).reshape(TOKENS, D)

    def latent_block(operands):
        query_rows, context_rows = operands
        return latent_rows(query_rows, latent_keys, latent_values) + context_rows.astype(jnp.float32)
    mixed = lax.map(latent_block, (queries.reshape(N_SEQ, TOK_DEV, D), context.reshape(N_SEQ, TOK_DEV, D))).reshape(TOKENS, D)
    positions = jnp.arange(TOKENS, dtype=jnp.int32)
    doc_ids = lax.optimization_barrier(jnp.sum((doc_starts[None, :] <= positions[:, None]).astype(jnp.int32), axis=1)) - 1
    doc_totals = jax.ops.segment_sum(mixed, doc_ids, num_segments=DOCS)
    doc_counts = jax.ops.segment_sum(jnp.ones((TOKENS,), jnp.float32), doc_ids, num_segments=DOCS)
    embedding = doc_totals / doc_counts[:, None]
    owners = doc_owner.reshape(-1, 2)[:, 0].reshape(N_SEQ, PIECES)
    route_hits = (owners[None, :, :] == jnp.arange(N_SEQ, dtype=jnp.int32)[:, None, None]).astype(jnp.float32)
    pooled = jnp.einsum('rsp,spjc->rsjc', route_hits, embedding.reshape(N_SEQ, PIECES, 2, D), precision=lax.Precision.HIGHEST)
    return (context, pooled.astype(jnp.bfloat16))
```

```python
import functools
import math

import jax
import jax.numpy as jnp
from jax import lax
from jax.experimental import pallas as pl
from jax.experimental.pallas import tpu as pltpu
from jax.sharding import PartitionSpec as P

HD = 128
LEVELS = 4
BLK = 256
PIECES = 4
SCALE = math.log2(math.e) / math.sqrt(HD)
PARAMS = pltpu.CompilerParams(vmem_limit_bytes=40 * 1024 * 1024)
F32 = jnp.float32
BF16 = jnp.bfloat16


def dot_t(a, b):
    return lax.dot_general(a, b, (((1,), (1,)), ((), ())), preferred_element_type=F32)


def dot(a, b):
    return jnp.dot(a, b, preferred_element_type=F32)


def doc_rows(rows, split):
    place = lax.broadcasted_iota(jnp.int32, rows.shape, 0)
    first = jnp.sum(jnp.where(place < split, rows, 0.0), axis=0, keepdims=True)
    second = jnp.sum(jnp.where(place < split, 0.0, rows), axis=0, keepdims=True)
    return jnp.concatenate((first, second), axis=0)


def own_kernel(splits, q_ref, k_ref, v_ref, lk_ref, lv_ref, acc_ref, top_ref, sum_ref, lat_ref):
    q = q_ref[...]
    s = dot_t(q, k_ref[...]) * SCALE
    top = jnp.max(s, axis=1, keepdims=True)
    e = jnp.exp2(s - top)
    acc_ref[...] = dot(e.astype(BF16), v_ref[...])
    top_ref[...] = jnp.broadcast_to(top, top_ref.shape)
    sum_ref[...] = jnp.broadcast_to(jnp.sum(e, axis=1, keepdims=True), sum_ref.shape)
    s = dot_t(q, lk_ref[...]) * SCALE
    e = jnp.exp2(s - jnp.max(s, axis=1, keepdims=True))
    out = dot(e.astype(BF16), lv_ref[...]) / jnp.sum(e, axis=1, keepdims=True)
    piece = out.shape[0] // PIECES
    for p in range(PIECES):
        lat_ref[2 * p : 2 * p + 2, :] = doc_rows(out[p * piece : (p + 1) * piece], splits[p])


def slot_scores(live, q, keys, rows, block):
    scores = []
    for source, k_ref in enumerate(keys):
        s = dot_t(q, k_ref[rows, :]) * SCALE
        scores.append(jnp.where(live[source, block] == 1, s, -jnp.inf))
    return scores


def update_kernel(sources, live, q_ref, *refs):
    keys, vals = refs[:sources], refs[sources : 2 * sources]
    acc_in, top_in, sum_in, acc_ref, top_ref, sum_ref = refs[2 * sources :]
    for block in range(q_ref.shape[0] // BLK):
        rows = pl.ds(block * BLK, BLK)
        scores = slot_scores(live, q_ref[rows, :], keys, rows, block)
        old = top_in[rows, :1]
        top = old
        for s in scores:
            top = jnp.maximum(top, jnp.max(s, axis=1, keepdims=True))
        shrink = jnp.exp2(old - top)
        total = sum_in[rows, :1] * shrink
        acc = acc_in[rows, :] * shrink
        for s, v_ref in zip(scores, vals):
            e = jnp.exp2(s - top)
            total = total + jnp.sum(e, axis=1, keepdims=True)
            acc = acc + dot(e.astype(BF16), v_ref[rows, :])
        acc_ref[rows, :] = acc
        top_ref[rows, :] = jnp.broadcast_to(top, acc.shape)
        sum_ref[rows, :] = jnp.broadcast_to(total, acc.shape)


def weigh_kernel(sources, live, q_ref, *refs):
    keys = refs[:sources]
    acc_in, top_in, sum_in, acc_ref = refs[sources : sources + 4]
    outs = refs[sources + 4 :]
    for block in range(q_ref.shape[0] // BLK):
        rows = pl.ds(block * BLK, BLK)
        scores = slot_scores(live, q_ref[rows, :], keys, rows, block)
        old = top_in[rows, :1]
        top = old
        for s in scores:
            top = jnp.maximum(top, jnp.max(s, axis=1, keepdims=True))
        shrink = jnp.exp2(old - top)
        total = sum_in[rows, :1] * shrink
        exps = []
        for s in scores:
            e = jnp.exp2(s - top)
            total = total + jnp.sum(e, axis=1, keepdims=True)
            exps.append(e)
        inverse = 1.0 / total
        acc_ref[rows, :] = acc_in[rows, :] * (shrink * inverse)
        for e, out in zip(exps, outs):
            out[rows, :] = (e * inverse).astype(BF16)


def finish_kernel(sources, shards, splits, places, acc_ref, lat_ref, *refs):
    weights, vals = refs[:sources], refs[sources : 2 * sources]
    ctx_ref = refs[2 * sources]
    outs = refs[2 * sources + 1 :]
    rows_here = acc_ref.shape[0]
    piece = rows_here // PIECES
    parts = []
    for block in range(rows_here // BLK):
        rows = pl.ds(block * BLK, BLK)
        acc = acc_ref[rows, :]
        for w_ref, v_ref in zip(weights, vals):
            acc = acc + dot(w_ref[rows, :], v_ref[rows, :])
        ctx = acc.astype(BF16)
        ctx_ref[rows, :] = ctx
        ctx = ctx.astype(F32)
        for start in range(0, BLK, piece):
            parts.append(ctx[start : start + piece])
    means = []
    side = lax.broadcasted_iota(jnp.int32, (2, HD), 0)
    for p in range(PIECES):
        count = jnp.where(side == 0, splits[p], piece - splits[p]).astype(F32)
        means.append((doc_rows(parts[p], splits[p]) + lat_ref[2 * p : 2 * p + 2, :]) / count)
    for r in range(shards):
        chosen = jnp.zeros((2, HD), F32)
        for p in range(PIECES):
            chosen = jnp.where(places[p] == r, means[p], chosen)
        chosen = chosen.astype(BF16)
        if len(outs) == 1:
            outs[0][r] = chosen
        else:
            outs[r][...] = chosen


def spec(rows, columns=HD):
    return pl.BlockSpec((rows, columns), lambda h: (0, h))


def smem():
    return pl.BlockSpec(memory_space=pltpu.SMEM)


def shape(rows, columns, kind=F32):
    return jax.ShapeDtypeStruct((rows, columns), kind)


def shift(value, pairs):
    return lax.ppermute(value, "seq", pairs)


def body(queries, keys, values, latent_keys, latent_values, pattern, doc_starts, doc_owner):
    rows, columns = queries.shape
    heads = columns // HD
    seq_index = lax.axis_index("seq")
    seq_count = lax.axis_size("seq")
    blocks = rows // BLK
    levels = [j for j in range(LEVELS) if 2**j < seq_count]

    def both_ways(value, distance):
        behind = shift(value, [(s, s + distance) for s in range(seq_count - distance)])
        ahead = shift(value, [(s, s - distance) for s in range(distance, seq_count)])
        return [behind, ahead]

    def live_flags(level, merged):
        distance = 2**level
        flags = []
        for side, partner in ((0, seq_index - distance), (1, seq_index + distance)):
            inside = (partner >= 0) & (partner < seq_count)
            flags.append((pattern[:, 2 * level + side] == 1) & inside)
        if merged:
            return jnp.where(seq_index >= distance, flags[0], flags[1])[None].astype(jnp.int32)
        return jnp.stack(flags).astype(jnp.int32)

    last = levels[-1]
    merged = 2 * 2**last >= seq_count
    near_keys = both_ways(keys, 1)
    near_vals = both_ways(values, 1)

    def far(value, near):
        distance = 2**last
        if not merged:
            return both_ways(value, distance)
        if seq_count == 4:
            sent = jnp.where(seq_index == 2, near[0], jnp.where(seq_index == 1, near[1], value))
            return [shift(sent, [(0, 2), (3, 1), (2, 3), (1, 0)])]
        pairs = [(s, s + distance) for s in range(seq_count - distance)]
        pairs += [(s, s - distance) for s in range(distance, seq_count)]
        return [shift(value, pairs)]

    my_pieces = lax.dynamic_index_in_dim(doc_starts.reshape(seq_count, PIECES, 2), seq_index, 0, keepdims=False)
    splits = my_pieces[:, 1] - my_pieces[:, 0]
    owners = lax.dynamic_index_in_dim(doc_owner.reshape(seq_count, PIECES, 2), seq_index, 0, keepdims=False)[:, 0]
    rotate = seq_count <= 4
    places = lax.rem(owners - seq_index + seq_count, seq_count) if rotate else owners

    state_shapes = (shape(rows, columns),) * 3
    acc, top, total, lat = pl.pallas_call(
        own_kernel,
        grid=(heads,),
        in_specs=[smem()] + [spec(rows)] * 3 + [spec(latent_keys.shape[0])] * 2,
        out_specs=[spec(rows)] * 3 + [spec(2 * PIECES)],
        out_shape=state_shapes + (shape(2 * PIECES, columns),),
        compiler_params=PARAMS,
        cost_estimate=pl.CostEstimate(
            flops=8 * rows * columns * rows, bytes_accessed=12 * rows * columns * 2, transcendentals=2 * heads * rows * rows
        ),
        name="own",
    )(splits, queries, keys, values, latent_keys, latent_values)

    state = (acc, top, total)
    for level in levels[:-1]:
        if level == 0:
            got_keys, got_vals = near_keys, near_vals
        else:
            got_keys, got_vals = both_ways(keys, 2**level), both_ways(values, 2**level)
        sources = len(got_keys)
        first = 2 + 2 * sources
        state = pl.pallas_call(
            functools.partial(update_kernel, sources),
            grid=(heads,),
            in_specs=[smem()] + [spec(rows)] * (4 + 2 * sources),
            out_specs=[spec(rows)] * 3,
            out_shape=state_shapes,
            input_output_aliases={first + i: i for i in range(3)},
            compiler_params=PARAMS,
            cost_estimate=pl.CostEstimate(
                flops=4 * sources * rows * columns * BLK,
                bytes_accessed=(12 + 4 * sources) * rows * columns * 2,
                transcendentals=sources * heads * rows * BLK,
            ),
            name="near",
        )(live_flags(level, False), queries, *got_keys, *got_vals, *state)

    far_keys = far(keys, near_keys)
    far_vals = far(values, near_vals)
    sources = len(far_keys)
    acc, *weights = pl.pallas_call(
        functools.partial(weigh_kernel, sources),
        grid=(heads,),
        in_specs=[smem()] + [spec(rows)] * (4 + sources),
        out_specs=[spec(rows)] + [spec(rows, BLK)] * sources,
        out_shape=(shape(rows, columns),) + (shape(rows, heads * BLK, BF16),) * sources,
        input_output_aliases={2 + sources: 0},
        compiler_params=PARAMS,
        cost_estimate=pl.CostEstimate(
            flops=2 * sources * rows * columns * BLK,
            bytes_accessed=(10 + 3 * sources) * rows * columns * 2,
            transcendentals=sources * heads * rows * BLK,
        ),
        name="weigh",
    )(live_flags(last, merged), queries, *far_keys, *state)

    if rotate:
        out_specs = [pl.BlockSpec((2, HD), lambda h: (0, h))] * seq_count
        out_shapes = (shape(2, columns, BF16),) * seq_count
    else:
        out_specs = [pl.BlockSpec((seq_count, 2, HD), lambda h: (0, 0, h))]
        out_shapes = (jax.ShapeDtypeStruct((seq_count, 2, columns), BF16),)
    context, *means = pl.pallas_call(
        functools.partial(finish_kernel, sources, seq_count),
        grid=(heads,),
        in_specs=[smem()] * 2 + [spec(rows), spec(2 * PIECES)] + [spec(rows, BLK)] * sources + [spec(rows)] * sources,
        out_specs=[spec(rows)] + out_specs,
        out_shape=(shape(rows, columns, BF16),) + out_shapes,
        compiler_params=PARAMS,
        cost_estimate=pl.CostEstimate(
            flops=2 * sources * rows * columns * BLK, bytes_accessed=(3 + 3 * sources) * rows * columns * 2, transcendentals=0
        ),
        name="finish",
    )(splits, places, acc, lat, *weights, *far_vals)

    if not rotate:
        return context, lax.all_to_all(means[0], "seq", split_axis=0, concat_axis=0, tiled=True)[None]
    got = [means[0]]
    for r in range(1, seq_count):
        got.append(shift(means[r], [(s, (s + r) % seq_count) for s in range(seq_count)]))
    pooled = []
    for s in range(seq_count):
        back = lax.rem(seq_index - s + seq_count, seq_count)
        row = got[0]
        for r in range(1, seq_count):
            row = jnp.where(back == r, got[r], row)
        pooled.append(row)
    return context, jnp.stack(pooled)[None]


def solution(mesh):
    in_specs = (
        P(("groups", "seq"), ("head", "sub")),
        P(("groups", "seq"), ("head", "sub")),
        P(("groups", "seq"), ("head", "sub")),
        P("groups", ("head", "sub")),
        P("groups", ("head", "sub")),
        P(("groups", "seq"), None),
        P("groups"),
        P("groups"),
    )
    out_specs = (
        P(("groups", "seq"), ("head", "sub")),
        P(("groups", "seq"), None, None, ("head", "sub")),
    )
    return jax.shard_map(body, mesh=mesh, in_specs=in_specs, out_specs=out_specs, check_vma=False)
```

```python
import functools
import math

import jax
import jax.numpy as jnp
from jax import lax
from jax.experimental import pallas as pl
from jax.experimental.pallas import tpu as pltpu
from jax.sharding import PartitionSpec as P

HD = 128
LEVELS = 4
BLK = 256
PIECES = 4
SCALE = math.log2(math.e) / math.sqrt(HD)
PARAMS = pltpu.CompilerParams(vmem_limit_bytes=40 * 1024 * 1024)
F32 = jnp.float32
BF16 = jnp.bfloat16


def dot_t(a, b):
    return lax.dot_general(a, b, (((1,), (1,)), ((), ())), preferred_element_type=F32)


def dot(a, b):
    return jnp.dot(a, b, preferred_element_type=F32)


def doc_rows(rows, split):
    place = lax.broadcasted_iota(jnp.int32, rows.shape, 0)
    first = jnp.sum(jnp.where(place < split, rows, 0.0), axis=0, keepdims=True)
    second = jnp.sum(jnp.where(place < split, 0.0, rows), axis=0, keepdims=True)
    return jnp.concatenate((first, second), axis=0)


def own_kernel(where, starts, q_ref, k_ref, v_ref, lk_ref, lv_ref, acc_ref, top_ref, sum_ref, lat_ref):
    q = q_ref[...]
    s = dot_t(q, k_ref[...]) * SCALE
    top = jnp.max(s, axis=1, keepdims=True)
    e = jnp.exp2(s - top)
    acc_ref[...] = dot(e.astype(BF16), v_ref[...])
    top_ref[...] = jnp.broadcast_to(top, top_ref.shape)
    sum_ref[...] = jnp.broadcast_to(jnp.sum(e, axis=1, keepdims=True), sum_ref.shape)
    s = dot_t(q, lk_ref[...]) * SCALE
    e = jnp.exp2(s - jnp.max(s, axis=1, keepdims=True))
    out = dot(e.astype(BF16), lv_ref[...]) / jnp.sum(e, axis=1, keepdims=True)
    piece = out.shape[0] // PIECES
    for p in range(PIECES):
        split = split_of(where, starts, p)
        lat_ref[2 * p : 2 * p + 2, :] = doc_rows(out[p * piece : (p + 1) * piece], split)


def split_of(where, starts, p):
    first = 2 * (PIECES * where[0] + p)
    return starts[first + 1] - starts[first]


def slot_live(where, pattern, shards, level, side, block):
    partner = where[0] + (2 * side - 1) * 2**level
    return (pattern[block, 2 * level + side] == 1) & (partner >= 0) & (partner < shards)


def live_scores(live, q, k):
    return jnp.where(live, dot_t(q, k) * SCALE, -jnp.inf)


def near_kernel(shards, level, where, pattern, q_ref, kb_ref, ka_ref, vb_ref, va_ref, *refs):
    acc_in, top_in, sum_in, acc_ref, top_ref, sum_ref = refs
    for block in range(q_ref.shape[0] // BLK):
        rows = pl.ds(block * BLK, BLK)
        q = q_ref[rows, :]
        scores = [
            live_scores(slot_live(where, pattern, shards, level, side, block), q, k_ref[rows, :])
            for side, k_ref in enumerate((kb_ref, ka_ref))
        ]
        old = top_in[rows, :1]
        top = old
        for s in scores:
            top = jnp.maximum(top, jnp.max(s, axis=1, keepdims=True))
        shrink = jnp.exp2(old - top)
        total = sum_in[rows, :1] * shrink
        acc = acc_in[rows, :] * shrink
        for s, v_ref in zip(scores, (vb_ref, va_ref)):
            e = jnp.exp2(s - top)
            total = total + jnp.sum(e, axis=1, keepdims=True)
            acc = acc + dot(e.astype(BF16), v_ref[rows, :])
        acc_ref[rows, :] = acc
        top_ref[rows, :] = jnp.broadcast_to(top, acc.shape)
        sum_ref[rows, :] = jnp.broadcast_to(total, acc.shape)


def far_kernel(shards, level, merged, where, pattern, q_ref, kb_ref, ka_ref, acc_in, top_in, sum_in, acc_ref, *outs):
    behind = where[0] >= 2**level
    for block in range(q_ref.shape[0] // BLK):
        rows = pl.ds(block * BLK, BLK)
        q = q_ref[rows, :]
        live = [slot_live(where, pattern, shards, level, side, block) for side in range(2)]
        pair = [k_ref[rows, :] for k_ref in (kb_ref, ka_ref)]
        if merged:
            live = [(behind & live[0]) | (jnp.logical_not(behind) & live[1])]
            pair = [jnp.where(behind, pair[0], pair[1])]
        scores = [live_scores(on, q, k) for on, k in zip(live, pair)]
        old = top_in[rows, :1]
        top = old
        for s in scores:
            top = jnp.maximum(top, jnp.max(s, axis=1, keepdims=True))
        shrink = jnp.exp2(old - top)
        total = sum_in[rows, :1] * shrink
        exps = []
        for s in scores:
            e = jnp.exp2(s - top)
            total = total + jnp.sum(e, axis=1, keepdims=True)
            exps.append(e)
        inverse = 1.0 / total
        acc_ref[rows, :] = acc_in[rows, :] * (shrink * inverse)
        for e, out in zip(exps, outs):
            out[rows, :] = (e * inverse).astype(BF16)


def finish_kernel(shards, level, merged, where, starts, owners, acc_ref, lat_ref, *refs):
    sources = 1 if merged else 2
    weights, (vb_ref, va_ref) = refs[:sources], refs[sources : sources + 2]
    ctx_ref, outs = refs[sources + 2], refs[sources + 3 :]
    rows_here, columns = acc_ref.shape
    piece = rows_here // PIECES
    splits = [split_of(where, starts, p) for p in range(PIECES)]
    behind = where[0] >= 2**level
    sums = []
    for h in range(columns // HD):
        head = pl.ds(h * HD, HD)
        slots = pl.ds(h * BLK, BLK)
        found = []
        for block in range(rows_here // BLK):
            rows = pl.ds(block * BLK, BLK)
            pair = [v_ref[rows, head] for v_ref in (vb_ref, va_ref)]
            if merged:
                pair = [jnp.where(behind, pair[0], pair[1])]
            acc = acc_ref[rows, head]
            for w_ref, v in zip(weights, pair):
                acc = acc + dot(w_ref[rows, slots], v)
            ctx = acc.astype(BF16)
            ctx_ref[rows, head] = ctx
            ctx = ctx.astype(F32)
            for start in range(0, BLK, piece):
                found.append(doc_rows(ctx[start : start + piece], splits[len(found)]))
        sums.append(found)
    side = lax.broadcasted_iota(jnp.int32, (2, columns), 0)
    means = []
    for p in range(PIECES):
        count = jnp.where(side == 0, splits[p], piece - splits[p]).astype(F32)
        total = jnp.concatenate([found[p] for found in sums], axis=1) + lat_ref[2 * p : 2 * p + 2, :]
        means.append(total / count)
    for r in range(shards):
        if len(outs) == 1:
            target = r
        else:
            target = lax.rem(where[0] + r, shards)
        chosen = jnp.zeros((2, columns), F32)
        for p in range(PIECES):
            chosen = jnp.where(owners[2 * (PIECES * where[0] + p)] == target, means[p], chosen)
        if len(outs) == 1:
            outs[0][r] = chosen.astype(BF16)
        else:
            outs[r][...] = chosen.astype(BF16)


def spec(rows, columns=HD):
    return pl.BlockSpec((rows, columns), lambda h: (0, h))


def smem(count):
    return [pl.BlockSpec(memory_space=pltpu.SMEM)] * count


def vmem(count):
    return [pl.BlockSpec(memory_space=pltpu.VMEM)] * count


def shape(rows, columns, kind=F32):
    return jax.ShapeDtypeStruct((rows, columns), kind)


def body(queries, keys, values, latent_keys, latent_values, pattern, doc_starts, doc_owner):
    rows, columns = queries.shape
    heads = columns // HD
    shards = lax.axis_size("seq")
    seq_index = lax.axis_index("seq")
    where = seq_index.astype(jnp.int32).reshape(1)
    levels = [j for j in range(LEVELS) if 2**j < shards]
    last = levels[-1]
    merged = 2 * 2**last >= shards
    rotate = shards <= 4

    def both_ways(value, distance):
        behind = lax.ppermute(value, "seq", [(s, s + distance) for s in range(shards - distance)])
        ahead = lax.ppermute(value, "seq", [(s, s - distance) for s in range(distance, shards)])
        return [behind, ahead]

    def far(value, near):
        if last != 1:
            return both_ways(value, 2**last)
        behind = lax.ppermute(near[0], "seq", [(s, s + 1) for s in range(1, shards - 1)])
        ahead = lax.ppermute(near[1], "seq", [(s, s - 1) for s in range(1, shards - 1)])
        return [behind, ahead]

    near_keys = both_ways(keys, 1)
    near_vals = both_ways(values, 1)
    state_shapes = (shape(rows, columns),) * 3
    *state, lat = pl.pallas_call(
        own_kernel,
        grid=(heads,),
        in_specs=smem(2) + [spec(rows)] * 3 + [spec(latent_keys.shape[0])] * 2,
        out_specs=[spec(rows)] * 3 + [spec(2 * PIECES)],
        out_shape=state_shapes + (shape(2 * PIECES, columns),),
        compiler_params=PARAMS,
        cost_estimate=pl.CostEstimate(
            flops=8 * rows * columns * rows, bytes_accessed=12 * rows * columns * 2, transcendentals=2 * heads * rows * rows
        ),
        name="own",
    )(where, doc_starts, queries, keys, values, latent_keys, latent_values)
    near_keys, state = lax.optimization_barrier((near_keys, state))

    for level in levels[:-1]:
        if level == 0:
            got = near_keys + near_vals
        else:
            got = both_ways(keys, 2**level) + both_ways(values, 2**level)
        state = pl.pallas_call(
            functools.partial(near_kernel, shards, level),
            grid=(heads,),
            in_specs=smem(2) + [spec(rows)] * 8,
            out_specs=[spec(rows)] * 3,
            out_shape=state_shapes,
            input_output_aliases={7 + i: i for i in range(3)},
            compiler_params=PARAMS,
            cost_estimate=pl.CostEstimate(
                flops=8 * rows * columns * BLK, bytes_accessed=20 * rows * columns * 2, transcendentals=2 * heads * rows * BLK
            ),
            name="near",
        )(where, pattern, queries, *got, *state)

    far_keys = far(keys, near_keys)
    far_vals = far(values, near_vals)
    sources = 1 if merged else 2
    acc, *weights = pl.pallas_call(
        functools.partial(far_kernel, shards, last, merged),
        grid=(heads,),
        in_specs=smem(2) + [spec(rows)] * 6,
        out_specs=[spec(rows)] + [spec(rows, BLK)] * sources,
        out_shape=(shape(rows, columns),) + (shape(rows, heads * BLK, BF16),) * sources,
        input_output_aliases={5: 0},
        compiler_params=PARAMS,
        cost_estimate=pl.CostEstimate(
            flops=2 * sources * rows * columns * BLK,
            bytes_accessed=(10 + 3 * sources) * rows * columns * 2,
            transcendentals=sources * heads * rows * BLK,
        ),
        name="far",
    )(where, pattern, queries, *far_keys, *state)

    if rotate:
        sent = (shape(2, columns, BF16),) * shards
    else:
        sent = (jax.ShapeDtypeStruct((shards, 2, columns), BF16),)
    context, *means = pl.pallas_call(
        functools.partial(finish_kernel, shards, last, merged),
        in_specs=smem(3) + vmem(4 + sources),
        out_specs=vmem(1 + len(sent)),
        out_shape=(shape(rows, columns, BF16),) + sent,
        compiler_params=PARAMS,
        cost_estimate=pl.CostEstimate(
            flops=2 * sources * rows * columns * BLK, bytes_accessed=(3 + 3 * sources) * rows * columns * 2, transcendentals=0
        ),
        name="finish",
    )(where, doc_starts, doc_owner, acc, lat, *weights, *far_vals)

    if not rotate:
        return context, lax.all_to_all(means[0], "seq", split_axis=0, concat_axis=0, tiled=True)[None]
    got = [means[0]]
    for r in range(1, shards):
        got.append(lax.ppermute(means[r], "seq", [(s, (s + r) % shards) for s in range(shards)]))
    pooled = []
    for s in range(shards):
        back = lax.rem(seq_index - s + shards, shards)
        row = got[0]
        for r in range(1, shards):
            row = jnp.where(back == r, got[r], row)
        pooled.append(row)
    return context, jnp.stack(pooled)[None]


def solution(mesh):
    in_specs = (
        P(("groups", "seq"), ("head", "sub")),
        P(("groups", "seq"), ("head", "sub")),
        P(("groups", "seq"), ("head", "sub")),
        P("groups", ("head", "sub")),
        P("groups", ("head", "sub")),
        P(("groups", "seq"), None),
        P("groups"),
        P("groups"),
    )
    out_specs = (
        P(("groups", "seq"), ("head", "sub")),
        P(("groups", "seq"), None, None, ("head", "sub")),
    )
    return jax.shard_map(body, mesh=mesh, in_specs=in_specs, out_specs=out_specs, check_vma=False)
```

```python
import functools
import math

import jax
import jax.numpy as jnp
from jax import lax
from jax.experimental import pallas as pl
from jax.experimental.pallas import tpu as pltpu
from jax.sharding import PartitionSpec as P

HD = 128
LEVELS = 4
BLK = 256
PIECES = 4
SCALE = math.log2(math.e) / math.sqrt(HD)
PARAMS = pltpu.CompilerParams(vmem_limit_bytes=24 * 1024 * 1024)
F32 = jnp.float32
BF16 = jnp.bfloat16


def dot_t(a, b):
    return lax.dot_general(a, b, (((1,), (1,)), ((), ())), preferred_element_type=F32)


def dot(a, b):
    return jnp.dot(a, b, preferred_element_type=F32)


def doc_rows(rows, split):
    place = lax.broadcasted_iota(jnp.int32, rows.shape, 0)
    first = jnp.sum(jnp.where(place < split, rows, 0.0), axis=0, keepdims=True)
    second = jnp.sum(jnp.where(place < split, 0.0, rows), axis=0, keepdims=True)
    return jnp.concatenate((first, second), axis=0)


def own_kernel(q_ref, k_ref, v_ref, acc_ref, top_ref, sum_ref):
    for h in range(q_ref.shape[1] // HD):
        head = slice(h * HD, (h + 1) * HD)
        s = dot_t(q_ref[:, head], k_ref[:, head]) * SCALE
        top = jnp.max(s, axis=1, keepdims=True)
        e = jnp.exp2(s - top)
        acc = dot(e.astype(BF16), v_ref[:, head])
        acc_ref[:, head] = acc
        top_ref[:, head] = jnp.broadcast_to(top, acc.shape)
        sum_ref[:, head] = jnp.broadcast_to(jnp.sum(e, axis=1, keepdims=True), acc.shape)


def latent_kernel(where, starts, q_ref, lk_ref, lv_ref, lat_ref):
    for h in range(q_ref.shape[1] // HD):
        head = slice(h * HD, (h + 1) * HD)
        s = dot_t(q_ref[:, head], lk_ref[:, head]) * SCALE
        e = jnp.exp2(s - jnp.max(s, axis=1, keepdims=True))
        out = dot(e.astype(BF16), lv_ref[:, head]) / jnp.sum(e, axis=1, keepdims=True)
        piece = out.shape[0] // PIECES
        for p in range(PIECES):
            split = split_of(where, starts, p)
            lat_ref[2 * p : 2 * p + 2, head] = doc_rows(out[p * piece : (p + 1) * piece], split)


def split_of(where, starts, p, shard=None):
    first = 2 * (PIECES * (where[0] if shard is None else shard) + p)
    return starts[first + 1] - starts[first]


def slot_live(where, pattern, shards, level, side, block):
    partner = where[0] + (2 * side - 1) * 2**level
    return (pattern[block, 2 * level + side] == 1) & (partner >= 0) & (partner < shards)


def live_scores(live, q, k):
    return jnp.where(live, dot_t(q, k) * SCALE, -jnp.inf)


def near_kernel(shards, level, where, pattern, q_ref, kb_ref, ka_ref, vb_ref, va_ref, *refs):
    acc_in, top_in, sum_in, acc_ref, top_ref, sum_ref = refs
    for block in range(q_ref.shape[0] // BLK):
        rows = pl.ds(block * BLK, BLK)
        q = q_ref[rows, :]
        scores = [
            live_scores(slot_live(where, pattern, shards, level, side, block), q, k_ref[rows, :])
            for side, k_ref in enumerate((kb_ref, ka_ref))
        ]
        old = top_in[rows, :1]
        top = old
        for s in scores:
            top = jnp.maximum(top, jnp.max(s, axis=1, keepdims=True))
        shrink = jnp.exp2(old - top)
        total = sum_in[rows, :1] * shrink
        acc = acc_in[rows, :] * shrink
        for s, v_ref in zip(scores, (vb_ref, va_ref)):
            e = jnp.exp2(s - top)
            total = total + jnp.sum(e, axis=1, keepdims=True)
            acc = acc + dot(e.astype(BF16), v_ref[rows, :])
        acc_ref[rows, :] = acc
        top_ref[rows, :] = jnp.broadcast_to(top, acc.shape)
        sum_ref[rows, :] = jnp.broadcast_to(total, acc.shape)


def far_kernel(shards, level, merged, where, pattern, q_ref, kb_ref, ka_ref, acc_in, top_in, sum_in, acc_ref, *outs):
    behind = where[0] >= 2**level
    for block in range(q_ref.shape[0] // BLK):
        rows = pl.ds(block * BLK, BLK)
        q = q_ref[rows, :]
        live = [slot_live(where, pattern, shards, level, side, block) for side in range(2)]
        pair = [k_ref[rows, :] for k_ref in (kb_ref, ka_ref)]
        if merged:
            live = [(behind & live[0]) | (jnp.logical_not(behind) & live[1])]
            pair = [jnp.where(behind, pair[0], pair[1])]
        scores = [live_scores(on, q, k) for on, k in zip(live, pair)]
        old = top_in[rows, :1]
        top = old
        for s in scores:
            top = jnp.maximum(top, jnp.max(s, axis=1, keepdims=True))
        shrink = jnp.exp2(old - top)
        total = sum_in[rows, :1] * shrink
        exps = []
        for s in scores:
            e = jnp.exp2(s - top)
            total = total + jnp.sum(e, axis=1, keepdims=True)
            exps.append(e)
        inverse = 1.0 / total
        acc_ref[rows, :] = acc_in[rows, :] * (shrink * inverse)
        for e, out in zip(exps, outs):
            out[rows, :] = (e * inverse).astype(BF16)


def finish_kernel(shards, level, merged, where, starts, owners, acc_ref, lat_ref, *refs):
    sources = 1 if merged else 2
    weights, (vb_ref, va_ref) = refs[:sources], refs[sources : sources + 2]
    ctx_ref, outs = refs[sources + 2], refs[sources + 3 :]
    rows_here, columns = acc_ref.shape
    piece = rows_here // PIECES
    splits = [split_of(where, starts, p) for p in range(PIECES)]
    behind = where[0] >= 2**level
    sums = []
    for h in range(columns // HD):
        head = pl.ds(h * HD, HD)
        slots = pl.ds(h * BLK, BLK)
        found = []
        for block in range(rows_here // BLK):
            rows = pl.ds(block * BLK, BLK)
            pair = [v_ref[rows, head] for v_ref in (vb_ref, va_ref)]
            if merged:
                pair = [jnp.where(behind, pair[0], pair[1])]
            acc = acc_ref[rows, head]
            for w_ref, v in zip(weights, pair):
                acc = acc + dot(w_ref[rows, slots], v)
            ctx = acc.astype(BF16)
            ctx_ref[rows, head] = ctx
            ctx = ctx.astype(F32)
            for start in range(0, BLK, piece):
                found.append(doc_rows(ctx[start : start + piece], splits[len(found)]))
        sums.append(found)
    side = lax.broadcasted_iota(jnp.int32, (2, columns), 0)
    means = []
    for p in range(PIECES):
        count = jnp.where(side == 0, splits[p], piece - splits[p]).astype(F32)
        total = jnp.concatenate([found[p] for found in sums], axis=1) + lat_ref[2 * p : 2 * p + 2, :]
        means.append(total / count)
    for r in range(shards):
        if len(outs) == 1:
            target = r
        else:
            target = lax.rem(where[0] + r, shards)
        chosen = jnp.zeros((2, columns), F32)
        for p in range(PIECES):
            chosen = jnp.where(owners[2 * (PIECES * where[0] + p)] == target, means[p], chosen)
        if len(outs) == 1:
            outs[0][r] = chosen.astype(BF16)
        else:
            outs[r][...] = chosen.astype(BF16)


def weigh_kernel(block, shards, where, pattern, starts, q_ref, nb_ref, na_ref, fb_ref, fa_ref, *refs):
    acc_in, top_in, sum_in, acc_ref, wb_ref, wa_ref, wf_ref, sums_ref = refs
    behind = where[0] >= 2
    far_live = [slot_live(where, pattern, shards, 1, side, block) for side in range(2)]
    live = [slot_live(where, pattern, shards, 0, side, block) for side in range(2)]
    live.append((behind & far_live[0]) | (jnp.logical_not(behind) & far_live[1]))
    pieces = sums_ref.shape[0] // 2
    piece = BLK // pieces
    for h in range(q_ref.shape[1] // HD):
        head = slice(h * HD, (h + 1) * HD)
        slots = slice(h * BLK, (h + 1) * BLK)
        q = q_ref[:, head]
        keys = [nb_ref[:, head], na_ref[:, head], jnp.where(behind, fb_ref[:, head], fa_ref[:, head])]
        scores = [live_scores(on, q, k) for on, k in zip(live, keys)]
        old = top_in[:, h * HD : h * HD + 1]
        top = jnp.max(jnp.maximum(jnp.maximum(scores[0], scores[1]), scores[2]), axis=1, keepdims=True)
        top = jnp.maximum(top, old)
        shrink = jnp.exp2(old - top)
        exps = [jnp.exp2(s - top) for s in scores]
        total = sum_in[:, h * HD : h * HD + 1] * shrink
        total = total + jnp.sum(exps[0] + exps[1] + exps[2], axis=1, keepdims=True)
        inverse = 1.0 / total
        acc_ref[:, head] = acc_in[:, head] * (shrink * inverse)
        wb_ref[:, slots] = (exps[0] * inverse).astype(BF16)
        wa_ref[:, slots] = (exps[1] * inverse).astype(BF16)
        far = exps[2] * inverse
        wf_ref[:, slots] = far.astype(BF16)
        for p in range(pieces):
            split = split_of(where, starts, block * pieces + p)
            sums_ref[2 * p : 2 * p + 2, slots] = doc_rows(far[p * piece : (p + 1) * piece], split)


def mix_kernel(block, where, starts, acc_in, wb_ref, wa_ref, vb_ref, va_ref, v_ref, sums_ref, lat_ref, *refs):
    acc_ref, mean_ref, part_ref = refs
    pieces = mean_ref.shape[0] // 2
    piece = BLK // pieces
    partner = lax.rem(where[0] + 2, 4)
    side = lax.broadcasted_iota(jnp.int32, (2, HD), 0)

    def counts(split):
        return jnp.where(side == 0, split, piece - split).astype(F32)

    for h in range(acc_in.shape[1] // HD):
        head = slice(h * HD, (h + 1) * HD)
        slots = slice(h * BLK, (h + 1) * BLK)
        acc = acc_in[:, head] + dot(wb_ref[:, slots], vb_ref[:, head]) + dot(wa_ref[:, slots], va_ref[:, head])
        acc_ref[:, head] = acc
        part = dot(sums_ref[:, slots].astype(BF16), v_ref[:, head])
        for p in range(pieces):
            rows = slice(2 * p, 2 * p + 2)
            index = block * pieces + p
            split = split_of(where, starts, index)
            found = doc_rows(acc[p * piece : (p + 1) * piece], split)
            mean_ref[rows, head] = (found + lat_ref[2 * index : 2 * index + 2, head]) / counts(split)
            part_ref[rows, head] = part[2 * index : 2 * index + 2] / counts(split_of(where, starts, index, partner))


def route_kernel(where, owners, *refs):
    halves, out_ref = refs[:-1], refs[-1]
    means, parts = halves[: len(halves) // 2], halves[len(halves) // 2 :]
    pieces = means[0].shape[0] // 2
    for target in range(out_ref.shape[0]):
        for first, group, shard in ((0, means, where[0]), (2, parts, lax.rem(where[0] + 2, 4))):
            chosen = jnp.zeros((2, out_ref.shape[2]), F32)
            for p in range(PIECES):
                row = 2 * (p % pieces)
                mine = owners[2 * (PIECES * shard + p)] == target
                chosen = jnp.where(mine, group[p // pieces][row : row + 2, :], chosen)
            out_ref[target, first : first + 2, :] = chosen


def pool_kernel(got_ref, out_ref):
    for s in range(4):
        out_ref[0, s] = (got_ref[s, :2, :] + got_ref[s ^ 2, 2:, :]).astype(BF16)


def context_kernel(block, where, acc_ref, w_ref, vb_ref, va_ref, *refs):
    out_ref, stage, sem = refs[-3:]
    behind = where[0] >= 2
    copies = []
    for h in range(acc_ref.shape[1] // HD):
        head = pl.ds(h * HD, HD)
        v = jnp.where(behind, vb_ref[:, head], va_ref[:, head])
        stage[:, head] = (acc_ref[:, head] + dot(w_ref[:, pl.ds(h * BLK, BLK)], v)).astype(BF16)
        if h % 2:
            pair = pl.ds((h - 1) * HD, 2 * HD)
            copy = pltpu.make_async_copy(stage.at[:, pair], out_ref.at[pl.ds(block * BLK, BLK), pair], sem.at[h // 2])
            copy.start()
            copies.append(copy)
    for copy in copies:
        copy.wait()


def spec(rows, columns=HD):
    return pl.BlockSpec((rows, columns), lambda h: (0, h))


def smem(count):
    return [pl.BlockSpec(memory_space=pltpu.SMEM)] * count


def vmem(count):
    return [pl.BlockSpec(memory_space=pltpu.VMEM)] * count


def shape(rows, columns, kind=F32):
    return jax.ShapeDtypeStruct((rows, columns), kind)


def step_of(heads):
    return 2 if heads % 2 == 0 else 1


def own_call(queries, keys, values):
    rows, columns = queries.shape
    heads = columns // HD
    wide = step_of(heads) * HD
    return pl.pallas_call(
        own_kernel,
        grid=(columns // wide,),
        in_specs=[spec(rows, wide)] * 3,
        out_specs=[spec(rows, wide)] * 3,
        out_shape=(shape(rows, columns),) * 3,
        compiler_params=PARAMS,
        cost_estimate=pl.CostEstimate(
            flops=4 * rows * columns * rows, bytes_accessed=18 * rows * columns, transcendentals=heads * rows * rows
        ),
        name="own",
    )(queries, keys, values)


def latent_call(where, doc_starts, queries, latent_keys, latent_values):
    rows, columns = queries.shape
    latents = latent_keys.shape[0]
    heads = columns // HD
    wide = step_of(heads) * HD
    return pl.pallas_call(
        latent_kernel,
        grid=(columns // wide,),
        in_specs=smem(2) + [spec(rows, wide)] + [spec(latents, wide)] * 2,
        out_specs=spec(2 * PIECES, wide),
        out_shape=shape(2 * PIECES, columns),
        compiler_params=PARAMS,
        cost_estimate=pl.CostEstimate(
            flops=4 * rows * columns * latents, bytes_accessed=6 * rows * columns, transcendentals=heads * rows * latents
        ),
        name="latent",
    )(where, doc_starts, queries, latent_keys, latent_values)


def four_shards(queries, keys, values, latent_keys, latent_values, pattern, doc_starts, doc_owner):
    rows, columns = queries.shape
    heads = columns // HD
    step = step_of(heads)
    wide = step * HD
    slots = heads * BLK
    blocks = rows // BLK
    docs = 2 * PIECES // blocks
    where = lax.axis_index("seq").astype(jnp.int32).reshape(1)
    right, left = [(0, 1), (1, 2), (2, 3)], [(1, 0), (2, 1), (3, 2)]

    def move(value, pairs):
        return lax.ppermute(value, "seq", pairs)

    def near(value):
        return [move(value, right), move(value, left)]

    def onward(pair):
        return [move(pair[0], right[1:]), move(pair[1], left[:-1])]

    def part(array, block):
        return array[block * BLK : (block + 1) * BLK]

    def row_spec(block, width=wide):
        return pl.BlockSpec((BLK, width), lambda h: (block, h))

    def weigh(block, near_keys, far_keys, state):
        return pl.pallas_call(
            functools.partial(weigh_kernel, block, 4),
            grid=(heads // step,),
            in_specs=smem(3) + [row_spec(block)] + [row_spec(0)] * 4 + [row_spec(block)] * 3,
            out_specs=[row_spec(0)] + [row_spec(0, step * BLK)] * 3 + [spec(docs, step * BLK)],
            out_shape=(shape(BLK, columns),) + (shape(BLK, slots, BF16),) * 3 + (shape(docs, slots),),
            compiler_params=PARAMS,
            cost_estimate=pl.CostEstimate(
                flops=6 * BLK * columns * BLK, bytes_accessed=22 * BLK * columns, transcendentals=3 * heads * BLK * BLK
            ),
            name="weigh",
        )(where, pattern, doc_starts, queries, *near_keys, *far_keys, *state)

    def mix(block, acc, weights, near_vals, sums, lat):
        return pl.pallas_call(
            functools.partial(mix_kernel, block),
            grid=(heads // step,),
            in_specs=smem(2)
            + [row_spec(0)]
            + [row_spec(0, step * BLK)] * 2
            + [row_spec(0)] * 2
            + [row_spec(block), spec(2 * PIECES, step * BLK), spec(2 * PIECES, wide)],
            out_specs=[row_spec(0)] + [spec(docs, wide)] * 2,
            out_shape=(shape(BLK, columns),) + (shape(docs, columns),) * 2,
            compiler_params=PARAMS,
            cost_estimate=pl.CostEstimate(flops=5 * BLK * columns * BLK, bytes_accessed=22 * BLK * columns, transcendentals=0),
            name="mix",
        )(where, doc_starts, acc, *weights, *near_vals, values, sums, lat)

    def finish(block, acc, weights, far_vals, context):
        held = [] if context is None else [context]
        return pl.pallas_call(
            functools.partial(context_kernel, block),
            in_specs=smem(1) + vmem(4) + [pl.BlockSpec(memory_space=pl.ANY)] * len(held),
            out_specs=pl.BlockSpec(memory_space=pl.ANY),
            out_shape=shape(rows, columns, BF16),
            scratch_shapes=[pltpu.VMEM((BLK, columns), BF16), pltpu.SemaphoreType.DMA((heads // 2,))],
            input_output_aliases={5: 0} if held else {},
            compiler_params=PARAMS,
            cost_estimate=pl.CostEstimate(flops=2 * BLK * columns * BLK, bytes_accessed=14 * BLK * columns, transcendentals=0),
            name="finish",
        )(where, acc, weights, *far_vals, *held)

    near_keys = [near(part(keys, 0))]
    lat = latent_call(where, doc_starts, queries, latent_keys, latent_values)
    lat, late_keys = lax.optimization_barrier((lat, part(keys, 1)))
    near_keys.append(near(late_keys))
    state = own_call(queries, keys, values)
    near_keys[0], state = lax.optimization_barrier((near_keys[0], state))
    far_keys = [onward(pair) for pair in near_keys]
    late_vals, near_keys[1] = lax.optimization_barrier(([part(values, block) for block in range(blocks)], near_keys[1]))
    near_vals = [near(value) for value in late_vals]
    acc, near_weights, far_weights, sums = [], [], [], []
    for block in range(blocks):
        out = weigh(block, near_keys[block], far_keys[block], state)
        acc.append(out[0])
        near_weights.append(out[1:3])
        far_weights.append(out[3])
        sums.append(out[4])
    sums = move(jnp.concatenate(sums), [(s, s ^ 2) for s in range(4)])
    far_vals = [onward(near_vals[0])]
    means, parts = [], []
    for block in range(blocks):
        acc[block], mean, far_part = mix(block, acc[block], near_weights[block], near_vals[block], sums, lat)
        means.append(mean)
        parts.append(far_part)
    sent = pl.pallas_call(
        route_kernel,
        in_specs=smem(2) + vmem(2 * blocks),
        out_specs=pl.BlockSpec(memory_space=pltpu.VMEM),
        out_shape=jax.ShapeDtypeStruct((4, 4, columns), F32),
        compiler_params=PARAMS,
        name="route",
    )(where, doc_owner, *means, *parts)
    sent, last_vals = lax.optimization_barrier((sent, near_vals[1]))
    far_vals.append(onward(last_vals))
    context = finish(0, acc[0], far_weights[0], far_vals[0], None)
    sent, context = lax.optimization_barrier((sent, context))
    got = lax.all_to_all(sent, "seq", split_axis=0, concat_axis=0, tiled=True)
    pooled = pl.pallas_call(
        pool_kernel,
        in_specs=vmem(1),
        out_specs=pl.BlockSpec(memory_space=pltpu.VMEM),
        out_shape=jax.ShapeDtypeStruct((1, 4, 2, columns), BF16),
        compiler_params=PARAMS,
        name="pool",
    )(got)
    context = finish(1, acc[1], far_weights[1], far_vals[1], context)
    return context, pooled


def body(queries, keys, values, latent_keys, latent_values, pattern, doc_starts, doc_owner):
    rows, columns = queries.shape
    heads = columns // HD
    shards = lax.axis_size("seq")
    seq_index = lax.axis_index("seq")
    where = seq_index.astype(jnp.int32).reshape(1)
    levels = [j for j in range(LEVELS) if 2**j < shards]
    last = levels[-1]
    merged = 2 * 2**last >= shards
    rotate = shards <= 4

    def both_ways(value, distance):
        behind = lax.ppermute(value, "seq", [(s, s + distance) for s in range(shards - distance)])
        ahead = lax.ppermute(value, "seq", [(s, s - distance) for s in range(distance, shards)])
        return [behind, ahead]

    def far(value, near):
        if last != 1:
            return both_ways(value, 2**last)
        behind = lax.ppermute(near[0], "seq", [(s, s + 1) for s in range(1, shards - 1)])
        ahead = lax.ppermute(near[1], "seq", [(s, s - 1) for s in range(1, shards - 1)])
        return [behind, ahead]

    if shards == 4:
        return four_shards(queries, keys, values, latent_keys, latent_values, pattern, doc_starts, doc_owner)
    near_keys = both_ways(keys, 1)
    near_vals = both_ways(values, 1)
    state_shapes = (shape(rows, columns),) * 3
    lat = latent_call(where, doc_starts, queries, latent_keys, latent_values)
    state = own_call(queries, keys, values)
    near_keys, state = lax.optimization_barrier((near_keys, state))

    for level in levels[:-1]:
        if level == 0:
            got = near_keys + near_vals
        else:
            got = both_ways(keys, 2**level) + both_ways(values, 2**level)
        state = pl.pallas_call(
            functools.partial(near_kernel, shards, level),
            grid=(heads,),
            in_specs=smem(2) + [spec(rows)] * 8,
            out_specs=[spec(rows)] * 3,
            out_shape=state_shapes,
            input_output_aliases={7 + i: i for i in range(3)},
            compiler_params=PARAMS,
            cost_estimate=pl.CostEstimate(
                flops=8 * rows * columns * BLK, bytes_accessed=20 * rows * columns * 2, transcendentals=2 * heads * rows * BLK
            ),
            name="near",
        )(where, pattern, queries, *got, *state)

    far_keys = far(keys, near_keys)
    far_vals = far(values, near_vals)
    sources = 1 if merged else 2
    acc, *weights = pl.pallas_call(
        functools.partial(far_kernel, shards, last, merged),
        grid=(heads,),
        in_specs=smem(2) + [spec(rows)] * 6,
        out_specs=[spec(rows)] + [spec(rows, BLK)] * sources,
        out_shape=(shape(rows, columns),) + (shape(rows, heads * BLK, BF16),) * sources,
        input_output_aliases={5: 0},
        compiler_params=PARAMS,
        cost_estimate=pl.CostEstimate(
            flops=2 * sources * rows * columns * BLK,
            bytes_accessed=(10 + 3 * sources) * rows * columns * 2,
            transcendentals=sources * heads * rows * BLK,
        ),
        name="far",
    )(where, pattern, queries, *far_keys, *state)

    if rotate:
        sent = (shape(2, columns, BF16),) * shards
    else:
        sent = (jax.ShapeDtypeStruct((shards, 2, columns), BF16),)
    context, *means = pl.pallas_call(
        functools.partial(finish_kernel, shards, last, merged),
        in_specs=smem(3) + vmem(4 + sources),
        out_specs=vmem(1 + len(sent)),
        out_shape=(shape(rows, columns, BF16),) + sent,
        compiler_params=PARAMS,
        cost_estimate=pl.CostEstimate(
            flops=2 * sources * rows * columns * BLK, bytes_accessed=(3 + 3 * sources) * rows * columns * 2, transcendentals=0
        ),
        name="finish",
    )(where, doc_starts, doc_owner, acc, lat, *weights, *far_vals)

    if not rotate:
        return context, lax.all_to_all(means[0], "seq", split_axis=0, concat_axis=0, tiled=True)[None]
    got = [means[0]]
    for r in range(1, shards):
        got.append(lax.ppermute(means[r], "seq", [(s, (s + r) % shards) for s in range(shards)]))
    pooled = []
    for s in range(shards):
        back = lax.rem(seq_index - s + shards, shards)
        row = got[0]
        for r in range(1, shards):
            row = jnp.where(back == r, got[r], row)
        pooled.append(row)
    return context, jnp.stack(pooled)[None]


def solution(mesh):
    in_specs = (
        P(("groups", "seq"), ("head", "sub")),
        P(("groups", "seq"), ("head", "sub")),
        P(("groups", "seq"), ("head", "sub")),
        P("groups", ("head", "sub")),
        P("groups", ("head", "sub")),
        P(("groups", "seq"), None),
        P("groups"),
        P("groups"),
    )
    out_specs = (
        P(("groups", "seq"), ("head", "sub")),
        P(("groups", "seq"), None, None, ("head", "sub")),
    )
    return jax.shard_map(body, mesh=mesh, in_specs=in_specs, out_specs=out_specs, check_vma=False)
```

```python
import functools
import math

import jax
import jax.numpy as jnp
from jax import lax
from jax.experimental import pallas as pl
from jax.experimental.pallas import tpu as pltpu
from jax.sharding import PartitionSpec as P

HD = 128
LEVELS = 4
BLK = 256
PIECES = 4
SCALE = math.log2(math.e) / math.sqrt(HD)
PARAMS = pltpu.CompilerParams(vmem_limit_bytes=24 * 1024 * 1024)
F32 = jnp.float32
BF16 = jnp.bfloat16


def dot_t(a, b):
    return lax.dot_general(a, b, (((1,), (1,)), ((), ())), preferred_element_type=F32)


def dot(a, b):
    return jnp.dot(a, b, preferred_element_type=F32)


def doc_rows(rows, split):
    place = lax.broadcasted_iota(jnp.int32, rows.shape, 0)
    first = jnp.sum(jnp.where(place < split, rows, 0.0), axis=0, keepdims=True)
    second = jnp.sum(jnp.where(place < split, 0.0, rows), axis=0, keepdims=True)
    return jnp.concatenate((first, second), axis=0)


def own_kernel(q_ref, k_ref, v_ref, acc_ref, top_ref, sum_ref):
    for h in range(q_ref.shape[1] // HD):
        head = slice(h * HD, (h + 1) * HD)
        s = dot_t(q_ref[:, head], k_ref[:, head]) * SCALE
        top = jnp.max(s, axis=1, keepdims=True)
        e = jnp.exp2(s - top)
        acc = dot(e.astype(BF16), v_ref[:, head])
        acc_ref[:, head] = acc
        top_ref[:, head] = jnp.broadcast_to(top, acc.shape)
        sum_ref[:, head] = jnp.broadcast_to(jnp.sum(e, axis=1, keepdims=True), acc.shape)


def latent_kernel(where, starts, q_ref, lk_ref, lv_ref, lat_ref):
    for h in range(q_ref.shape[1] // HD):
        head = slice(h * HD, (h + 1) * HD)
        s = dot_t(q_ref[:, head], lk_ref[:, head]) * SCALE
        e = jnp.exp2(s - jnp.max(s, axis=1, keepdims=True))
        out = dot(e.astype(BF16), lv_ref[:, head]) / jnp.sum(e, axis=1, keepdims=True)
        piece = out.shape[0] // PIECES
        for p in range(PIECES):
            split = split_of(where, starts, p)
            lat_ref[2 * p : 2 * p + 2, head] = doc_rows(out[p * piece : (p + 1) * piece], split)


def split_of(where, starts, p, shard=None):
    first = 2 * (PIECES * (where[0] if shard is None else shard) + p)
    return starts[first + 1] - starts[first]


def slot_live(where, pattern, shards, level, side, block):
    partner = where[0] + (2 * side - 1) * 2**level
    return (pattern[block, 2 * level + side] == 1) & (partner >= 0) & (partner < shards)


def live_scores(live, q, k):
    return jnp.where(live, dot_t(q, k) * SCALE, -jnp.inf)


def near_kernel(shards, level, where, pattern, q_ref, kb_ref, ka_ref, vb_ref, va_ref, *refs):
    acc_in, top_in, sum_in, acc_ref, top_ref, sum_ref = refs
    for block in range(q_ref.shape[0] // BLK):
        rows = pl.ds(block * BLK, BLK)
        q = q_ref[rows, :]
        scores = [
            live_scores(slot_live(where, pattern, shards, level, side, block), q, k_ref[rows, :])
            for side, k_ref in enumerate((kb_ref, ka_ref))
        ]
        old = top_in[rows, :1]
        top = old
        for s in scores:
            top = jnp.maximum(top, jnp.max(s, axis=1, keepdims=True))
        shrink = jnp.exp2(old - top)
        total = sum_in[rows, :1] * shrink
        acc = acc_in[rows, :] * shrink
        for s, v_ref in zip(scores, (vb_ref, va_ref)):
            e = jnp.exp2(s - top)
            total = total + jnp.sum(e, axis=1, keepdims=True)
            acc = acc + dot(e.astype(BF16), v_ref[rows, :])
        acc_ref[rows, :] = acc
        top_ref[rows, :] = jnp.broadcast_to(top, acc.shape)
        sum_ref[rows, :] = jnp.broadcast_to(total, acc.shape)


def far_kernel(shards, level, merged, where, pattern, q_ref, kb_ref, ka_ref, acc_in, top_in, sum_in, acc_ref, *outs):
    behind = where[0] >= 2**level
    for block in range(q_ref.shape[0] // BLK):
        rows = pl.ds(block * BLK, BLK)
        q = q_ref[rows, :]
        live = [slot_live(where, pattern, shards, level, side, block) for side in range(2)]
        pair = [k_ref[rows, :] for k_ref in (kb_ref, ka_ref)]
        if merged:
            live = [(behind & live[0]) | (jnp.logical_not(behind) & live[1])]
            pair = [jnp.where(behind, pair[0], pair[1])]
        scores = [live_scores(on, q, k) for on, k in zip(live, pair)]
        old = top_in[rows, :1]
        top = old
        for s in scores:
            top = jnp.maximum(top, jnp.max(s, axis=1, keepdims=True))
        shrink = jnp.exp2(old - top)
        total = sum_in[rows, :1] * shrink
        exps = []
        for s in scores:
            e = jnp.exp2(s - top)
            total = total + jnp.sum(e, axis=1, keepdims=True)
            exps.append(e)
        inverse = 1.0 / total
        acc_ref[rows, :] = acc_in[rows, :] * (shrink * inverse)
        for e, out in zip(exps, outs):
            out[rows, :] = (e * inverse).astype(BF16)


def finish_kernel(shards, level, merged, where, starts, owners, acc_ref, lat_ref, *refs):
    sources = 1 if merged else 2
    weights, (vb_ref, va_ref) = refs[:sources], refs[sources : sources + 2]
    ctx_ref, outs = refs[sources + 2], refs[sources + 3 :]
    rows_here, columns = acc_ref.shape
    piece = rows_here // PIECES
    splits = [split_of(where, starts, p) for p in range(PIECES)]
    behind = where[0] >= 2**level
    sums = []
    for h in range(columns // HD):
        head = pl.ds(h * HD, HD)
        slots = pl.ds(h * BLK, BLK)
        found = []
        for block in range(rows_here // BLK):
            rows = pl.ds(block * BLK, BLK)
            pair = [v_ref[rows, head] for v_ref in (vb_ref, va_ref)]
            if merged:
                pair = [jnp.where(behind, pair[0], pair[1])]
            acc = acc_ref[rows, head]
            for w_ref, v in zip(weights, pair):
                acc = acc + dot(w_ref[rows, slots], v)
            ctx = acc.astype(BF16)
            ctx_ref[rows, head] = ctx
            ctx = ctx.astype(F32)
            for start in range(0, BLK, piece):
                found.append(doc_rows(ctx[start : start + piece], splits[len(found)]))
        sums.append(found)
    side = lax.broadcasted_iota(jnp.int32, (2, columns), 0)
    means = []
    for p in range(PIECES):
        count = jnp.where(side == 0, splits[p], piece - splits[p]).astype(F32)
        total = jnp.concatenate([found[p] for found in sums], axis=1) + lat_ref[2 * p : 2 * p + 2, :]
        means.append(total / count)
    for r in range(shards):
        if len(outs) == 1:
            target = r
        else:
            target = lax.rem(where[0] + r, shards)
        chosen = jnp.zeros((2, columns), F32)
        for p in range(PIECES):
            chosen = jnp.where(owners[2 * (PIECES * where[0] + p)] == target, means[p], chosen)
        if len(outs) == 1:
            outs[0][r] = chosen.astype(BF16)
        else:
            outs[r][...] = chosen.astype(BF16)


def weigh_kernel(block, shards, where, pattern, starts, q_ref, nb_ref, na_ref, fb_ref, fa_ref, *refs):
    acc_in, top_in, sum_in, acc_ref, wb_ref, wa_ref, wf_ref, sums_ref = refs
    behind = where[0] >= 2
    far_live = [slot_live(where, pattern, shards, 1, side, block) for side in range(2)]
    live = [slot_live(where, pattern, shards, 0, side, block) for side in range(2)]
    live.append((behind & far_live[0]) | (jnp.logical_not(behind) & far_live[1]))
    bias = [jnp.where(on, 0.0, -jnp.inf) for on in live]
    pieces = sums_ref.shape[0] // 2
    piece = BLK // pieces
    place = lax.broadcasted_iota(jnp.int32, (piece, HD), 0)
    firsts = [place < split_of(where, starts, block * pieces + p) for p in range(pieces)]
    lanes = [slice(i * HD, (i + 1) * HD) for i in range(BLK // HD)]
    for h in range(q_ref.shape[1] // HD):
        head = slice(h * HD, (h + 1) * HD)
        keys = [nb_ref[:, head], na_ref[:, head], jnp.where(behind, fb_ref[:, head], fa_ref[:, head])]
        for p in range(pieces):
            rows = slice(p * piece, (p + 1) * piece)
            q = q_ref[rows, head]
            scores = []
            for k, low in zip(keys, bias):
                s = dot_t(q, k)
                scores += [s[:, part] * SCALE + low for part in lanes]
            old = top_in[rows, head]
            top = jnp.maximum(jnp.max(functools.reduce(jnp.maximum, scores), axis=1, keepdims=True), old)
            shrink = jnp.exp2(old - top)
            exps = [jnp.exp2(s - top) for s in scores]
            added = jnp.sum(functools.reduce(jnp.add, exps), axis=1, keepdims=True)
            inverse = 1.0 / (sum_in[rows, head] * shrink + added)
            acc_ref[rows, head] = acc_in[rows, head] * (shrink * inverse)
            for i, e in enumerate(exps):
                out = (wb_ref, wa_ref, wf_ref)[i // len(lanes)]
                first = h * BLK + i % len(lanes) * HD
                w = e * inverse
                out[rows, first : first + HD] = w.astype(BF16)
                if out is wf_ref:
                    sums = [jnp.sum(x, axis=0, keepdims=True) for x in (jnp.where(firsts[p], w, 0.0), jnp.where(firsts[p], 0.0, w))]
                    sums_ref[2 * p : 2 * p + 2, first : first + HD] = jnp.concatenate(sums, axis=0)


def doc_counts(split, piece, columns):
    side = lax.broadcasted_iota(jnp.int32, (2, columns), 0)
    return jnp.where(side == 0, split, piece - split).astype(F32)


def mix_kernel(block, where, starts, acc_in, wb_ref, wa_ref, vb_ref, va_ref, lat_ref, acc_ref, mean_ref):
    pieces = mean_ref.shape[0] // 2
    piece = BLK // pieces
    for h in range(acc_in.shape[1] // HD):
        head = slice(h * HD, (h + 1) * HD)
        slots = slice(h * BLK, (h + 1) * BLK)
        acc = acc_in[:, head] + dot(wb_ref[:, slots], vb_ref[:, head]) + dot(wa_ref[:, slots], va_ref[:, head])
        acc_ref[:, head] = acc
        for p in range(pieces):
            index = block * pieces + p
            split = split_of(where, starts, index)
            found = doc_rows(acc[p * piece : (p + 1) * piece], split) + lat_ref[2 * index : 2 * index + 2, head]
            mean_ref[2 * p : 2 * p + 2, head] = found / doc_counts(split, piece, HD)


def part_kernel(where, starts, sums_ref, v_ref, part_ref):
    piece = v_ref.shape[0] // PIECES
    per_block = BLK // piece
    partner = lax.rem(where[0] + 2, 4)
    counts = [doc_counts(split_of(where, starts, p, partner), piece, HD) for p in range(PIECES)]
    for h in range(v_ref.shape[1] // HD):
        head = slice(h * HD, (h + 1) * HD)
        sums = sums_ref[:, h * BLK : (h + 1) * BLK]
        found = [dot(sums.astype(BF16), v_ref[block * BLK : (block + 1) * BLK, head]) for block in range(v_ref.shape[0] // BLK)]
        for p in range(PIECES):
            rows = slice(2 * p, 2 * p + 2)
            part_ref[rows, head] = found[p // per_block][rows] / counts[p]


def route_kernel(where, owners, part_ref, *refs):
    mean_refs, out_ref = refs[:-1], refs[-1]
    here, partner = where[0], lax.rem(where[0] + 2, 4)
    means = jnp.concatenate([mean_ref[...] for mean_ref in mean_refs], axis=0)
    parts = part_ref[...]
    for target in range(out_ref.shape[0]):
        rows = []
        for group, shard in ((means, here), (parts, partner)):
            chosen = jnp.zeros((2, out_ref.shape[2]), F32)
            for p in range(PIECES):
                chosen = jnp.where(owners[2 * (PIECES * shard + p)] == target, group[2 * p : 2 * p + 2], chosen)
            rows.append(chosen)
        out_ref[target] = jnp.concatenate(rows, axis=0).astype(BF16)


def pool_kernel(got_ref, out_ref):
    got = [got_ref[s].astype(F32) for s in range(4)]
    for s in range(4):
        out_ref[0, s] = (got[s][:2] + got[s ^ 2][2:]).astype(BF16)


def context_kernel(block, where, acc_ref, w_ref, vb_ref, va_ref, *refs):
    out_ref, stage, sem = refs[-3:]
    behind = where[0] >= 2
    copies = []
    for h in range(acc_ref.shape[1] // HD):
        head = pl.ds(h * HD, HD)
        v = jnp.where(behind, vb_ref[:, head], va_ref[:, head])
        stage[:, head] = (acc_ref[:, head] + dot(w_ref[:, pl.ds(h * BLK, BLK)], v)).astype(BF16)
        if h % 2:
            pair = pl.ds((h - 1) * HD, 2 * HD)
            copy = pltpu.make_async_copy(stage.at[:, pair], out_ref.at[pl.ds(block * BLK, BLK), pair], sem.at[h // 2])
            copy.start()
            copies.append(copy)
    for copy in copies:
        copy.wait()


def spec(rows, columns=HD):
    return pl.BlockSpec((rows, columns), lambda h: (0, h))


def smem(count):
    return [pl.BlockSpec(memory_space=pltpu.SMEM)] * count


def vmem(count):
    return [pl.BlockSpec(memory_space=pltpu.VMEM)] * count


def shape(rows, columns, kind=F32):
    return jax.ShapeDtypeStruct((rows, columns), kind)


def step_of(heads):
    return 2 if heads % 2 == 0 else 1


def own_call(queries, keys, values, block=None):
    rows, columns = queries.shape
    heads = columns // HD
    wide = step_of(heads) * HD
    here = rows if block is None else BLK
    return pl.pallas_call(
        own_kernel,
        grid=(columns // wide,),
        in_specs=[pl.BlockSpec((here, wide), lambda h: (block or 0, h))] + [spec(rows, wide)] * 2,
        out_specs=[spec(here, wide)] * 3,
        out_shape=(shape(here, columns),) * 3,
        compiler_params=PARAMS,
        cost_estimate=pl.CostEstimate(
            flops=4 * here * columns * rows, bytes_accessed=18 * here * columns, transcendentals=heads * here * rows
        ),
        name="own",
    )(queries, keys, values)


def latent_call(where, doc_starts, queries, latent_keys, latent_values):
    rows, columns = queries.shape
    latents = latent_keys.shape[0]
    heads = columns // HD
    wide = step_of(heads) * HD
    return pl.pallas_call(
        latent_kernel,
        grid=(columns // wide,),
        in_specs=smem(2) + [spec(rows, wide)] + [spec(latents, wide)] * 2,
        out_specs=spec(2 * PIECES, wide),
        out_shape=shape(2 * PIECES, columns),
        compiler_params=PARAMS,
        cost_estimate=pl.CostEstimate(
            flops=4 * rows * columns * latents, bytes_accessed=6 * rows * columns, transcendentals=heads * rows * latents
        ),
        name="latent",
    )(where, doc_starts, queries, latent_keys, latent_values)


def four_shards(queries, keys, values, latent_keys, latent_values, pattern, doc_starts, doc_owner):
    rows, columns = queries.shape
    heads = columns // HD
    step = step_of(heads)
    wide = step * HD
    slots = heads * BLK
    blocks = rows // BLK
    docs = 2 * PIECES // blocks
    where = lax.axis_index("seq").astype(jnp.int32).reshape(1)
    right, left = [(0, 1), (1, 2), (2, 3)], [(1, 0), (2, 1), (3, 2)]

    def move(value, pairs):
        return lax.ppermute(value, "seq", pairs)

    def near(value):
        return [move(value, right), move(value, left)]

    def onward(pair):
        return [move(pair[0], right[1:]), move(pair[1], left[:-1])]

    def part(array, block):
        return array[block * BLK : (block + 1) * BLK]

    def row_spec(block, width=wide):
        return pl.BlockSpec((BLK, width), lambda h: (block, h))

    def weigh(block, near_keys, far_keys, state):
        return pl.pallas_call(
            functools.partial(weigh_kernel, block, 4),
            grid=(heads // step,),
            in_specs=smem(3) + [row_spec(block)] + [row_spec(0)] * 7,
            out_specs=[row_spec(0)] + [row_spec(0, step * BLK)] * 3 + [spec(docs, step * BLK)],
            out_shape=(shape(BLK, columns),) + (shape(BLK, slots, BF16),) * 3 + (shape(docs, slots),),
            compiler_params=PARAMS,
            cost_estimate=pl.CostEstimate(
                flops=6 * BLK * columns * BLK, bytes_accessed=22 * BLK * columns, transcendentals=3 * heads * BLK * BLK
            ),
            name="weigh",
        )(where, pattern, doc_starts, queries, *near_keys, *far_keys, *state)

    def mix(block, acc, weights, near_vals, lat):
        return pl.pallas_call(
            functools.partial(mix_kernel, block),
            grid=(heads // step,),
            in_specs=smem(2) + [row_spec(0)] + [row_spec(0, step * BLK)] * 2 + [row_spec(0)] * 2 + [spec(2 * PIECES, wide)],
            out_specs=[row_spec(0), spec(docs, wide)],
            out_shape=(shape(BLK, columns), shape(docs, columns)),
            compiler_params=PARAMS,
            cost_estimate=pl.CostEstimate(flops=4 * BLK * columns * BLK, bytes_accessed=20 * BLK * columns, transcendentals=0),
            name="mix",
        )(where, doc_starts, acc, *weights, *near_vals, lat)

    def finish(block, acc, weights, far_vals, context):
        held = [] if context is None else [context]
        return pl.pallas_call(
            functools.partial(context_kernel, block),
            in_specs=smem(1) + vmem(4) + [pl.BlockSpec(memory_space=pl.ANY)] * len(held),
            out_specs=pl.BlockSpec(memory_space=pl.ANY),
            out_shape=shape(rows, columns, BF16),
            scratch_shapes=[pltpu.VMEM((BLK, columns), BF16), pltpu.SemaphoreType.DMA((heads // 2,))],
            input_output_aliases={5: 0} if held else {},
            compiler_params=PARAMS,
            cost_estimate=pl.CostEstimate(flops=2 * BLK * columns * BLK, bytes_accessed=14 * BLK * columns, transcendentals=0),
            name="finish",
        )(where, acc, weights, *far_vals, *held)

    near_keys = [near(part(keys, 0))]
    lat = latent_call(where, doc_starts, queries, latent_keys, latent_values)
    lat, late_keys, late_vals = lax.optimization_barrier((lat, keys, values))
    near_keys.append(near(part(late_keys, 1)))
    state = own_call(queries, keys, values, 0)
    near_keys[0], state = lax.optimization_barrier((near_keys[0], state))
    near_keys[1], late_queries = lax.optimization_barrier((near_keys[1], queries))
    far_keys = [onward(pair) for pair in near_keys]
    late_state = own_call(late_queries, keys, values, 1)
    late_vals, late_state = lax.optimization_barrier((late_vals, late_state))
    near_vals = [near(part(late_vals, 0))]
    out = [weigh(0, near_keys[0], far_keys[0], state)]
    out[0], last_vals = lax.optimization_barrier((out[0], late_vals))
    near_vals.append(near(part(last_vals, 1)))
    out.append(weigh(1, near_keys[1], far_keys[1], late_state))
    sums = jnp.concatenate([o[4] for o in out])
    near_vals[0], out[1], sums = lax.optimization_barrier((near_vals[0], out[1], sums))
    sums = move(sums, [(s, s ^ 2) for s in range(4)])
    mixed = [mix(0, out[0][0], out[0][1:3], near_vals[0], lat)]
    far_vals = [onward(near_vals[0])]
    parts = pl.pallas_call(
        part_kernel,
        grid=(heads // step,),
        in_specs=smem(2) + [spec(2 * PIECES, step * BLK), spec(rows, wide)],
        out_specs=spec(2 * PIECES, wide),
        out_shape=shape(2 * PIECES, columns),
        compiler_params=PARAMS,
        cost_estimate=pl.CostEstimate(flops=32 * BLK * columns, bytes_accessed=3 * rows * columns, transcendentals=0),
        name="part",
    )(where, doc_starts, sums, values)
    near_vals[1], parts = lax.optimization_barrier((near_vals[1], parts))
    far_vals.append(onward(near_vals[1]))
    mixed.append(mix(1, out[1][0], out[1][1:3], near_vals[1], lat))
    acc = [m[0] for m in mixed]
    far_weights = [o[3] for o in out]
    sent = pl.pallas_call(
        route_kernel,
        in_specs=smem(2) + vmem(3),
        out_specs=pl.BlockSpec(memory_space=pltpu.VMEM),
        out_shape=jax.ShapeDtypeStruct((4, 4, columns), BF16),
        compiler_params=PARAMS,
        name="route",
    )(where, doc_owner, parts, *[m[1] for m in mixed])
    context = finish(0, acc[0], far_weights[0], far_vals[0], None)
    sent, context = lax.optimization_barrier((sent, context))
    got = lax.all_to_all(sent, "seq", split_axis=0, concat_axis=0, tiled=True)
    pooled = pl.pallas_call(
        pool_kernel,
        in_specs=vmem(1),
        out_specs=pl.BlockSpec(memory_space=pltpu.VMEM),
        out_shape=jax.ShapeDtypeStruct((1, 4, 2, columns), BF16),
        compiler_params=PARAMS,
        name="pool",
    )(got)
    context = finish(1, acc[1], far_weights[1], far_vals[1], context)
    return context, pooled


def body(queries, keys, values, latent_keys, latent_values, pattern, doc_starts, doc_owner):
    rows, columns = queries.shape
    heads = columns // HD
    shards = lax.axis_size("seq")
    seq_index = lax.axis_index("seq")
    where = seq_index.astype(jnp.int32).reshape(1)
    levels = [j for j in range(LEVELS) if 2**j < shards]
    last = levels[-1]
    merged = 2 * 2**last >= shards
    rotate = shards <= 4

    def both_ways(value, distance):
        behind = lax.ppermute(value, "seq", [(s, s + distance) for s in range(shards - distance)])
        ahead = lax.ppermute(value, "seq", [(s, s - distance) for s in range(distance, shards)])
        return [behind, ahead]

    def far(value, near):
        if last != 1:
            return both_ways(value, 2**last)
        behind = lax.ppermute(near[0], "seq", [(s, s + 1) for s in range(1, shards - 1)])
        ahead = lax.ppermute(near[1], "seq", [(s, s - 1) for s in range(1, shards - 1)])
        return [behind, ahead]

    if shards == 4:
        return four_shards(queries, keys, values, latent_keys, latent_values, pattern, doc_starts, doc_owner)
    near_keys = both_ways(keys, 1)
    near_vals = both_ways(values, 1)
    state_shapes = (shape(rows, columns),) * 3
    lat = latent_call(where, doc_starts, queries, latent_keys, latent_values)
    state = own_call(queries, keys, values)
    near_keys, state = lax.optimization_barrier((near_keys, state))

    for level in levels[:-1]:
        if level == 0:
            got = near_keys + near_vals
        else:
            got = both_ways(keys, 2**level) + both_ways(values, 2**level)
        state = pl.pallas_call(
            functools.partial(near_kernel, shards, level),
            grid=(heads,),
            in_specs=smem(2) + [spec(rows)] * 8,
            out_specs=[spec(rows)] * 3,
            out_shape=state_shapes,
            input_output_aliases={7 + i: i for i in range(3)},
            compiler_params=PARAMS,
            cost_estimate=pl.CostEstimate(
                flops=8 * rows * columns * BLK, bytes_accessed=20 * rows * columns * 2, transcendentals=2 * heads * rows * BLK
            ),
            name="near",
        )(where, pattern, queries, *got, *state)

    far_keys = far(keys, near_keys)
    far_vals = far(values, near_vals)
    sources = 1 if merged else 2
    acc, *weights = pl.pallas_call(
        functools.partial(far_kernel, shards, last, merged),
        grid=(heads,),
        in_specs=smem(2) + [spec(rows)] * 6,
        out_specs=[spec(rows)] + [spec(rows, BLK)] * sources,
        out_shape=(shape(rows, columns),) + (shape(rows, heads * BLK, BF16),) * sources,
        input_output_aliases={5: 0},
        compiler_params=PARAMS,
        cost_estimate=pl.CostEstimate(
            flops=2 * sources * rows * columns * BLK,
            bytes_accessed=(10 + 3 * sources) * rows * columns * 2,
            transcendentals=sources * heads * rows * BLK,
        ),
        name="far",
    )(where, pattern, queries, *far_keys, *state)

    if rotate:
        sent = (shape(2, columns, BF16),) * shards
    else:
        sent = (jax.ShapeDtypeStruct((shards, 2, columns), BF16),)
    context, *means = pl.pallas_call(
        functools.partial(finish_kernel, shards, last, merged),
        in_specs=smem(3) + vmem(4 + sources),
        out_specs=vmem(1 + len(sent)),
        out_shape=(shape(rows, columns, BF16),) + sent,
        compiler_params=PARAMS,
        cost_estimate=pl.CostEstimate(
            flops=2 * sources * rows * columns * BLK, bytes_accessed=(3 + 3 * sources) * rows * columns * 2, transcendentals=0
        ),
        name="finish",
    )(where, doc_starts, doc_owner, acc, lat, *weights, *far_vals)

    if not rotate:
        return context, lax.all_to_all(means[0], "seq", split_axis=0, concat_axis=0, tiled=True)[None]
    got = [means[0]]
    for r in range(1, shards):
        got.append(lax.ppermute(means[r], "seq", [(s, (s + r) % shards) for s in range(shards)]))
    pooled = []
    for s in range(shards):
        back = lax.rem(seq_index - s + shards, shards)
        row = got[0]
        for r in range(1, shards):
            row = jnp.where(back == r, got[r], row)
        pooled.append(row)
    return context, jnp.stack(pooled)[None]


def solution(mesh):
    in_specs = (
        P(("groups", "seq"), ("head", "sub")),
        P(("groups", "seq"), ("head", "sub")),
        P(("groups", "seq"), ("head", "sub")),
        P("groups", ("head", "sub")),
        P("groups", ("head", "sub")),
        P(("groups", "seq"), None),
        P("groups"),
        P("groups"),
    )
    out_specs = (
        P(("groups", "seq"), ("head", "sub")),
        P(("groups", "seq"), None, None, ("head", "sub")),
    )
    return jax.shard_map(body, mesh=mesh, in_specs=in_specs, out_specs=out_specs, check_vma=False)
```

```python
import functools
import math

import jax
import jax.numpy as jnp
from jax import lax
from jax.experimental import pallas as pl
from jax.experimental.pallas import tpu as pltpu
from jax.sharding import PartitionSpec as P

HD = 128
LEVELS = 4
BLK = 256
PIECES = 4
SCALE = math.log2(math.e) / math.sqrt(HD)
PARAMS = pltpu.CompilerParams(vmem_limit_bytes=24 * 1024 * 1024)
F32 = jnp.float32
BF16 = jnp.bfloat16


def dot_t(a, b):
    return lax.dot_general(a, b, (((1,), (1,)), ((), ())), preferred_element_type=F32)


def dot(a, b):
    return jnp.dot(a, b, preferred_element_type=F32)


def doc_rows(rows, split):
    place = lax.broadcasted_iota(jnp.int32, rows.shape, 0)
    first = jnp.sum(jnp.where(place < split, rows, 0.0), axis=0, keepdims=True)
    second = jnp.sum(jnp.where(place < split, 0.0, rows), axis=0, keepdims=True)
    return jnp.concatenate((first, second), axis=0)


def own_kernel(q_ref, k_ref, v_ref, acc_ref, top_ref, sum_ref):
    for h in range(q_ref.shape[1] // HD):
        head = slice(h * HD, (h + 1) * HD)
        s = dot_t(q_ref[:, head], k_ref[:, head]) * SCALE
        top = jnp.max(s, axis=1, keepdims=True)
        e = jnp.exp2(s - top)
        acc = dot(e.astype(BF16), v_ref[:, head])
        acc_ref[:, head] = acc
        top_ref[:, head] = jnp.broadcast_to(top, acc.shape)
        sum_ref[:, head] = jnp.broadcast_to(jnp.sum(e, axis=1, keepdims=True), acc.shape)


def latent_kernel(where, starts, q_ref, lk_ref, lv_ref, lat_ref):
    for h in range(q_ref.shape[1] // HD):
        head = slice(h * HD, (h + 1) * HD)
        s = dot_t(q_ref[:, head], lk_ref[:, head]) * SCALE
        e = jnp.exp2(s - jnp.max(s, axis=1, keepdims=True))
        out = dot(e.astype(BF16), lv_ref[:, head]) / jnp.sum(e, axis=1, keepdims=True)
        piece = out.shape[0] // PIECES
        for p in range(PIECES):
            split = split_of(where, starts, p)
            lat_ref[2 * p : 2 * p + 2, head] = doc_rows(out[p * piece : (p + 1) * piece], split)


def split_of(where, starts, p, shard=None):
    first = 2 * (PIECES * (where[0] if shard is None else shard) + p)
    return starts[first + 1] - starts[first]


def slot_live(where, pattern, shards, level, side, block):
    partner = where[0] + (2 * side - 1) * 2**level
    return (pattern[block, 2 * level + side] == 1) & (partner >= 0) & (partner < shards)


def live_scores(live, q, k):
    return jnp.where(live, dot_t(q, k) * SCALE, -jnp.inf)


def near_kernel(shards, level, where, pattern, q_ref, kb_ref, ka_ref, vb_ref, va_ref, *refs):
    acc_in, top_in, sum_in, acc_ref, top_ref, sum_ref = refs
    for block in range(q_ref.shape[0] // BLK):
        rows = pl.ds(block * BLK, BLK)
        q = q_ref[rows, :]
        scores = [
            live_scores(slot_live(where, pattern, shards, level, side, block), q, k_ref[rows, :])
            for side, k_ref in enumerate((kb_ref, ka_ref))
        ]
        old = top_in[rows, :1]
        top = old
        for s in scores:
            top = jnp.maximum(top, jnp.max(s, axis=1, keepdims=True))
        shrink = jnp.exp2(old - top)
        total = sum_in[rows, :1] * shrink
        acc = acc_in[rows, :] * shrink
        for s, v_ref in zip(scores, (vb_ref, va_ref)):
            e = jnp.exp2(s - top)
            total = total + jnp.sum(e, axis=1, keepdims=True)
            acc = acc + dot(e.astype(BF16), v_ref[rows, :])
        acc_ref[rows, :] = acc
        top_ref[rows, :] = jnp.broadcast_to(top, acc.shape)
        sum_ref[rows, :] = jnp.broadcast_to(total, acc.shape)


def far_kernel(shards, level, merged, where, pattern, q_ref, kb_ref, ka_ref, acc_in, top_in, sum_in, acc_ref, *outs):
    behind = where[0] >= 2**level
    for block in range(q_ref.shape[0] // BLK):
        rows = pl.ds(block * BLK, BLK)
        q = q_ref[rows, :]
        live = [slot_live(where, pattern, shards, level, side, block) for side in range(2)]
        pair = [k_ref[rows, :] for k_ref in (kb_ref, ka_ref)]
        if merged:
            live = [(behind & live[0]) | (jnp.logical_not(behind) & live[1])]
            pair = [jnp.where(behind, pair[0], pair[1])]
        scores = [live_scores(on, q, k) for on, k in zip(live, pair)]
        old = top_in[rows, :1]
        top = old
        for s in scores:
            top = jnp.maximum(top, jnp.max(s, axis=1, keepdims=True))
        shrink = jnp.exp2(old - top)
        total = sum_in[rows, :1] * shrink
        exps = []
        for s in scores:
            e = jnp.exp2(s - top)
            total = total + jnp.sum(e, axis=1, keepdims=True)
            exps.append(e)
        inverse = 1.0 / total
        acc_ref[rows, :] = acc_in[rows, :] * (shrink * inverse)
        for e, out in zip(exps, outs):
            out[rows, :] = (e * inverse).astype(BF16)


def finish_kernel(shards, level, merged, where, starts, owners, acc_ref, lat_ref, *refs):
    sources = 1 if merged else 2
    weights, (vb_ref, va_ref) = refs[:sources], refs[sources : sources + 2]
    ctx_ref, outs = refs[sources + 2], refs[sources + 3 :]
    rows_here, columns = acc_ref.shape
    piece = rows_here // PIECES
    splits = [split_of(where, starts, p) for p in range(PIECES)]
    behind = where[0] >= 2**level
    sums = []
    for h in range(columns // HD):
        head = pl.ds(h * HD, HD)
        slots = pl.ds(h * BLK, BLK)
        found = []
        for block in range(rows_here // BLK):
            rows = pl.ds(block * BLK, BLK)
            pair = [v_ref[rows, head] for v_ref in (vb_ref, va_ref)]
            if merged:
                pair = [jnp.where(behind, pair[0], pair[1])]
            acc = acc_ref[rows, head]
            for w_ref, v in zip(weights, pair):
                acc = acc + dot(w_ref[rows, slots], v)
            ctx = acc.astype(BF16)
            ctx_ref[rows, head] = ctx
            ctx = ctx.astype(F32)
            for start in range(0, BLK, piece):
                found.append(doc_rows(ctx[start : start + piece], splits[len(found)]))
        sums.append(found)
    side = lax.broadcasted_iota(jnp.int32, (2, columns), 0)
    means = []
    for p in range(PIECES):
        count = jnp.where(side == 0, splits[p], piece - splits[p]).astype(F32)
        total = jnp.concatenate([found[p] for found in sums], axis=1) + lat_ref[2 * p : 2 * p + 2, :]
        means.append(total / count)
    for r in range(shards):
        if len(outs) == 1:
            target = r
        else:
            target = lax.rem(where[0] + r, shards)
        chosen = jnp.zeros((2, columns), F32)
        for p in range(PIECES):
            chosen = jnp.where(owners[2 * (PIECES * where[0] + p)] == target, means[p], chosen)
        if len(outs) == 1:
            outs[0][r] = chosen.astype(BF16)
        else:
            outs[r][...] = chosen.astype(BF16)


def weigh_kernel(shards, where, pattern, starts, q_ref, nb_ref, na_ref, fb_ref, fa_ref, *refs):
    acc_in, top_in, sum_in, acc_ref, wb_ref, wa_ref, wf_ref, sums_ref = refs
    behind = where[0] >= 2
    blocks = q_ref.shape[0] // BLK
    bias = []
    for block in range(blocks):
        far_live = [slot_live(where, pattern, shards, 1, side, block) for side in range(2)]
        live = [slot_live(where, pattern, shards, 0, side, block) for side in range(2)]
        live.append((behind & far_live[0]) | (jnp.logical_not(behind) & far_live[1]))
        bias.append([jnp.where(on, 0.0, -jnp.inf) for on in live])
    piece = q_ref.shape[0] // PIECES
    place = lax.broadcasted_iota(jnp.int32, (piece, HD), 0)
    firsts = [place < split_of(where, starts, p) for p in range(PIECES)]
    lanes = [slice(i * HD, (i + 1) * HD) for i in range(BLK // HD)]
    for h in range(q_ref.shape[1] // HD):
        head = slice(h * HD, (h + 1) * HD)
        for p in range(PIECES):
            rows = slice(p * piece, (p + 1) * piece)
            block = p * piece // BLK
            if p * piece % BLK == 0:
                held = slice(block * BLK, (block + 1) * BLK)
                far = jnp.where(behind, fb_ref[held, head], fa_ref[held, head])
                keys = [nb_ref[held, head], na_ref[held, head], far]
            q = q_ref[rows, head]
            scores = []
            for k, low in zip(keys, bias[block]):
                s = dot_t(q, k)
                scores += [s[:, part] * SCALE + low for part in lanes]
            old = top_in[rows, head]
            top = jnp.maximum(jnp.max(functools.reduce(jnp.maximum, scores), axis=1, keepdims=True), old)
            shrink = jnp.exp2(old - top)
            exps = [jnp.exp2(s - top) for s in scores]
            added = jnp.sum(functools.reduce(jnp.add, exps), axis=1, keepdims=True)
            inverse = 1.0 / (sum_in[rows, head] * shrink + added)
            acc_ref[rows, head] = acc_in[rows, head] * (shrink * inverse)
            for i, e in enumerate(exps):
                out = (wb_ref, wa_ref, wf_ref)[i // len(lanes)]
                first = h * BLK + i % len(lanes) * HD
                w = e * inverse
                out[rows, first : first + HD] = w.astype(BF16)
                if out is wf_ref:
                    sums = [jnp.sum(x, axis=0, keepdims=True) for x in (jnp.where(firsts[p], w, 0.0), jnp.where(firsts[p], 0.0, w))]
                    sums_ref[2 * p : 2 * p + 2, first : first + HD] = jnp.concatenate(sums, axis=0)


def doc_counts(split, piece, columns):
    side = lax.broadcasted_iota(jnp.int32, (2, columns), 0)
    return jnp.where(side == 0, split, piece - split).astype(F32)


def mix_kernel(block, where, starts, acc_in, wb_ref, wa_ref, vb_ref, va_ref, lat_ref, acc_ref, mean_ref):
    pieces = mean_ref.shape[0] // 2
    piece = BLK // pieces
    for h in range(acc_in.shape[1] // HD):
        head = slice(h * HD, (h + 1) * HD)
        slots = slice(h * BLK, (h + 1) * BLK)
        acc = acc_in[:, head] + dot(wb_ref[:, slots], vb_ref[:, head]) + dot(wa_ref[:, slots], va_ref[:, head])
        acc_ref[:, head] = acc
        for p in range(pieces):
            index = block * pieces + p
            split = split_of(where, starts, index)
            found = doc_rows(acc[p * piece : (p + 1) * piece], split) + lat_ref[2 * index : 2 * index + 2, head]
            mean_ref[2 * p : 2 * p + 2, head] = found / doc_counts(split, piece, HD)


def part_kernel(where, starts, sums_ref, v_ref, part_ref):
    piece = v_ref.shape[0] // PIECES
    per_block = BLK // piece
    partner = lax.rem(where[0] + 2, 4)
    counts = [doc_counts(split_of(where, starts, p, partner), piece, HD) for p in range(PIECES)]
    for h in range(v_ref.shape[1] // HD):
        head = slice(h * HD, (h + 1) * HD)
        sums = sums_ref[:, h * BLK : (h + 1) * BLK]
        found = [dot(sums.astype(BF16), v_ref[block * BLK : (block + 1) * BLK, head]) for block in range(v_ref.shape[0] // BLK)]
        for p in range(PIECES):
            rows = slice(2 * p, 2 * p + 2)
            part_ref[rows, head] = found[p // per_block][rows] / counts[p]


def route_kernel(where, owners, part_ref, *refs):
    mean_refs, out_ref = refs[:-1], refs[-1]
    here, partner = where[0], lax.rem(where[0] + 2, 4)
    means = jnp.concatenate([mean_ref[...] for mean_ref in mean_refs], axis=0)
    parts = part_ref[...]
    for target in range(out_ref.shape[0]):
        rows = []
        for group, shard in ((means, here), (parts, partner)):
            chosen = jnp.zeros((2, out_ref.shape[2]), F32)
            for p in range(PIECES):
                chosen = jnp.where(owners[2 * (PIECES * shard + p)] == target, group[2 * p : 2 * p + 2], chosen)
            rows.append(chosen)
        out_ref[target] = jnp.concatenate(rows, axis=0).astype(BF16)


def context_kernel(block, where, acc_ref, w_ref, vb_ref, va_ref, *refs):
    stage, sem = refs[-2:]
    if len(refs) == 3:
        out_ref = refs[0]
    else:
        got_ref, _, out_ref, pooled_ref = refs[:4]
    behind = where[0] >= 2
    copies = []
    for h in range(acc_ref.shape[1] // HD):
        head = pl.ds(h * HD, HD)
        v = jnp.where(behind, vb_ref[:, head], va_ref[:, head])
        stage[:, head] = (acc_ref[:, head] + dot(w_ref[pl.ds(block * BLK, BLK), pl.ds(h * BLK, BLK)], v)).astype(BF16)
        if h % 2:
            pair = pl.ds((h - 1) * HD, 2 * HD)
            copy = pltpu.make_async_copy(stage.at[:, pair], out_ref.at[pl.ds(block * BLK, BLK), pair], sem.at[h // 2])
            copy.start()
            copies.append(copy)
    if len(refs) > 3:
        got = [got_ref[s].astype(F32) for s in range(4)]
        for s in range(4):
            pooled_ref[0, s] = (got[s][:2] + got[s ^ 2][2:]).astype(BF16)
    for copy in copies:
        copy.wait()


def spec(rows, columns=HD):
    return pl.BlockSpec((rows, columns), lambda h: (0, h))


def smem(count):
    return [pl.BlockSpec(memory_space=pltpu.SMEM)] * count


def vmem(count):
    return [pl.BlockSpec(memory_space=pltpu.VMEM)] * count


def shape(rows, columns, kind=F32):
    return jax.ShapeDtypeStruct((rows, columns), kind)


def step_of(heads):
    return 2 if heads % 2 == 0 else 1


def own_call(queries, keys, values):
    rows, columns = queries.shape
    heads = columns // HD
    wide = step_of(heads) * HD
    return pl.pallas_call(
        own_kernel,
        grid=(columns // wide,),
        in_specs=[spec(rows, wide)] * 3,
        out_specs=[spec(rows, wide)] * 3,
        out_shape=(shape(rows, columns),) * 3,
        compiler_params=PARAMS,
        cost_estimate=pl.CostEstimate(
            flops=4 * rows * columns * rows, bytes_accessed=18 * rows * columns, transcendentals=heads * rows * rows
        ),
        name="own",
    )(queries, keys, values)


def latent_call(where, doc_starts, queries, latent_keys, latent_values, first=0, last=None):
    rows, columns = queries.shape
    latents = latent_keys.shape[0]
    wide = step_of(columns // HD) * HD
    steps = (last or columns // wide) - first
    return pl.pallas_call(
        latent_kernel,
        grid=(steps,),
        in_specs=smem(2) + [pl.BlockSpec((size, wide), lambda h: (0, h + first)) for size in (rows, latents, latents)],
        out_specs=spec(2 * PIECES, wide),
        out_shape=shape(2 * PIECES, steps * wide),
        compiler_params=PARAMS,
        cost_estimate=pl.CostEstimate(
            flops=4 * rows * steps * wide * latents * (1 if first == 0 else 10),
            bytes_accessed=6 * rows * steps * wide,
            transcendentals=steps * wide // HD * rows * latents,
        ),
        name="latent",
    )(where, doc_starts, queries, latent_keys, latent_values)


def four_shards(queries, keys, values, latent_keys, latent_values, pattern, doc_starts, doc_owner):
    rows, columns = queries.shape
    heads = columns // HD
    step = step_of(heads)
    wide = step * HD
    slots = heads * BLK
    blocks = rows // BLK
    docs = 2 * PIECES // blocks
    where = lax.axis_index("seq").astype(jnp.int32).reshape(1)
    right, left = [(0, 1), (1, 2), (2, 3)], [(1, 0), (2, 1), (3, 2)]

    def move(value, pairs):
        return lax.ppermute(value, "seq", pairs)

    def near(value):
        return [move(value, right), move(value, left)]

    def onward(pair):
        return [move(pair[0], right[1:]), move(pair[1], left[:-1])]

    def part(array, block):
        return array[block * BLK : (block + 1) * BLK]

    def row_spec(block, width=wide):
        return pl.BlockSpec((BLK, width), lambda h: (block, h))

    def weigh(near_keys, far_keys, state):
        return pl.pallas_call(
            functools.partial(weigh_kernel, 4),
            grid=(heads // step,),
            in_specs=smem(3) + [spec(rows, wide)] * 8,
            out_specs=[spec(rows, wide)] + [spec(rows, step * BLK)] * 3 + [spec(2 * PIECES, step * BLK)],
            out_shape=(shape(rows, columns),) + (shape(rows, slots, BF16),) * 3 + (shape(2 * PIECES, slots),),
            compiler_params=PARAMS,
            cost_estimate=pl.CostEstimate(
                flops=6 * rows * columns * BLK, bytes_accessed=22 * rows * columns, transcendentals=3 * heads * rows * BLK
            ),
            name="weigh",
        )(where, pattern, doc_starts, queries, *near_keys, *far_keys, *state)

    def mix(block, acc, weights, near_vals, lat):
        return pl.pallas_call(
            functools.partial(mix_kernel, block),
            grid=(heads // step,),
            in_specs=smem(2)
            + [row_spec(block)]
            + [row_spec(block, step * BLK)] * 2
            + [row_spec(0)] * 2
            + [spec(2 * PIECES, wide)],
            out_specs=[row_spec(0), spec(docs, wide)],
            out_shape=(shape(BLK, columns), shape(docs, columns)),
            compiler_params=PARAMS,
            cost_estimate=pl.CostEstimate(flops=4 * BLK * columns * BLK, bytes_accessed=20 * BLK * columns, transcendentals=0),
            name="mix",
        )(where, doc_starts, acc, *weights, *near_vals, lat)

    def finish(block, acc, weights, far_vals, held):
        context = shape(rows, columns, BF16)
        pooled = jax.ShapeDtypeStruct((1, 4, 2, columns), BF16)
        anywhere = pl.BlockSpec(memory_space=pl.ANY)
        whole = pl.BlockSpec(memory_space=pltpu.VMEM)
        return pl.pallas_call(
            functools.partial(context_kernel, block),
            in_specs=smem(1) + vmem(4) + ([whole, anywhere] if held else []),
            out_specs=[anywhere, whole] if held else anywhere,
            out_shape=(context, pooled) if held else context,
            scratch_shapes=[pltpu.VMEM((BLK, columns), BF16), pltpu.SemaphoreType.DMA((heads // 2,))],
            input_output_aliases={6: 0} if held else {},
            compiler_params=PARAMS,
            cost_estimate=pl.CostEstimate(flops=2 * BLK * columns * BLK, bytes_accessed=14 * BLK * columns, transcendentals=0),
            name="finish",
        )(where, acc, weights, *far_vals, *held)

    near_keys = near(keys)
    lats = [latent_call(where, doc_starts, queries, latent_keys, latent_values, 0, 1)]
    lats, late_vals, late_queries = lax.optimization_barrier((lats, values, queries))
    near_vals = [near(part(late_vals, 0))]
    state = own_call(late_queries, keys, values)
    near_keys, state = lax.optimization_barrier((near_keys, state))
    far_keys = onward(near_keys)
    near_vals[0], late_vals, late_queries = lax.optimization_barrier((near_vals[0], late_vals, late_queries))
    lats.append(latent_call(where, doc_starts, late_queries, latent_keys, latent_values, 1))
    lat = jnp.concatenate(lats, axis=1)
    near_vals.append(near(part(late_vals, 1)))
    far_keys, lat = lax.optimization_barrier((far_keys, lat))
    weighed = weigh(near_keys, far_keys, state)
    near_vals[1], weighed = lax.optimization_barrier((near_vals[1], weighed))
    acc, *near_weights, far_weights, sums = weighed
    sums = move(sums, [(s, s ^ 2) for s in range(4)])
    far_vals = [onward(near_vals[0])]
    mixed = [mix(0, acc, near_weights, near_vals[0], lat)]
    near_vals[1], mixed[0] = lax.optimization_barrier((near_vals[1], mixed[0]))
    far_vals.append(onward(near_vals[1]))
    parts = pl.pallas_call(
        part_kernel,
        grid=(heads // step,),
        in_specs=smem(2) + [spec(2 * PIECES, step * BLK), spec(rows, wide)],
        out_specs=spec(2 * PIECES, wide),
        out_shape=shape(2 * PIECES, columns),
        compiler_params=PARAMS,
        cost_estimate=pl.CostEstimate(flops=64 * rows * columns * 128, bytes_accessed=3 * rows * columns, transcendentals=0),
        name="part",
    )(where, doc_starts, sums, values)
    acc, parts = lax.optimization_barrier((acc, parts))
    mixed.append(mix(1, acc, near_weights, near_vals[1], lat))
    sent = pl.pallas_call(
        route_kernel,
        in_specs=smem(2) + vmem(3),
        out_specs=pl.BlockSpec(memory_space=pltpu.VMEM),
        out_shape=jax.ShapeDtypeStruct((4, 4, columns), BF16),
        compiler_params=PARAMS,
        name="route",
    )(where, doc_owner, parts, *[m[1] for m in mixed])
    mixed[0], parts = lax.optimization_barrier((mixed[0], parts))
    context = finish(0, mixed[0][0], far_weights, far_vals[0], [])
    sent, context = lax.optimization_barrier((sent, context))
    got = lax.all_to_all(sent, "seq", split_axis=0, concat_axis=0, tiled=True)
    return finish(1, mixed[1][0], far_weights, far_vals[1], [got, context])


def body(queries, keys, values, latent_keys, latent_values, pattern, doc_starts, doc_owner):
    rows, columns = queries.shape
    heads = columns // HD
    shards = lax.axis_size("seq")
    seq_index = lax.axis_index("seq")
    where = seq_index.astype(jnp.int32).reshape(1)
    levels = [j for j in range(LEVELS) if 2**j < shards]
    last = levels[-1]
    merged = 2 * 2**last >= shards
    rotate = shards <= 4

    def both_ways(value, distance):
        behind = lax.ppermute(value, "seq", [(s, s + distance) for s in range(shards - distance)])
        ahead = lax.ppermute(value, "seq", [(s, s - distance) for s in range(distance, shards)])
        return [behind, ahead]

    def far(value, near):
        if last != 1:
            return both_ways(value, 2**last)
        behind = lax.ppermute(near[0], "seq", [(s, s + 1) for s in range(1, shards - 1)])
        ahead = lax.ppermute(near[1], "seq", [(s, s - 1) for s in range(1, shards - 1)])
        return [behind, ahead]

    if shards == 4:
        return four_shards(queries, keys, values, latent_keys, latent_values, pattern, doc_starts, doc_owner)
    near_keys = both_ways(keys, 1)
    near_vals = both_ways(values, 1)
    state_shapes = (shape(rows, columns),) * 3
    lat = latent_call(where, doc_starts, queries, latent_keys, latent_values)
    state = own_call(queries, keys, values)
    near_keys, state = lax.optimization_barrier((near_keys, state))

    for level in levels[:-1]:
        if level == 0:
            got = near_keys + near_vals
        else:
            got = both_ways(keys, 2**level) + both_ways(values, 2**level)
        state = pl.pallas_call(
            functools.partial(near_kernel, shards, level),
            grid=(heads,),
            in_specs=smem(2) + [spec(rows)] * 8,
            out_specs=[spec(rows)] * 3,
            out_shape=state_shapes,
            input_output_aliases={7 + i: i for i in range(3)},
            compiler_params=PARAMS,
            cost_estimate=pl.CostEstimate(
                flops=8 * rows * columns * BLK, bytes_accessed=20 * rows * columns * 2, transcendentals=2 * heads * rows * BLK
            ),
            name="near",
        )(where, pattern, queries, *got, *state)

    far_keys = far(keys, near_keys)
    far_vals = far(values, near_vals)
    sources = 1 if merged else 2
    acc, *weights = pl.pallas_call(
        functools.partial(far_kernel, shards, last, merged),
        grid=(heads,),
        in_specs=smem(2) + [spec(rows)] * 6,
        out_specs=[spec(rows)] + [spec(rows, BLK)] * sources,
        out_shape=(shape(rows, columns),) + (shape(rows, heads * BLK, BF16),) * sources,
        input_output_aliases={5: 0},
        compiler_params=PARAMS,
        cost_estimate=pl.CostEstimate(
            flops=2 * sources * rows * columns * BLK,
            bytes_accessed=(10 + 3 * sources) * rows * columns * 2,
            transcendentals=sources * heads * rows * BLK,
        ),
        name="far",
    )(where, pattern, queries, *far_keys, *state)

    if rotate:
        sent = (shape(2, columns, BF16),) * shards
    else:
        sent = (jax.ShapeDtypeStruct((shards, 2, columns), BF16),)
    context, *means = pl.pallas_call(
        functools.partial(finish_kernel, shards, last, merged),
        in_specs=smem(3) + vmem(4 + sources),
        out_specs=vmem(1 + len(sent)),
        out_shape=(shape(rows, columns, BF16),) + sent,
        compiler_params=PARAMS,
        cost_estimate=pl.CostEstimate(
            flops=2 * sources * rows * columns * BLK, bytes_accessed=(3 + 3 * sources) * rows * columns * 2, transcendentals=0
        ),
        name="finish",
    )(where, doc_starts, doc_owner, acc, lat, *weights, *far_vals)

    if not rotate:
        return context, lax.all_to_all(means[0], "seq", split_axis=0, concat_axis=0, tiled=True)[None]
    got = [means[0]]
    for r in range(1, shards):
        got.append(lax.ppermute(means[r], "seq", [(s, (s + r) % shards) for s in range(shards)]))
    pooled = []
    for s in range(shards):
        back = lax.rem(seq_index - s + shards, shards)
        row = got[0]
        for r in range(1, shards):
            row = jnp.where(back == r, got[r], row)
        pooled.append(row)
    return context, jnp.stack(pooled)[None]


def solution(mesh):
    in_specs = (
        P(("groups", "seq"), ("head", "sub")),
        P(("groups", "seq"), ("head", "sub")),
        P(("groups", "seq"), ("head", "sub")),
        P("groups", ("head", "sub")),
        P("groups", ("head", "sub")),
        P(("groups", "seq"), None),
        P("groups"),
        P("groups"),
    )
    out_specs = (
        P(("groups", "seq"), ("head", "sub")),
        P(("groups", "seq"), None, None, ("head", "sub")),
    )
    return jax.shard_map(body, mesh=mesh, in_specs=in_specs, out_specs=out_specs, check_vma=False)
```

```python
import functools
import math

import jax
import jax.numpy as jnp
from jax import lax
from jax.experimental import pallas as pl
from jax.experimental.pallas import tpu as pltpu
from jax.sharding import PartitionSpec as P

HD = 128
LEVELS = 4
BLK = 256
PIECES = 4
SCALE = math.log2(math.e) / math.sqrt(HD)
PARAMS = pltpu.CompilerParams(vmem_limit_bytes=16 * 1024 * 1024)
F32 = jnp.float32
BF16 = jnp.bfloat16


def dot_t(a, b):
    return lax.dot_general(a, b, (((1,), (1,)), ((), ())), preferred_element_type=F32)


def dot(a, b):
    return jnp.dot(a, b, preferred_element_type=F32)


def doc_rows(rows, split):
    place = lax.broadcasted_iota(jnp.int32, rows.shape, 0)
    first = jnp.sum(jnp.where(place < split, rows, 0.0), axis=0, keepdims=True)
    second = jnp.sum(jnp.where(place < split, 0.0, rows), axis=0, keepdims=True)
    return jnp.concatenate((first, second), axis=0)


def own_kernel(q_ref, k_ref, v_ref, acc_ref, top_ref, sum_ref):
    for h in range(q_ref.shape[1] // HD):
        head = slice(h * HD, (h + 1) * HD)
        s = dot_t(q_ref[:, head], k_ref[:, head]) * SCALE
        top = jnp.max(s, axis=1, keepdims=True)
        e = jnp.exp2(s - top)
        acc = dot(e.astype(BF16), v_ref[:, head])
        acc_ref[:, head] = acc
        top_ref[:, head] = jnp.broadcast_to(top, acc.shape)
        sum_ref[:, head] = jnp.broadcast_to(jnp.sum(e, axis=1, keepdims=True), acc.shape)


def latent_kernel(where, starts, q_ref, lk_ref, lv_ref, lat_ref):
    for h in range(q_ref.shape[1] // HD):
        head = slice(h * HD, (h + 1) * HD)
        s = dot_t(q_ref[:, head], lk_ref[:, head]) * SCALE
        e = jnp.exp2(s - jnp.max(s, axis=1, keepdims=True))
        out = dot(e.astype(BF16), lv_ref[:, head]) / jnp.sum(e, axis=1, keepdims=True)
        piece = out.shape[0] // PIECES
        for p in range(PIECES):
            split = split_of(where, starts, p)
            lat_ref[2 * p : 2 * p + 2, head] = doc_rows(out[p * piece : (p + 1) * piece], split)


def split_of(where, starts, p, shard=None):
    first = 2 * (PIECES * (where[0] if shard is None else shard) + p)
    return starts[first + 1] - starts[first]


def slot_live(where, pattern, shards, level, side, block):
    partner = where[0] + (2 * side - 1) * 2**level
    return (pattern[block, 2 * level + side] == 1) & (partner >= 0) & (partner < shards)


def live_scores(live, q, k):
    return jnp.where(live, dot_t(q, k) * SCALE, -jnp.inf)


def near_kernel(shards, level, where, pattern, q_ref, kb_ref, ka_ref, vb_ref, va_ref, *refs):
    acc_in, top_in, sum_in, acc_ref, top_ref, sum_ref = refs
    for block in range(q_ref.shape[0] // BLK):
        rows = pl.ds(block * BLK, BLK)
        q = q_ref[rows, :]
        scores = [
            live_scores(slot_live(where, pattern, shards, level, side, block), q, k_ref[rows, :])
            for side, k_ref in enumerate((kb_ref, ka_ref))
        ]
        old = top_in[rows, :1]
        top = old
        for s in scores:
            top = jnp.maximum(top, jnp.max(s, axis=1, keepdims=True))
        shrink = jnp.exp2(old - top)
        total = sum_in[rows, :1] * shrink
        acc = acc_in[rows, :] * shrink
        for s, v_ref in zip(scores, (vb_ref, va_ref)):
            e = jnp.exp2(s - top)
            total = total + jnp.sum(e, axis=1, keepdims=True)
            acc = acc + dot(e.astype(BF16), v_ref[rows, :])
        acc_ref[rows, :] = acc
        top_ref[rows, :] = jnp.broadcast_to(top, acc.shape)
        sum_ref[rows, :] = jnp.broadcast_to(total, acc.shape)


def far_kernel(shards, level, merged, where, pattern, q_ref, kb_ref, ka_ref, acc_in, top_in, sum_in, acc_ref, *outs):
    behind = where[0] >= 2**level
    for block in range(q_ref.shape[0] // BLK):
        rows = pl.ds(block * BLK, BLK)
        q = q_ref[rows, :]
        live = [slot_live(where, pattern, shards, level, side, block) for side in range(2)]
        pair = [k_ref[rows, :] for k_ref in (kb_ref, ka_ref)]
        if merged:
            live = [(behind & live[0]) | (jnp.logical_not(behind) & live[1])]
            pair = [jnp.where(behind, pair[0], pair[1])]
        scores = [live_scores(on, q, k) for on, k in zip(live, pair)]
        old = top_in[rows, :1]
        top = old
        for s in scores:
            top = jnp.maximum(top, jnp.max(s, axis=1, keepdims=True))
        shrink = jnp.exp2(old - top)
        total = sum_in[rows, :1] * shrink
        exps = []
        for s in scores:
            e = jnp.exp2(s - top)
            total = total + jnp.sum(e, axis=1, keepdims=True)
            exps.append(e)
        inverse = 1.0 / total
        acc_ref[rows, :] = acc_in[rows, :] * (shrink * inverse)
        for e, out in zip(exps, outs):
            out[rows, :] = (e * inverse).astype(BF16)


def finish_kernel(shards, level, merged, where, starts, owners, acc_ref, lat_ref, *refs):
    sources = 1 if merged else 2
    weights, (vb_ref, va_ref) = refs[:sources], refs[sources : sources + 2]
    ctx_ref, outs = refs[sources + 2], refs[sources + 3 :]
    rows_here, columns = acc_ref.shape
    piece = rows_here // PIECES
    splits = [split_of(where, starts, p) for p in range(PIECES)]
    behind = where[0] >= 2**level
    sums = []
    for h in range(columns // HD):
        head = pl.ds(h * HD, HD)
        slots = pl.ds(h * BLK, BLK)
        found = []
        for block in range(rows_here // BLK):
            rows = pl.ds(block * BLK, BLK)
            pair = [v_ref[rows, head] for v_ref in (vb_ref, va_ref)]
            if merged:
                pair = [jnp.where(behind, pair[0], pair[1])]
            acc = acc_ref[rows, head]
            for w_ref, v in zip(weights, pair):
                acc = acc + dot(w_ref[rows, slots], v)
            ctx = acc.astype(BF16)
            ctx_ref[rows, head] = ctx
            ctx = ctx.astype(F32)
            for start in range(0, BLK, piece):
                found.append(doc_rows(ctx[start : start + piece], splits[len(found)]))
        sums.append(found)
    side = lax.broadcasted_iota(jnp.int32, (2, columns), 0)
    means = []
    for p in range(PIECES):
        count = jnp.where(side == 0, splits[p], piece - splits[p]).astype(F32)
        total = jnp.concatenate([found[p] for found in sums], axis=1) + lat_ref[2 * p : 2 * p + 2, :]
        means.append(total / count)
    for r in range(shards):
        if len(outs) == 1:
            target = r
        else:
            target = lax.rem(where[0] + r, shards)
        chosen = jnp.zeros((2, columns), F32)
        for p in range(PIECES):
            chosen = jnp.where(owners[2 * (PIECES * where[0] + p)] == target, means[p], chosen)
        if len(outs) == 1:
            outs[0][r] = chosen.astype(BF16)
        else:
            outs[r][...] = chosen.astype(BF16)


def weigh_kernel(shards, where, pattern, starts, q_ref, nb_ref, na_ref, fb_ref, fa_ref, *refs):
    acc_in, top_in, sum_in, acc_ref, wb_ref, wa_ref, wf_ref, sums_ref = refs
    behind = where[0] >= 2
    blocks = q_ref.shape[0] // BLK
    bias = []
    for block in range(blocks):
        far_live = [slot_live(where, pattern, shards, 1, side, block) for side in range(2)]
        live = [slot_live(where, pattern, shards, 0, side, block) for side in range(2)]
        live.append((behind & far_live[0]) | (jnp.logical_not(behind) & far_live[1]))
        bias.append([jnp.where(on, 0.0, -jnp.inf) for on in live])
    piece = q_ref.shape[0] // PIECES
    place = lax.broadcasted_iota(jnp.int32, (piece, HD), 0)
    firsts = [place < split_of(where, starts, p) for p in range(PIECES)]
    lanes = [slice(i * HD, (i + 1) * HD) for i in range(BLK // HD)]
    for h in range(q_ref.shape[1] // HD):
        head = slice(h * HD, (h + 1) * HD)
        sums = [[] for _ in lanes]
        for p in range(PIECES):
            rows = slice(p * piece, (p + 1) * piece)
            block = p * piece // BLK
            if p * piece % BLK == 0:
                held = slice(block * BLK, (block + 1) * BLK)
                far = jnp.where(behind, fb_ref[held, head], fa_ref[held, head])
                keys = [nb_ref[held, head], na_ref[held, head], far]
            q = q_ref[rows, head]
            scores = []
            for k, low in zip(keys, bias[block]):
                s = dot_t(q, k)
                scores += [s[:, part] * SCALE + low for part in lanes]
            old = top_in[rows, head]
            top = jnp.maximum(jnp.max(functools.reduce(jnp.maximum, scores), axis=1, keepdims=True), old)
            shrink = jnp.exp2(old - top)
            exps = [jnp.exp2(s - top) for s in scores]
            added = jnp.sum(functools.reduce(jnp.add, exps), axis=1, keepdims=True)
            inverse = 1.0 / (sum_in[rows, head] * shrink + added)
            acc_ref[rows, head] = acc_in[rows, head] * (shrink * inverse)
            for i, e in enumerate(exps):
                out = (wb_ref, wa_ref, wf_ref)[i // len(lanes)]
                first = h * BLK + i % len(lanes) * HD
                w = e * inverse
                out[rows, first : first + HD] = w.astype(BF16)
                if out is wf_ref:
                    sums[i % len(lanes)] += [
                        jnp.sum(jnp.where(firsts[p], w, 0.0), axis=0, keepdims=True),
                        jnp.sum(jnp.where(firsts[p], 0.0, w), axis=0, keepdims=True),
                    ]
        for i, found in enumerate(sums):
            first = h * BLK + i * HD
            sums_ref[:, first : first + HD] = jnp.concatenate(found, axis=0).astype(sums_ref.dtype)


def doc_counts(split, piece, columns):
    side = lax.broadcasted_iota(jnp.int32, (2, columns), 0)
    return jnp.where(side == 0, split, piece - split).astype(F32)


def mix_kernel(block, where, starts, acc_in, wb_ref, wa_ref, vb_ref, va_ref, lat_ref, acc_ref, mean_ref):
    pieces = mean_ref.shape[0] // 2
    piece = BLK // pieces
    for h in range(acc_in.shape[1] // HD):
        head = slice(h * HD, (h + 1) * HD)
        slots = slice(h * BLK, (h + 1) * BLK)
        acc = acc_in[:, head] + dot(wb_ref[:, slots], vb_ref[:, head]) + dot(wa_ref[:, slots], va_ref[:, head])
        acc_ref[:, head] = acc
        for p in range(pieces):
            index = block * pieces + p
            split = split_of(where, starts, index)
            found = doc_rows(acc[p * piece : (p + 1) * piece], split) + lat_ref[2 * index : 2 * index + 2, head]
            mean_ref[2 * p : 2 * p + 2, head] = found / doc_counts(split, piece, HD)


def part_kernel(where, starts, sums_ref, v_ref, part_ref):
    piece = v_ref.shape[0] // PIECES
    per_block = BLK // piece
    partner = lax.rem(where[0] + 2, 4)
    counts = [doc_counts(split_of(where, starts, p, partner), piece, HD) for p in range(PIECES)]
    for h in range(v_ref.shape[1] // HD):
        head = slice(h * HD, (h + 1) * HD)
        sums = sums_ref[:, h * BLK : (h + 1) * BLK]
        found = [dot(sums.astype(BF16), v_ref[block * BLK : (block + 1) * BLK, head]) for block in range(v_ref.shape[0] // BLK)]
        for p in range(PIECES):
            rows = slice(2 * p, 2 * p + 2)
            part_ref[rows, head] = found[p // per_block][rows] / counts[p]


def route_kernel(where, owners, part_ref, *refs):
    mean_refs, out_ref = refs[:-1], refs[-1]
    here, partner = where[0], lax.rem(where[0] + 2, 4)
    means = jnp.concatenate([mean_ref[...] for mean_ref in mean_refs], axis=0)
    parts = part_ref[...]
    for target in range(out_ref.shape[0]):
        rows = []
        for group, shard in ((means, here), (parts, partner)):
            chosen = jnp.zeros((2, out_ref.shape[2]), F32)
            for p in range(PIECES):
                chosen = jnp.where(owners[2 * (PIECES * shard + p)] == target, group[2 * p : 2 * p + 2], chosen)
            rows.append(chosen)
        out_ref[target] = jnp.concatenate(rows, axis=0).astype(BF16)


def pool_kernel(got_ref, out_ref):
    got = [got_ref[s].astype(F32) for s in range(4)]
    for s in range(4):
        out_ref[0, s] = (got[s][:2] + got[s ^ 2][2:]).astype(BF16)


def context_kernel(block, where, acc_ref, w_ref, vb_ref, va_ref, *refs):
    out_ref, stage, sem = refs[-3:]
    behind = where[0] >= 2
    copies = []
    for h in range(acc_ref.shape[1] // HD):
        head = pl.ds(h * HD, HD)
        v = jnp.where(behind, vb_ref[:, head], va_ref[:, head])
        stage[:, head] = (acc_ref[:, head] + dot(w_ref[pl.ds(block * BLK, BLK), pl.ds(h * BLK, BLK)], v)).astype(BF16)
        if h % 2:
            pair = pl.ds((h - 1) * HD, 2 * HD)
            copy = pltpu.make_async_copy(stage.at[:, pair], out_ref.at[pl.ds(block * BLK, BLK), pair], sem.at[h // 2])
            copy.start()
            copies.append(copy)
    for copy in copies:
        copy.wait()


def spec(rows, columns=HD):
    return pl.BlockSpec((rows, columns), lambda h: (0, h))


def smem(count):
    return [pl.BlockSpec(memory_space=pltpu.SMEM)] * count


def vmem(count):
    return [pl.BlockSpec(memory_space=pltpu.VMEM)] * count


def shape(rows, columns, kind=F32):
    return jax.ShapeDtypeStruct((rows, columns), kind)


def step_of(heads):
    return 2 if heads % 2 == 0 else 1


def own_call(queries, keys, values):
    rows, columns = queries.shape
    heads = columns // HD
    wide = step_of(heads) * HD
    return pl.pallas_call(
        own_kernel,
        grid=(columns // wide,),
        in_specs=[spec(rows, wide)] * 3,
        out_specs=[spec(rows, wide)] * 3,
        out_shape=(shape(rows, columns),) * 3,
        compiler_params=PARAMS,
        cost_estimate=pl.CostEstimate(
            flops=4 * rows * columns * rows, bytes_accessed=18 * rows * columns, transcendentals=heads * rows * rows
        ),
        name="own",
    )(queries, keys, values)


def latent_call(where, doc_starts, queries, latent_keys, latent_values, first=0, last=None):
    rows, columns = queries.shape
    latents = latent_keys.shape[0]
    wide = step_of(columns // HD) * HD
    steps = (last or columns // wide) - first
    return pl.pallas_call(
        latent_kernel,
        grid=(steps,),
        in_specs=smem(2) + [pl.BlockSpec((size, wide), lambda h: (0, h + first)) for size in (rows, latents, latents)],
        out_specs=spec(2 * PIECES, wide),
        out_shape=shape(2 * PIECES, steps * wide),
        compiler_params=PARAMS,
        cost_estimate=pl.CostEstimate(
            flops=4 * rows * steps * wide * latents * (1 if first == 0 else 10),
            bytes_accessed=6 * rows * steps * wide,
            transcendentals=steps * wide // HD * rows * latents,
        ),
        name="latent",
    )(where, doc_starts, queries, latent_keys, latent_values)


def four_shards(queries, keys, values, latent_keys, latent_values, pattern, doc_starts, doc_owner):
    rows, columns = queries.shape
    heads = columns // HD
    step = step_of(heads)
    wide = step * HD
    slots = heads * BLK
    blocks = rows // BLK
    docs = 2 * PIECES // blocks
    where = lax.axis_index("seq").astype(jnp.int32).reshape(1)
    right, left = [(0, 1), (1, 2), (2, 3)], [(1, 0), (2, 1), (3, 2)]

    def move(value, pairs):
        return lax.ppermute(value, "seq", pairs)

    def near(value):
        return [move(value, right), move(value, left)]

    def onward(pair):
        return [move(pair[0], right[1:]), move(pair[1], left[:-1])]

    def part(array, block):
        return array[block * BLK : (block + 1) * BLK]

    def row_spec(block, width=wide):
        return pl.BlockSpec((BLK, width), lambda h: (block, h))

    def weigh(near_keys, far_keys, state):
        return pl.pallas_call(
            functools.partial(weigh_kernel, 4),
            grid=(heads // step,),
            in_specs=smem(3) + [spec(rows, wide)] * 8,
            out_specs=[spec(rows, wide)] + [spec(rows, step * BLK)] * 3 + [spec(2 * PIECES, step * BLK)],
            out_shape=(shape(rows, columns),) + (shape(rows, slots, BF16),) * 3 + (shape(2 * PIECES, slots, BF16),),
            compiler_params=PARAMS,
            cost_estimate=pl.CostEstimate(
                flops=6 * rows * columns * BLK, bytes_accessed=22 * rows * columns, transcendentals=3 * heads * rows * BLK
            ),
            name="weigh",
        )(where, pattern, doc_starts, queries, *near_keys, *far_keys, *state)

    def mix(block, acc, weights, near_vals, lat):
        return pl.pallas_call(
            functools.partial(mix_kernel, block),
            grid=(heads // step,),
            in_specs=smem(2)
            + [row_spec(block)]
            + [row_spec(block, step * BLK)] * 2
            + [row_spec(0)] * 2
            + [spec(2 * PIECES, wide)],
            out_specs=[row_spec(0), spec(docs, wide)],
            out_shape=(shape(BLK, columns), shape(docs, columns)),
            compiler_params=PARAMS,
            cost_estimate=pl.CostEstimate(flops=4 * BLK * columns * BLK, bytes_accessed=20 * BLK * columns, transcendentals=0),
            name="mix",
        )(where, doc_starts, acc, *weights, *near_vals, lat)

    def finish(block, acc, weights, far_vals, context):
        held = [] if context is None else [context]
        anywhere = pl.BlockSpec(memory_space=pl.ANY)
        return pl.pallas_call(
            functools.partial(context_kernel, block),
            in_specs=smem(1) + vmem(4) + [anywhere] * len(held),
            out_specs=anywhere,
            out_shape=shape(rows, columns, BF16),
            scratch_shapes=[pltpu.VMEM((BLK, columns), BF16), pltpu.SemaphoreType.DMA((heads // 2,))],
            input_output_aliases={5: 0} if held else {},
            compiler_params=PARAMS,
            cost_estimate=pl.CostEstimate(flops=2 * BLK * columns * BLK, bytes_accessed=14 * BLK * columns, transcendentals=0),
            name="finish",
        )(where, acc, weights, *far_vals, *held)

    near_keys = near(keys)
    lats = [latent_call(where, doc_starts, queries, latent_keys, latent_values, 0, 1)]
    lats, late_vals, late_queries = lax.optimization_barrier((lats, values, queries))
    near_vals = [near(part(late_vals, 0))]
    state = own_call(late_queries, keys, values)
    near_keys, state = lax.optimization_barrier((near_keys, state))
    far_keys = onward(near_keys)
    near_vals[0], late_vals, late_queries = lax.optimization_barrier((near_vals[0], late_vals, late_queries))
    lats.append(latent_call(where, doc_starts, late_queries, latent_keys, latent_values, 1))
    lat = jnp.concatenate(lats, axis=1)
    near_vals.append(near(part(late_vals, 1)))
    far_keys, lat = lax.optimization_barrier((far_keys, lat))
    weighed = weigh(near_keys, far_keys, state)
    near_vals[1], weighed = lax.optimization_barrier((near_vals[1], weighed))
    acc, *near_weights, far_weights, sums = weighed
    sums = move(sums, [(s, s ^ 2) for s in range(4)])
    far_vals = [onward(near_vals[0])]
    mixed = [mix(0, acc, near_weights, near_vals[0], lat)]
    near_vals[1], mixed[0] = lax.optimization_barrier((near_vals[1], mixed[0]))
    far_vals.append(onward(near_vals[1]))
    parts = pl.pallas_call(
        part_kernel,
        grid=(heads // step,),
        in_specs=smem(2) + [spec(2 * PIECES, step * BLK), spec(rows, wide)],
        out_specs=spec(2 * PIECES, wide),
        out_shape=shape(2 * PIECES, columns),
        compiler_params=PARAMS,
        cost_estimate=pl.CostEstimate(flops=64 * rows * columns * 144, bytes_accessed=3 * rows * columns, transcendentals=0),
        name="part",
    )(where, doc_starts, sums, values)
    acc, parts = lax.optimization_barrier((acc, parts))
    mixed.append(mix(1, acc, near_weights, near_vals[1], lat))
    sent = pl.pallas_call(
        route_kernel,
        in_specs=smem(2) + vmem(3),
        out_specs=pl.BlockSpec(memory_space=pltpu.VMEM),
        out_shape=jax.ShapeDtypeStruct((4, 4, columns), BF16),
        compiler_params=PARAMS,
        name="route",
    )(where, doc_owner, parts, *[m[1] for m in mixed])
    mixed[0], parts = lax.optimization_barrier((mixed[0], parts))
    context = finish(0, mixed[0][0], far_weights, far_vals[0], None)
    sent, context = lax.optimization_barrier((sent, context))
    got = lax.all_to_all(sent, "seq", split_axis=0, concat_axis=0, tiled=True)
    context = finish(1, mixed[1][0], far_weights, far_vals[1], context)
    got, context = lax.optimization_barrier((got, context))
    pooled = pl.pallas_call(
        pool_kernel,
        in_specs=vmem(1),
        out_specs=pl.BlockSpec(memory_space=pltpu.VMEM),
        out_shape=jax.ShapeDtypeStruct((1, 4, 2, columns), BF16),
        compiler_params=PARAMS,
        name="pool",
    )(got)
    return context, pooled


def body(queries, keys, values, latent_keys, latent_values, pattern, doc_starts, doc_owner):
    rows, columns = queries.shape
    heads = columns // HD
    shards = lax.axis_size("seq")
    seq_index = lax.axis_index("seq")
    where = seq_index.astype(jnp.int32).reshape(1)
    levels = [j for j in range(LEVELS) if 2**j < shards]
    last = levels[-1]
    merged = 2 * 2**last >= shards
    rotate = shards <= 4

    def both_ways(value, distance):
        behind = lax.ppermute(value, "seq", [(s, s + distance) for s in range(shards - distance)])
        ahead = lax.ppermute(value, "seq", [(s, s - distance) for s in range(distance, shards)])
        return [behind, ahead]

    def far(value, near):
        if last != 1:
            return both_ways(value, 2**last)
        behind = lax.ppermute(near[0], "seq", [(s, s + 1) for s in range(1, shards - 1)])
        ahead = lax.ppermute(near[1], "seq", [(s, s - 1) for s in range(1, shards - 1)])
        return [behind, ahead]

    if shards == 4:
        return four_shards(queries, keys, values, latent_keys, latent_values, pattern, doc_starts, doc_owner)
    near_keys = both_ways(keys, 1)
    near_vals = both_ways(values, 1)
    state_shapes = (shape(rows, columns),) * 3
    lat = latent_call(where, doc_starts, queries, latent_keys, latent_values)
    state = own_call(queries, keys, values)
    near_keys, state = lax.optimization_barrier((near_keys, state))

    for level in levels[:-1]:
        if level == 0:
            got = near_keys + near_vals
        else:
            got = both_ways(keys, 2**level) + both_ways(values, 2**level)
        state = pl.pallas_call(
            functools.partial(near_kernel, shards, level),
            grid=(heads,),
            in_specs=smem(2) + [spec(rows)] * 8,
            out_specs=[spec(rows)] * 3,
            out_shape=state_shapes,
            input_output_aliases={7 + i: i for i in range(3)},
            compiler_params=PARAMS,
            cost_estimate=pl.CostEstimate(
                flops=8 * rows * columns * BLK, bytes_accessed=20 * rows * columns * 2, transcendentals=2 * heads * rows * BLK
            ),
            name="near",
        )(where, pattern, queries, *got, *state)

    far_keys = far(keys, near_keys)
    far_vals = far(values, near_vals)
    sources = 1 if merged else 2
    acc, *weights = pl.pallas_call(
        functools.partial(far_kernel, shards, last, merged),
        grid=(heads,),
        in_specs=smem(2) + [spec(rows)] * 6,
        out_specs=[spec(rows)] + [spec(rows, BLK)] * sources,
        out_shape=(shape(rows, columns),) + (shape(rows, heads * BLK, BF16),) * sources,
        input_output_aliases={5: 0},
        compiler_params=PARAMS,
        cost_estimate=pl.CostEstimate(
            flops=2 * sources * rows * columns * BLK,
            bytes_accessed=(10 + 3 * sources) * rows * columns * 2,
            transcendentals=sources * heads * rows * BLK,
        ),
        name="far",
    )(where, pattern, queries, *far_keys, *state)

    if rotate:
        sent = (shape(2, columns, BF16),) * shards
    else:
        sent = (jax.ShapeDtypeStruct((shards, 2, columns), BF16),)
    context, *means = pl.pallas_call(
        functools.partial(finish_kernel, shards, last, merged),
        in_specs=smem(3) + vmem(4 + sources),
        out_specs=vmem(1 + len(sent)),
        out_shape=(shape(rows, columns, BF16),) + sent,
        compiler_params=PARAMS,
        cost_estimate=pl.CostEstimate(
            flops=2 * sources * rows * columns * BLK, bytes_accessed=(3 + 3 * sources) * rows * columns * 2, transcendentals=0
        ),
        name="finish",
    )(where, doc_starts, doc_owner, acc, lat, *weights, *far_vals)

    if not rotate:
        return context, lax.all_to_all(means[0], "seq", split_axis=0, concat_axis=0, tiled=True)[None]
    got = [means[0]]
    for r in range(1, shards):
        got.append(lax.ppermute(means[r], "seq", [(s, (s + r) % shards) for s in range(shards)]))
    pooled = []
    for s in range(shards):
        back = lax.rem(seq_index - s + shards, shards)
        row = got[0]
        for r in range(1, shards):
            row = jnp.where(back == r, got[r], row)
        pooled.append(row)
    return context, jnp.stack(pooled)[None]


def solution(mesh):
    in_specs = (
        P(("groups", "seq"), ("head", "sub")),
        P(("groups", "seq"), ("head", "sub")),
        P(("groups", "seq"), ("head", "sub")),
        P("groups", ("head", "sub")),
        P("groups", ("head", "sub")),
        P(("groups", "seq"), None),
        P("groups"),
        P("groups"),
    )
    out_specs = (
        P(("groups", "seq"), ("head", "sub")),
        P(("groups", "seq"), None, None, ("head", "sub")),
    )
    return jax.shard_map(body, mesh=mesh, in_specs=in_specs, out_specs=out_specs, check_vma=False)
```

```python
import functools
import math

import jax
import jax.numpy as jnp
from jax import lax
from jax.experimental import pallas as pl
from jax.experimental.pallas import tpu as pltpu
from jax.sharding import PartitionSpec as P

HD = 128
LEVELS = 4
BLK = 256
PIECES = 4
SCALE = math.log2(math.e) / math.sqrt(HD)
PARAMS = pltpu.CompilerParams(vmem_limit_bytes=24 * 1024 * 1024)
F32 = jnp.float32
BF16 = jnp.bfloat16


def dot_t(a, b):
    return lax.dot_general(a, b, (((1,), (1,)), ((), ())), preferred_element_type=F32)


def dot(a, b):
    return jnp.dot(a, b, preferred_element_type=F32)


def doc_rows(rows, split):
    place = lax.broadcasted_iota(jnp.int32, rows.shape, 0)
    first = jnp.sum(jnp.where(place < split, rows, 0.0), axis=0, keepdims=True)
    second = jnp.sum(jnp.where(place < split, 0.0, rows), axis=0, keepdims=True)
    return jnp.concatenate((first, second), axis=0)


def own_kernel(q_ref, k_ref, v_ref, acc_ref, top_ref, sum_ref):
    for h in range(q_ref.shape[1] // HD):
        head = slice(h * HD, (h + 1) * HD)
        s = dot_t(q_ref[:, head], k_ref[:, head]) * SCALE
        top = jnp.max(s, axis=1, keepdims=True)
        e = jnp.exp2(s - top)
        acc = dot(e.astype(BF16), v_ref[:, head])
        acc_ref[:, head] = acc
        top_ref[:, head] = jnp.broadcast_to(top, acc.shape)
        sum_ref[:, head] = jnp.broadcast_to(jnp.sum(e, axis=1, keepdims=True), acc.shape)


def latent_kernel(where, starts, q_ref, lk_ref, lv_ref, lat_ref):
    for h in range(q_ref.shape[1] // HD):
        head = slice(h * HD, (h + 1) * HD)
        s = dot_t(q_ref[:, head], lk_ref[:, head]) * SCALE
        e = jnp.exp2(s - jnp.max(s, axis=1, keepdims=True))
        out = dot(e.astype(BF16), lv_ref[:, head]) / jnp.sum(e, axis=1, keepdims=True)
        piece = out.shape[0] // PIECES
        for p in range(PIECES):
            split = split_of(where, starts, p)
            lat_ref[2 * p : 2 * p + 2, head] = doc_rows(out[p * piece : (p + 1) * piece], split)


def split_of(where, starts, p, shard=None):
    first = 2 * (PIECES * (where[0] if shard is None else shard) + p)
    return starts[first + 1] - starts[first]


def slot_live(where, pattern, shards, level, side, block):
    partner = where[0] + (2 * side - 1) * 2**level
    return (pattern[block, 2 * level + side] == 1) & (partner >= 0) & (partner < shards)


def live_scores(live, q, k):
    return jnp.where(live, dot_t(q, k) * SCALE, -jnp.inf)


def near_kernel(shards, level, where, pattern, q_ref, kb_ref, ka_ref, vb_ref, va_ref, *refs):
    acc_in, top_in, sum_in, acc_ref, top_ref, sum_ref = refs
    for block in range(q_ref.shape[0] // BLK):
        rows = pl.ds(block * BLK, BLK)
        q = q_ref[rows, :]
        scores = [
            live_scores(slot_live(where, pattern, shards, level, side, block), q, k_ref[rows, :])
            for side, k_ref in enumerate((kb_ref, ka_ref))
        ]
        old = top_in[rows, :1]
        top = old
        for s in scores:
            top = jnp.maximum(top, jnp.max(s, axis=1, keepdims=True))
        shrink = jnp.exp2(old - top)
        total = sum_in[rows, :1] * shrink
        acc = acc_in[rows, :] * shrink
        for s, v_ref in zip(scores, (vb_ref, va_ref)):
            e = jnp.exp2(s - top)
            total = total + jnp.sum(e, axis=1, keepdims=True)
            acc = acc + dot(e.astype(BF16), v_ref[rows, :])
        acc_ref[rows, :] = acc
        top_ref[rows, :] = jnp.broadcast_to(top, acc.shape)
        sum_ref[rows, :] = jnp.broadcast_to(total, acc.shape)


def far_kernel(shards, level, merged, where, pattern, q_ref, kb_ref, ka_ref, acc_in, top_in, sum_in, acc_ref, *outs):
    behind = where[0] >= 2**level
    for block in range(q_ref.shape[0] // BLK):
        rows = pl.ds(block * BLK, BLK)
        q = q_ref[rows, :]
        live = [slot_live(where, pattern, shards, level, side, block) for side in range(2)]
        pair = [k_ref[rows, :] for k_ref in (kb_ref, ka_ref)]
        if merged:
            live = [(behind & live[0]) | (jnp.logical_not(behind) & live[1])]
            pair = [jnp.where(behind, pair[0], pair[1])]
        scores = [live_scores(on, q, k) for on, k in zip(live, pair)]
        old = top_in[rows, :1]
        top = old
        for s in scores:
            top = jnp.maximum(top, jnp.max(s, axis=1, keepdims=True))
        shrink = jnp.exp2(old - top)
        total = sum_in[rows, :1] * shrink
        exps = []
        for s in scores:
            e = jnp.exp2(s - top)
            total = total + jnp.sum(e, axis=1, keepdims=True)
            exps.append(e)
        inverse = 1.0 / total
        acc_ref[rows, :] = acc_in[rows, :] * (shrink * inverse)
        for e, out in zip(exps, outs):
            out[rows, :] = (e * inverse).astype(BF16)


def finish_kernel(shards, level, merged, where, starts, owners, acc_ref, lat_ref, *refs):
    sources = 1 if merged else 2
    weights, (vb_ref, va_ref) = refs[:sources], refs[sources : sources + 2]
    ctx_ref, outs = refs[sources + 2], refs[sources + 3 :]
    rows_here, columns = acc_ref.shape
    piece = rows_here // PIECES
    splits = [split_of(where, starts, p) for p in range(PIECES)]
    behind = where[0] >= 2**level
    sums = []
    for h in range(columns // HD):
        head = pl.ds(h * HD, HD)
        slots = pl.ds(h * BLK, BLK)
        found = []
        for block in range(rows_here // BLK):
            rows = pl.ds(block * BLK, BLK)
            pair = [v_ref[rows, head] for v_ref in (vb_ref, va_ref)]
            if merged:
                pair = [jnp.where(behind, pair[0], pair[1])]
            acc = acc_ref[rows, head]
            for w_ref, v in zip(weights, pair):
                acc = acc + dot(w_ref[rows, slots], v)
            ctx = acc.astype(BF16)
            ctx_ref[rows, head] = ctx
            ctx = ctx.astype(F32)
            for start in range(0, BLK, piece):
                found.append(doc_rows(ctx[start : start + piece], splits[len(found)]))
        sums.append(found)
    side = lax.broadcasted_iota(jnp.int32, (2, columns), 0)
    means = []
    for p in range(PIECES):
        count = jnp.where(side == 0, splits[p], piece - splits[p]).astype(F32)
        total = jnp.concatenate([found[p] for found in sums], axis=1) + lat_ref[2 * p : 2 * p + 2, :]
        means.append(total / count)
    for r in range(shards):
        if len(outs) == 1:
            target = r
        else:
            target = lax.rem(where[0] + r, shards)
        chosen = jnp.zeros((2, columns), F32)
        for p in range(PIECES):
            chosen = jnp.where(owners[2 * (PIECES * where[0] + p)] == target, means[p], chosen)
        if len(outs) == 1:
            outs[0][r] = chosen.astype(BF16)
        else:
            outs[r][...] = chosen.astype(BF16)


def live_bias(where, pattern, shards, level, side, block):
    return jnp.where(slot_live(where, pattern, shards, level, side, block), 0.0, -jnp.inf)


def halves(s, bias):
    return [s[:, i : i + HD] * SCALE + bias for i in range(0, BLK, HD)]


def near_weigh_kernel(shards, where, pattern, q_ref, nb_ref, na_ref, acc_in, top_in, sum_in, *refs):
    acc_ref, top_ref, sum_ref, wb_ref, wa_ref = refs
    biases = [[live_bias(where, pattern, shards, 0, side, block) for side in range(2)] for block in range(q_ref.shape[0] // BLK)]
    piece = q_ref.shape[0] // PIECES
    for h in range(q_ref.shape[1] // HD):
        head = slice(h * HD, (h + 1) * HD)
        for p in range(PIECES):
            rows = slice(p * piece, (p + 1) * piece)
            block = p * piece // BLK
            held = slice(block * BLK, (block + 1) * BLK)
            q = q_ref[rows, head]
            scores = [halves(dot_t(q, k_ref[held, head]), bias) for k_ref, bias in zip((nb_ref, na_ref), biases[block])]
            old = top_in[rows, head]
            top = jnp.max(functools.reduce(jnp.maximum, scores[0] + scores[1]), axis=1, keepdims=True)
            top = jnp.maximum(top, old)
            shrink = jnp.exp2(old - top)
            exps = [[jnp.exp2(x - top) for x in pair] for pair in scores]
            added = jnp.sum(functools.reduce(jnp.add, exps[0] + exps[1]), axis=1, keepdims=True)
            top_ref[rows, head] = top
            sum_ref[rows, head] = sum_in[rows, head] * shrink + added
            acc_ref[rows, head] = acc_in[rows, head] * shrink
            for pair, out in zip(exps, (wb_ref, wa_ref)):
                for i, e in enumerate(pair):
                    first = h * BLK + i * HD
                    out[rows, first : first + HD] = e.astype(BF16)


def far_weigh_kernel(shards, where, pattern, starts, q_ref, fb_ref, fa_ref, top_in, sum_in, scale_ref, wf_ref, sums_ref):
    behind = where[0] >= 2
    biases = []
    for block in range(q_ref.shape[0] // BLK):
        pair = [live_bias(where, pattern, shards, 1, side, block) for side in range(2)]
        biases.append(jnp.where(behind, pair[0], pair[1]))
    piece = q_ref.shape[0] // PIECES
    place = lax.broadcasted_iota(jnp.int32, (piece, HD), 0)
    firsts = [place < split_of(where, starts, p) for p in range(PIECES)]
    for h in range(q_ref.shape[1] // HD):
        head = slice(h * HD, (h + 1) * HD)
        sums = [[] for _ in range(BLK // HD)]
        for p in range(PIECES):
            rows = slice(p * piece, (p + 1) * piece)
            block = p * piece // BLK
            held = slice(block * BLK, (block + 1) * BLK)
            keys = jnp.where(behind, fb_ref[held, head], fa_ref[held, head])
            scores = halves(dot_t(q_ref[rows, head], keys), biases[block])
            old = top_in[rows, head]
            top = jnp.maximum(jnp.max(functools.reduce(jnp.maximum, scores), axis=1, keepdims=True), old)
            shrink = jnp.exp2(old - top)
            exps = [jnp.exp2(x - top) for x in scores]
            added = jnp.sum(functools.reduce(jnp.add, exps), axis=1, keepdims=True)
            inverse = 1.0 / (sum_in[rows, head] * shrink + added)
            scale_ref[rows, head] = shrink * inverse
            for i, e in enumerate(exps):
                first = h * BLK + i * HD
                w = e * inverse
                wf_ref[rows, first : first + HD] = w.astype(BF16)
                sums[i] += [
                    jnp.sum(jnp.where(firsts[p], w, 0.0), axis=0, keepdims=True),
                    jnp.sum(jnp.where(firsts[p], 0.0, w), axis=0, keepdims=True),
                ]
        for i, found in enumerate(sums):
            first = h * BLK + i * HD
            sums_ref[:, first : first + HD] = jnp.concatenate(found, axis=0).astype(sums_ref.dtype)


def doc_counts(split, piece, columns):
    side = lax.broadcasted_iota(jnp.int32, (2, columns), 0)
    return jnp.where(side == 0, split, piece - split).astype(F32)


def mix_kernel(block, where, starts, acc_in, scale_in, wb_ref, wa_ref, vb_ref, va_ref, lat_ref, acc_ref, mean_ref):
    pieces = mean_ref.shape[0] // 2
    piece = BLK // pieces
    for h in range(acc_in.shape[1] // HD):
        head = slice(h * HD, (h + 1) * HD)
        slots = slice(h * BLK, (h + 1) * BLK)
        acc = acc_in[:, head] + dot(wb_ref[:, slots], vb_ref[:, head]) + dot(wa_ref[:, slots], va_ref[:, head])
        acc = acc * scale_in[:, head]
        acc_ref[:, head] = acc
        for p in range(pieces):
            index = block * pieces + p
            split = split_of(where, starts, index)
            found = doc_rows(acc[p * piece : (p + 1) * piece], split) + lat_ref[2 * index : 2 * index + 2, head]
            mean_ref[2 * p : 2 * p + 2, head] = found / doc_counts(split, piece, HD)


def part_kernel(where, starts, sums_ref, v_ref, part_ref):
    piece = v_ref.shape[0] // PIECES
    per_block = BLK // piece
    partner = lax.rem(where[0] + 2, 4)
    counts = [doc_counts(split_of(where, starts, p, partner), piece, HD) for p in range(PIECES)]
    for h in range(v_ref.shape[1] // HD):
        head = slice(h * HD, (h + 1) * HD)
        sums = sums_ref[:, h * BLK : (h + 1) * BLK]
        found = [dot(sums.astype(BF16), v_ref[block * BLK : (block + 1) * BLK, head]) for block in range(v_ref.shape[0] // BLK)]
        for p in range(PIECES):
            rows = slice(2 * p, 2 * p + 2)
            part_ref[rows, head] = found[p // per_block][rows] / counts[p]


def route_kernel(where, owners, part_ref, *refs):
    mean_refs, out_ref = refs[:-1], refs[-1]
    here, partner = where[0], lax.rem(where[0] + 2, 4)
    means = jnp.concatenate([mean_ref[...] for mean_ref in mean_refs], axis=0)
    parts = part_ref[...]
    for target in range(out_ref.shape[0]):
        rows = []
        for group, shard in ((means, here), (parts, partner)):
            chosen = jnp.zeros((2, out_ref.shape[2]), F32)
            for p in range(PIECES):
                chosen = jnp.where(owners[2 * (PIECES * shard + p)] == target, group[2 * p : 2 * p + 2], chosen)
            rows.append(chosen)
        out_ref[target] = jnp.concatenate(rows, axis=0).astype(BF16)


def context_kernel(block, where, acc_ref, w_ref, vb_ref, va_ref, *refs):
    stage, sem = refs[-2:]
    if len(refs) == 3:
        out_ref = refs[0]
    else:
        got_ref, _, out_ref, pooled_ref = refs[:4]
    behind = where[0] >= 2
    copies = []
    for h in range(acc_ref.shape[1] // HD):
        head = pl.ds(h * HD, HD)
        v = jnp.where(behind, vb_ref[:, head], va_ref[:, head])
        stage[:, head] = (acc_ref[:, head] + dot(w_ref[pl.ds(block * BLK, BLK), pl.ds(h * BLK, BLK)], v)).astype(BF16)
        if h % 2:
            pair = pl.ds((h - 1) * HD, 2 * HD)
            copy = pltpu.make_async_copy(stage.at[:, pair], out_ref.at[pl.ds(block * BLK, BLK), pair], sem.at[h // 2])
            copy.start()
            copies.append(copy)
    if len(refs) > 3:
        got = [got_ref[s].astype(F32) for s in range(4)]
        for s in range(4):
            pooled_ref[0, s] = (got[s][:2] + got[s ^ 2][2:]).astype(BF16)
    for copy in copies:
        copy.wait()


def spec(rows, columns=HD):
    return pl.BlockSpec((rows, columns), lambda h: (0, h))


def smem(count):
    return [pl.BlockSpec(memory_space=pltpu.SMEM)] * count


def vmem(count):
    return [pl.BlockSpec(memory_space=pltpu.VMEM)] * count


def shape(rows, columns, kind=F32):
    return jax.ShapeDtypeStruct((rows, columns), kind)


def step_of(heads):
    return 2 if heads % 2 == 0 else 1


def own_call(queries, keys, values):
    rows, columns = queries.shape
    heads = columns // HD
    wide = step_of(heads) * HD
    return pl.pallas_call(
        own_kernel,
        grid=(columns // wide,),
        in_specs=[spec(rows, wide)] * 3,
        out_specs=[spec(rows, wide)] * 3,
        out_shape=(shape(rows, columns),) * 3,
        compiler_params=PARAMS,
        cost_estimate=pl.CostEstimate(
            flops=4 * rows * columns * rows, bytes_accessed=18 * rows * columns, transcendentals=heads * rows * rows
        ),
        name="own",
    )(queries, keys, values)


def latent_call(where, doc_starts, queries, latent_keys, latent_values, first=0, last=None):
    rows, columns = queries.shape
    latents = latent_keys.shape[0]
    wide = step_of(columns // HD) * HD
    steps = (last or columns // wide) - first
    return pl.pallas_call(
        latent_kernel,
        grid=(steps,),
        in_specs=smem(2) + [pl.BlockSpec((size, wide), lambda h: (0, h + first)) for size in (rows, latents, latents)],
        out_specs=spec(2 * PIECES, wide),
        out_shape=shape(2 * PIECES, steps * wide),
        compiler_params=PARAMS,
        cost_estimate=pl.CostEstimate(
            flops=4 * rows * steps * wide * latents * (1 if first == 0 else 10),
            bytes_accessed=6 * rows * steps * wide,
            transcendentals=steps * wide // HD * rows * latents,
        ),
        name="latent",
    )(where, doc_starts, queries, latent_keys, latent_values)


def four_shards(queries, keys, values, latent_keys, latent_values, pattern, doc_starts, doc_owner):
    rows, columns = queries.shape
    heads = columns // HD
    step = step_of(heads)
    wide = step * HD
    slots = heads * BLK
    blocks = rows // BLK
    docs = 2 * PIECES // blocks
    where = lax.axis_index("seq").astype(jnp.int32).reshape(1)
    right, left = [(0, 1), (1, 2), (2, 3)], [(1, 0), (2, 1), (3, 2)]

    def move(value, pairs):
        return lax.ppermute(value, "seq", pairs)

    def near(value):
        return [move(value, right), move(value, left)]

    def onward(pair):
        return [move(pair[0], right[1:]), move(pair[1], left[:-1])]

    def part(array, block):
        return array[block * BLK : (block + 1) * BLK]

    def row_spec(block, width=wide):
        return pl.BlockSpec((BLK, width), lambda h: (block, h))

    def weigh_near(near_keys, state):
        return pl.pallas_call(
            functools.partial(near_weigh_kernel, 4),
            grid=(heads // step,),
            in_specs=smem(2) + [spec(rows, wide)] * 6,
            out_specs=[spec(rows, wide)] * 3 + [spec(rows, step * BLK)] * 2,
            out_shape=(shape(rows, columns),) * 3 + (shape(rows, slots, BF16),) * 2,
            input_output_aliases={5: 0, 6: 1, 7: 2},
            compiler_params=PARAMS,
            cost_estimate=pl.CostEstimate(
                flops=4 * rows * columns * BLK, bytes_accessed=20 * rows * columns, transcendentals=2 * heads * rows * BLK
            ),
            name="weigh_near",
        )(where, pattern, queries, *near_keys, *state)

    def weigh_far(far_keys, top, total):
        return pl.pallas_call(
            functools.partial(far_weigh_kernel, 4),
            grid=(heads // step,),
            in_specs=smem(3) + [spec(rows, wide)] * 5,
            out_specs=[spec(rows, wide), spec(rows, step * BLK), spec(2 * PIECES, step * BLK)],
            out_shape=(shape(rows, columns), shape(rows, slots, BF16), shape(2 * PIECES, slots, BF16)),
            compiler_params=PARAMS,
            cost_estimate=pl.CostEstimate(
                flops=2 * rows * columns * BLK, bytes_accessed=22 * rows * columns, transcendentals=heads * rows * BLK
            ),
            name="weigh_far",
        )(where, pattern, doc_starts, queries, *far_keys, top, total)

    def mix(block, acc, scale, weights, near_vals, lat):
        return pl.pallas_call(
            functools.partial(mix_kernel, block),
            grid=(heads // step,),
            in_specs=smem(2)
            + [row_spec(block)] * 2
            + [row_spec(block, step * BLK)] * 2
            + [row_spec(0)] * 2
            + [spec(2 * PIECES, wide)],
            out_specs=[row_spec(0), spec(docs, wide)],
            out_shape=(shape(BLK, columns), shape(docs, columns)),
            compiler_params=PARAMS,
            cost_estimate=pl.CostEstimate(flops=4 * BLK * columns * BLK, bytes_accessed=20 * BLK * columns, transcendentals=0),
            name="mix",
        )(where, doc_starts, acc, scale, *weights, *near_vals, lat)

    def finish(block, acc, weights, far_vals, held):
        context = shape(rows, columns, BF16)
        pooled = jax.ShapeDtypeStruct((1, 4, 2, columns), BF16)
        anywhere = pl.BlockSpec(memory_space=pl.ANY)
        whole = pl.BlockSpec(memory_space=pltpu.VMEM)
        return pl.pallas_call(
            functools.partial(context_kernel, block),
            in_specs=smem(1) + vmem(4) + ([whole, anywhere] if held else []),
            out_specs=[anywhere, whole] if held else anywhere,
            out_shape=(context, pooled) if held else context,
            scratch_shapes=[pltpu.VMEM((BLK, columns), BF16), pltpu.SemaphoreType.DMA((heads // 2,))],
            input_output_aliases={6: 0} if held else {},
            compiler_params=PARAMS,
            cost_estimate=pl.CostEstimate(flops=2 * BLK * columns * BLK, bytes_accessed=14 * BLK * columns, transcendentals=0),
            name="finish",
        )(where, acc, weights, *far_vals, *held)

    near_keys = near(keys)
    lats = [latent_call(where, doc_starts, queries, latent_keys, latent_values, 0, 1)]
    lats, late_vals, late_queries = lax.optimization_barrier((lats, values, queries))
    near_vals = [near(part(late_vals, 0))]
    state = own_call(late_queries, keys, values)
    near_keys, state = lax.optimization_barrier((near_keys, state))
    far_keys = onward(near_keys)
    near_vals[0], late_vals, late_queries = lax.optimization_barrier((near_vals[0], late_vals, late_queries))
    lats.append(latent_call(where, doc_starts, late_queries, latent_keys, latent_values, 1))
    lat = jnp.concatenate(lats, axis=1)
    near_vals.append(near(part(late_vals, 1)))
    acc, top, total, *near_weights = weigh_near(near_keys, state)
    far_keys, lat, top = lax.optimization_barrier((far_keys, lat, top))
    weighed = weigh_far(far_keys, top, total)
    near_vals[0], weighed = lax.optimization_barrier((near_vals[0], weighed))
    scale, far_weights, sums = weighed
    sums = move(sums, [(s, s ^ 2) for s in range(4)])
    far_vals = [onward(near_vals[0])]
    parts = pl.pallas_call(
        part_kernel,
        grid=(heads // step,),
        in_specs=smem(2) + [spec(2 * PIECES, step * BLK), spec(rows, wide)],
        out_specs=spec(2 * PIECES, wide),
        out_shape=shape(2 * PIECES, columns),
        compiler_params=PARAMS,
        cost_estimate=pl.CostEstimate(flops=64 * rows * columns * 32, bytes_accessed=3 * rows * columns, transcendentals=0),
        name="part",
    )(where, doc_starts, sums, values)
    mixed = [mix(0, acc, scale, near_weights, near_vals[0], lat)]
    near_vals[1], parts, mixed[0] = lax.optimization_barrier((near_vals[1], parts, mixed[0]))
    far_vals.append(onward(near_vals[1]))
    mixed.append(mix(1, acc, scale, near_weights, near_vals[1], lat))
    context = finish(0, mixed[0][0], far_weights, far_vals[0], [])
    sent = pl.pallas_call(
        route_kernel,
        in_specs=smem(2) + vmem(3),
        out_specs=pl.BlockSpec(memory_space=pltpu.VMEM),
        out_shape=jax.ShapeDtypeStruct((4, 4, columns), BF16),
        compiler_params=PARAMS,
        name="route",
    )(where, doc_owner, parts, *[m[1] for m in mixed])
    sent, context = lax.optimization_barrier((sent, context))
    got = lax.all_to_all(sent, "seq", split_axis=0, concat_axis=0, tiled=True)
    return finish(1, mixed[1][0], far_weights, far_vals[1], [got, context])


def body(queries, keys, values, latent_keys, latent_values, pattern, doc_starts, doc_owner):
    rows, columns = queries.shape
    heads = columns // HD
    shards = lax.axis_size("seq")
    seq_index = lax.axis_index("seq")
    where = seq_index.astype(jnp.int32).reshape(1)
    levels = [j for j in range(LEVELS) if 2**j < shards]
    last = levels[-1]
    merged = 2 * 2**last >= shards
    rotate = shards <= 4

    def both_ways(value, distance):
        behind = lax.ppermute(value, "seq", [(s, s + distance) for s in range(shards - distance)])
        ahead = lax.ppermute(value, "seq", [(s, s - distance) for s in range(distance, shards)])
        return [behind, ahead]

    def far(value, near):
        if last != 1:
            return both_ways(value, 2**last)
        behind = lax.ppermute(near[0], "seq", [(s, s + 1) for s in range(1, shards - 1)])
        ahead = lax.ppermute(near[1], "seq", [(s, s - 1) for s in range(1, shards - 1)])
        return [behind, ahead]

    if shards == 4:
        return four_shards(queries, keys, values, latent_keys, latent_values, pattern, doc_starts, doc_owner)
    near_keys = both_ways(keys, 1)
    near_vals = both_ways(values, 1)
    state_shapes = (shape(rows, columns),) * 3
    lat = latent_call(where, doc_starts, queries, latent_keys, latent_values)
    state = own_call(queries, keys, values)
    near_keys, state = lax.optimization_barrier((near_keys, state))

    for level in levels[:-1]:
        if level == 0:
            got = near_keys + near_vals
        else:
            got = both_ways(keys, 2**level) + both_ways(values, 2**level)
        state = pl.pallas_call(
            functools.partial(near_kernel, shards, level),
            grid=(heads,),
            in_specs=smem(2) + [spec(rows)] * 8,
            out_specs=[spec(rows)] * 3,
            out_shape=state_shapes,
            input_output_aliases={7 + i: i for i in range(3)},
            compiler_params=PARAMS,
            cost_estimate=pl.CostEstimate(
                flops=8 * rows * columns * BLK, bytes_accessed=20 * rows * columns * 2, transcendentals=2 * heads * rows * BLK
            ),
            name="near",
        )(where, pattern, queries, *got, *state)

    far_keys = far(keys, near_keys)
    far_vals = far(values, near_vals)
    sources = 1 if merged else 2
    acc, *weights = pl.pallas_call(
        functools.partial(far_kernel, shards, last, merged),
        grid=(heads,),
        in_specs=smem(2) + [spec(rows)] * 6,
        out_specs=[spec(rows)] + [spec(rows, BLK)] * sources,
        out_shape=(shape(rows, columns),) + (shape(rows, heads * BLK, BF16),) * sources,
        input_output_aliases={5: 0},
        compiler_params=PARAMS,
        cost_estimate=pl.CostEstimate(
            flops=2 * sources * rows * columns * BLK,
            bytes_accessed=(10 + 3 * sources) * rows * columns * 2,
            transcendentals=sources * heads * rows * BLK,
        ),
        name="far",
    )(where, pattern, queries, *far_keys, *state)

    if rotate:
        sent = (shape(2, columns, BF16),) * shards
    else:
        sent = (jax.ShapeDtypeStruct((shards, 2, columns), BF16),)
    context, *means = pl.pallas_call(
        functools.partial(finish_kernel, shards, last, merged),
        in_specs=smem(3) + vmem(4 + sources),
        out_specs=vmem(1 + len(sent)),
        out_shape=(shape(rows, columns, BF16),) + sent,
        compiler_params=PARAMS,
        cost_estimate=pl.CostEstimate(
            flops=2 * sources * rows * columns * BLK, bytes_accessed=(3 + 3 * sources) * rows * columns * 2, transcendentals=0
        ),
        name="finish",
    )(where, doc_starts, doc_owner, acc, lat, *weights, *far_vals)

    if not rotate:
        return context, lax.all_to_all(means[0], "seq", split_axis=0, concat_axis=0, tiled=True)[None]
    got = [means[0]]
    for r in range(1, shards):
        got.append(lax.ppermute(means[r], "seq", [(s, (s + r) % shards) for s in range(shards)]))
    pooled = []
    for s in range(shards):
        back = lax.rem(seq_index - s + shards, shards)
        row = got[0]
        for r in range(1, shards):
            row = jnp.where(back == r, got[r], row)
        pooled.append(row)
    return context, jnp.stack(pooled)[None]


def solution(mesh):
    in_specs = (
        P(("groups", "seq"), ("head", "sub")),
        P(("groups", "seq"), ("head", "sub")),
        P(("groups", "seq"), ("head", "sub")),
        P("groups", ("head", "sub")),
        P("groups", ("head", "sub")),
        P(("groups", "seq"), None),
        P("groups"),
        P("groups"),
    )
    out_specs = (
        P(("groups", "seq"), ("head", "sub")),
        P(("groups", "seq"), None, None, ("head", "sub")),
    )
    return jax.shard_map(body, mesh=mesh, in_specs=in_specs, out_specs=out_specs, check_vma=False)
```

```python
import functools
import math

import jax
import jax.numpy as jnp
from jax import lax
from jax.experimental import pallas as pl
from jax.experimental.pallas import tpu as pltpu
from jax.sharding import PartitionSpec as P

HD = 128
LEVELS = 4
BLK = 256
PIECES = 4
SCALE = math.log2(math.e) / math.sqrt(HD)
PARAMS = pltpu.CompilerParams(vmem_limit_bytes=24 * 1024 * 1024)
F32 = jnp.float32
BF16 = jnp.bfloat16


def dot_t(a, b):
    return lax.dot_general(a, b, (((1,), (1,)), ((), ())), preferred_element_type=F32)


def dot(a, b):
    return jnp.dot(a, b, preferred_element_type=F32)


def doc_rows(rows, split):
    place = lax.broadcasted_iota(jnp.int32, rows.shape, 0)
    first = jnp.sum(jnp.where(place < split, rows, 0.0), axis=0, keepdims=True)
    second = jnp.sum(jnp.where(place < split, 0.0, rows), axis=0, keepdims=True)
    return jnp.concatenate((first, second), axis=0)


def own_kernel(q_ref, k_ref, v_ref, acc_ref, top_ref, sum_ref):
    for h in range(q_ref.shape[1] // HD):
        head = slice(h * HD, (h + 1) * HD)
        s = dot_t(q_ref[:, head], k_ref[:, head]) * SCALE
        top = jnp.max(s, axis=1, keepdims=True)
        e = jnp.exp2(s - top)
        acc = dot(e.astype(BF16), v_ref[:, head])
        acc_ref[:, head] = acc
        top_ref[:, head] = jnp.broadcast_to(top, acc.shape)
        sum_ref[:, head] = jnp.broadcast_to(jnp.sum(e, axis=1, keepdims=True), acc.shape)


def latent_kernel(where, starts, q_ref, lk_ref, lv_ref, lat_ref):
    for h in range(q_ref.shape[1] // HD):
        head = slice(h * HD, (h + 1) * HD)
        s = dot_t(q_ref[:, head], lk_ref[:, head]) * SCALE
        e = jnp.exp2(s - jnp.max(s, axis=1, keepdims=True))
        out = dot(e.astype(BF16), lv_ref[:, head]) / jnp.sum(e, axis=1, keepdims=True)
        piece = out.shape[0] // PIECES
        for p in range(PIECES):
            split = split_of(where, starts, p)
            lat_ref[2 * p : 2 * p + 2, head] = doc_rows(out[p * piece : (p + 1) * piece], split)


def split_of(where, starts, p, shard=None):
    first = 2 * (PIECES * (where[0] if shard is None else shard) + p)
    return starts[first + 1] - starts[first]


def slot_live(where, pattern, shards, level, side, block):
    partner = where[0] + (2 * side - 1) * 2**level
    return (pattern[block, 2 * level + side] == 1) & (partner >= 0) & (partner < shards)


def live_scores(live, q, k):
    return jnp.where(live, dot_t(q, k) * SCALE, -jnp.inf)


def near_kernel(shards, level, where, pattern, q_ref, kb_ref, ka_ref, vb_ref, va_ref, *refs):
    acc_in, top_in, sum_in, acc_ref, top_ref, sum_ref = refs
    for block in range(q_ref.shape[0] // BLK):
        rows = pl.ds(block * BLK, BLK)
        q = q_ref[rows, :]
        scores = [
            live_scores(slot_live(where, pattern, shards, level, side, block), q, k_ref[rows, :])
            for side, k_ref in enumerate((kb_ref, ka_ref))
        ]
        old = top_in[rows, :1]
        top = old
        for s in scores:
            top = jnp.maximum(top, jnp.max(s, axis=1, keepdims=True))
        shrink = jnp.exp2(old - top)
        total = sum_in[rows, :1] * shrink
        acc = acc_in[rows, :] * shrink
        for s, v_ref in zip(scores, (vb_ref, va_ref)):
            e = jnp.exp2(s - top)
            total = total + jnp.sum(e, axis=1, keepdims=True)
            acc = acc + dot(e.astype(BF16), v_ref[rows, :])
        acc_ref[rows, :] = acc
        top_ref[rows, :] = jnp.broadcast_to(top, acc.shape)
        sum_ref[rows, :] = jnp.broadcast_to(total, acc.shape)


def far_kernel(shards, level, merged, where, pattern, q_ref, kb_ref, ka_ref, acc_in, top_in, sum_in, acc_ref, *outs):
    behind = where[0] >= 2**level
    for block in range(q_ref.shape[0] // BLK):
        rows = pl.ds(block * BLK, BLK)
        q = q_ref[rows, :]
        live = [slot_live(where, pattern, shards, level, side, block) for side in range(2)]
        pair = [k_ref[rows, :] for k_ref in (kb_ref, ka_ref)]
        if merged:
            live = [(behind & live[0]) | (jnp.logical_not(behind) & live[1])]
            pair = [jnp.where(behind, pair[0], pair[1])]
        scores = [live_scores(on, q, k) for on, k in zip(live, pair)]
        old = top_in[rows, :1]
        top = old
        for s in scores:
            top = jnp.maximum(top, jnp.max(s, axis=1, keepdims=True))
        shrink = jnp.exp2(old - top)
        total = sum_in[rows, :1] * shrink
        exps = []
        for s in scores:
            e = jnp.exp2(s - top)
            total = total + jnp.sum(e, axis=1, keepdims=True)
            exps.append(e)
        inverse = 1.0 / total
        acc_ref[rows, :] = acc_in[rows, :] * (shrink * inverse)
        for e, out in zip(exps, outs):
            out[rows, :] = (e * inverse).astype(BF16)


def finish_kernel(shards, level, merged, where, starts, owners, acc_ref, lat_ref, *refs):
    sources = 1 if merged else 2
    weights, (vb_ref, va_ref) = refs[:sources], refs[sources : sources + 2]
    ctx_ref, outs = refs[sources + 2], refs[sources + 3 :]
    rows_here, columns = acc_ref.shape
    piece = rows_here // PIECES
    splits = [split_of(where, starts, p) for p in range(PIECES)]
    behind = where[0] >= 2**level
    sums = []
    for h in range(columns // HD):
        head = pl.ds(h * HD, HD)
        slots = pl.ds(h * BLK, BLK)
        found = []
        for block in range(rows_here // BLK):
            rows = pl.ds(block * BLK, BLK)
            pair = [v_ref[rows, head] for v_ref in (vb_ref, va_ref)]
            if merged:
                pair = [jnp.where(behind, pair[0], pair[1])]
            acc = acc_ref[rows, head]
            for w_ref, v in zip(weights, pair):
                acc = acc + dot(w_ref[rows, slots], v)
            ctx = acc.astype(BF16)
            ctx_ref[rows, head] = ctx
            ctx = ctx.astype(F32)
            for start in range(0, BLK, piece):
                found.append(doc_rows(ctx[start : start + piece], splits[len(found)]))
        sums.append(found)
    side = lax.broadcasted_iota(jnp.int32, (2, columns), 0)
    means = []
    for p in range(PIECES):
        count = jnp.where(side == 0, splits[p], piece - splits[p]).astype(F32)
        total = jnp.concatenate([found[p] for found in sums], axis=1) + lat_ref[2 * p : 2 * p + 2, :]
        means.append(total / count)
    for r in range(shards):
        if len(outs) == 1:
            target = r
        else:
            target = lax.rem(where[0] + r, shards)
        chosen = jnp.zeros((2, columns), F32)
        for p in range(PIECES):
            chosen = jnp.where(owners[2 * (PIECES * where[0] + p)] == target, means[p], chosen)
        if len(outs) == 1:
            outs[0][r] = chosen.astype(BF16)
        else:
            outs[r][...] = chosen.astype(BF16)


def live_bias(where, pattern, shards, level, side, block):
    return jnp.where(slot_live(where, pattern, shards, level, side, block), 0.0, -jnp.inf)


def halves(s, bias):
    return [s[:, i : i + HD] * SCALE + bias for i in range(0, BLK, HD)]


def near_weigh_kernel(shards, where, pattern, q_ref, nb_ref, na_ref, acc_in, top_in, sum_in, *refs):
    acc_ref, top_ref, sum_ref, wb_ref, wa_ref = refs
    biases = [[live_bias(where, pattern, shards, 0, side, block) for side in range(2)] for block in range(q_ref.shape[0] // BLK)]
    piece = q_ref.shape[0] // PIECES
    for h in range(q_ref.shape[1] // HD):
        head = slice(h * HD, (h + 1) * HD)
        for p in range(PIECES):
            rows = slice(p * piece, (p + 1) * piece)
            block = p * piece // BLK
            held = slice(block * BLK, (block + 1) * BLK)
            q = q_ref[rows, head]
            scores = [halves(dot_t(q, k_ref[held, head]), bias) for k_ref, bias in zip((nb_ref, na_ref), biases[block])]
            old = top_in[rows, head]
            top = jnp.max(functools.reduce(jnp.maximum, scores[0] + scores[1]), axis=1, keepdims=True)
            top = jnp.maximum(top, old)
            shrink = jnp.exp2(old - top)
            exps = [[jnp.exp2(x - top) for x in pair] for pair in scores]
            added = jnp.sum(functools.reduce(jnp.add, exps[0] + exps[1]), axis=1, keepdims=True)
            top_ref[rows, head] = top
            sum_ref[rows, head] = sum_in[rows, head] * shrink + added
            acc_ref[rows, head] = acc_in[rows, head] * shrink
            for pair, out in zip(exps, (wb_ref, wa_ref)):
                for i, e in enumerate(pair):
                    first = h * BLK + i * HD
                    out[rows, first : first + HD] = e.astype(BF16)


def far_weigh_kernel(shards, where, pattern, starts, q_ref, fb_ref, fa_ref, top_in, sum_in, scale_ref, wf_ref, sums_ref):
    behind = where[0] >= 2
    biases = []
    for block in range(q_ref.shape[0] // BLK):
        pair = [live_bias(where, pattern, shards, 1, side, block) for side in range(2)]
        biases.append(jnp.where(behind, pair[0], pair[1]))
    piece = q_ref.shape[0] // PIECES
    place = lax.broadcasted_iota(jnp.int32, (piece, HD), 0)
    firsts = [place < split_of(where, starts, p) for p in range(PIECES)]
    for h in range(q_ref.shape[1] // HD):
        head = slice(h * HD, (h + 1) * HD)
        sums = [[] for _ in range(BLK // HD)]
        for p in range(PIECES):
            rows = slice(p * piece, (p + 1) * piece)
            block = p * piece // BLK
            held = slice(block * BLK, (block + 1) * BLK)
            keys = jnp.where(behind, fb_ref[held, head], fa_ref[held, head])
            scores = halves(dot_t(q_ref[rows, head], keys), biases[block])
            old = top_in[rows, head]
            top = jnp.maximum(jnp.max(functools.reduce(jnp.maximum, scores), axis=1, keepdims=True), old)
            shrink = jnp.exp2(old - top)
            exps = [jnp.exp2(x - top) for x in scores]
            added = jnp.sum(functools.reduce(jnp.add, exps), axis=1, keepdims=True)
            inverse = 1.0 / (sum_in[rows, head] * shrink + added)
            scale_ref[rows, head] = shrink * inverse
            for i, e in enumerate(exps):
                first = h * BLK + i * HD
                w = e * inverse
                wf_ref[rows, first : first + HD] = w.astype(BF16)
                sums[i] += [
                    jnp.sum(jnp.where(firsts[p], w, 0.0), axis=0, keepdims=True),
                    jnp.sum(jnp.where(firsts[p], 0.0, w), axis=0, keepdims=True),
                ]
        for i, found in enumerate(sums):
            first = h * BLK + i * HD
            sums_ref[:, first : first + HD] = jnp.concatenate(found, axis=0).astype(sums_ref.dtype)


def doc_counts(split, piece, columns):
    side = lax.broadcasted_iota(jnp.int32, (2, columns), 0)
    return jnp.where(side == 0, split, piece - split).astype(F32)


def mix_kernel(block, where, starts, acc_in, scale_in, wb_ref, wa_ref, vb_ref, va_ref, lat_ref, acc_ref, mean_ref):
    pieces = mean_ref.shape[0] // 2
    piece = BLK // pieces
    for h in range(acc_in.shape[1] // HD):
        head = slice(h * HD, (h + 1) * HD)
        slots = slice(h * BLK, (h + 1) * BLK)
        acc = acc_in[:, head] + dot(wb_ref[:, slots], vb_ref[:, head]) + dot(wa_ref[:, slots], va_ref[:, head])
        acc = acc * scale_in[:, head]
        acc_ref[:, head] = acc
        for p in range(pieces):
            index = block * pieces + p
            split = split_of(where, starts, index)
            found = doc_rows(acc[p * piece : (p + 1) * piece], split) + lat_ref[2 * index : 2 * index + 2, head]
            mean_ref[2 * p : 2 * p + 2, head] = found / doc_counts(split, piece, HD)


def part_kernel(where, starts, sums_ref, v_ref, part_ref):
    piece = v_ref.shape[0] // PIECES
    per_block = BLK // piece
    partner = lax.rem(where[0] + 2, 4)
    counts = [doc_counts(split_of(where, starts, p, partner), piece, HD) for p in range(PIECES)]
    for h in range(v_ref.shape[1] // HD):
        head = slice(h * HD, (h + 1) * HD)
        sums = sums_ref[:, h * BLK : (h + 1) * BLK]
        found = [dot(sums.astype(BF16), v_ref[block * BLK : (block + 1) * BLK, head]) for block in range(v_ref.shape[0] // BLK)]
        for p in range(PIECES):
            rows = slice(2 * p, 2 * p + 2)
            part_ref[rows, head] = found[p // per_block][rows] / counts[p]


def route_kernel(where, owners, part_ref, *refs):
    mean_refs, out_ref = refs[:-1], refs[-1]
    here, partner = where[0], lax.rem(where[0] + 2, 4)
    means = jnp.concatenate([mean_ref[...] for mean_ref in mean_refs], axis=0)
    parts = part_ref[...]
    for target in range(out_ref.shape[0]):
        rows = []
        for group, shard in ((means, here), (parts, partner)):
            chosen = jnp.zeros((2, out_ref.shape[2]), F32)
            for p in range(PIECES):
                chosen = jnp.where(owners[2 * (PIECES * shard + p)] == target, group[2 * p : 2 * p + 2], chosen)
            rows.append(chosen)
        out_ref[target] = jnp.concatenate(rows, axis=0).astype(BF16)


def pool_kernel(got_ref, out_ref):
    got = [got_ref[s].astype(F32) for s in range(4)]
    for s in range(4):
        out_ref[0, s] = (got[s][:2] + got[s ^ 2][2:]).astype(BF16)


def context_kernel(block, where, acc_ref, w_ref, vb_ref, va_ref, *refs):
    out_ref, vals, stage, in_sems, out_sems = refs[-5:]
    behind = where[0] >= 2
    width = 2 * HD
    pairs = [pl.ds(first, width) for first in range(0, acc_ref.shape[1], width)]

    def fetch(source, i):
        return pltpu.make_async_copy(source.at[:, pairs[i]], vals.at[:, pairs[i]], in_sems.at[i])

    @pl.when(behind)
    def _():
        for i in range(len(pairs)):
            fetch(vb_ref, i).start()

    @pl.when(jnp.logical_not(behind))
    def _():
        for i in range(len(pairs)):
            fetch(va_ref, i).start()

    copies = []
    for i, pair in enumerate(pairs):
        fetch(vb_ref, i).wait()
        for h in range(2 * i, 2 * i + 2):
            head = pl.ds(h * HD, HD)
            found = dot(w_ref[pl.ds(block * BLK, BLK), pl.ds(h * BLK, BLK)], vals[:, head])
            stage[:, head] = (acc_ref[:, head] + found).astype(BF16)
        copy = pltpu.make_async_copy(stage.at[:, pair], out_ref.at[pl.ds(block * BLK, BLK), pair], out_sems.at[i])
        copy.start()
        copies.append(copy)
    for copy in copies:
        copy.wait()


def spec(rows, columns=HD):
    return pl.BlockSpec((rows, columns), lambda h: (0, h))


def smem(count):
    return [pl.BlockSpec(memory_space=pltpu.SMEM)] * count


def vmem(count):
    return [pl.BlockSpec(memory_space=pltpu.VMEM)] * count


def shape(rows, columns, kind=F32):
    return jax.ShapeDtypeStruct((rows, columns), kind)


def step_of(heads):
    return 2 if heads % 2 == 0 else 1


def own_call(queries, keys, values):
    rows, columns = queries.shape
    heads = columns // HD
    wide = step_of(heads) * HD
    return pl.pallas_call(
        own_kernel,
        grid=(columns // wide,),
        in_specs=[spec(rows, wide)] * 3,
        out_specs=[spec(rows, wide)] * 3,
        out_shape=(shape(rows, columns),) * 3,
        compiler_params=PARAMS,
        cost_estimate=pl.CostEstimate(
            flops=4 * rows * columns * rows, bytes_accessed=18 * rows * columns, transcendentals=heads * rows * rows
        ),
        name="own",
    )(queries, keys, values)


def latent_call(where, doc_starts, queries, latent_keys, latent_values, first=0, last=None):
    rows, columns = queries.shape
    latents = latent_keys.shape[0]
    wide = step_of(columns // HD) * HD
    steps = (last or columns // wide) - first
    return pl.pallas_call(
        latent_kernel,
        grid=(steps,),
        in_specs=smem(2) + [pl.BlockSpec((size, wide), lambda h: (0, h + first)) for size in (rows, latents, latents)],
        out_specs=spec(2 * PIECES, wide),
        out_shape=shape(2 * PIECES, steps * wide),
        compiler_params=PARAMS,
        cost_estimate=pl.CostEstimate(
            flops=4 * rows * steps * wide * latents * (1 if first == 0 else 10),
            bytes_accessed=6 * rows * steps * wide,
            transcendentals=steps * wide // HD * rows * latents,
        ),
        name="latent",
    )(where, doc_starts, queries, latent_keys, latent_values)


def four_shards(queries, keys, values, latent_keys, latent_values, pattern, doc_starts, doc_owner):
    rows, columns = queries.shape
    heads = columns // HD
    step = step_of(heads)
    wide = step * HD
    slots = heads * BLK
    blocks = rows // BLK
    docs = 2 * PIECES // blocks
    where = lax.axis_index("seq").astype(jnp.int32).reshape(1)
    right, left = [(0, 1), (1, 2), (2, 3)], [(1, 0), (2, 1), (3, 2)]

    def move(value, pairs):
        return lax.ppermute(value, "seq", pairs)

    def near(value):
        return [move(value, right), move(value, left)]

    def onward(pair):
        return [move(pair[0], right[1:]), move(pair[1], left[:-1])]

    def part(array, block):
        return array[block * BLK : (block + 1) * BLK]

    def row_spec(block, width=wide):
        return pl.BlockSpec((BLK, width), lambda h: (block, h))

    def weigh_near(near_keys, state):
        return pl.pallas_call(
            functools.partial(near_weigh_kernel, 4),
            grid=(heads // step,),
            in_specs=smem(2) + [spec(rows, wide)] * 6,
            out_specs=[spec(rows, wide)] * 3 + [spec(rows, step * BLK)] * 2,
            out_shape=(shape(rows, columns),) * 3 + (shape(rows, slots, BF16),) * 2,
            input_output_aliases={5: 0, 6: 1, 7: 2},
            compiler_params=PARAMS,
            cost_estimate=pl.CostEstimate(
                flops=4 * rows * columns * BLK, bytes_accessed=20 * rows * columns, transcendentals=2 * heads * rows * BLK
            ),
            name="weigh_near",
        )(where, pattern, queries, *near_keys, *state)

    def weigh_far(far_keys, top, total):
        return pl.pallas_call(
            functools.partial(far_weigh_kernel, 4),
            grid=(heads // step,),
            in_specs=smem(3) + [spec(rows, wide)] * 5,
            out_specs=[spec(rows, wide), spec(rows, step * BLK), spec(2 * PIECES, step * BLK)],
            out_shape=(shape(rows, columns), shape(rows, slots, BF16), shape(2 * PIECES, slots, BF16)),
            compiler_params=PARAMS,
            cost_estimate=pl.CostEstimate(
                flops=2 * rows * columns * BLK, bytes_accessed=22 * rows * columns, transcendentals=heads * rows * BLK
            ),
            name="weigh_far",
        )(where, pattern, doc_starts, queries, *far_keys, top, total)

    def mix(block, acc, scale, weights, near_vals, lat):
        return pl.pallas_call(
            functools.partial(mix_kernel, block),
            grid=(heads // step,),
            in_specs=smem(2)
            + [row_spec(block)] * 2
            + [row_spec(block, step * BLK)] * 2
            + [row_spec(0)] * 2
            + [spec(2 * PIECES, wide)],
            out_specs=[row_spec(0), spec(docs, wide)],
            out_shape=(shape(BLK, columns), shape(docs, columns)),
            compiler_params=PARAMS,
            cost_estimate=pl.CostEstimate(flops=4 * BLK * columns * BLK, bytes_accessed=20 * BLK * columns, transcendentals=0),
            name="mix",
        )(where, doc_starts, acc, scale, *weights, *near_vals, lat)

    def finish(block, acc, weights, far_vals, context):
        held = [] if context is None else [context]
        anywhere = pl.BlockSpec(memory_space=pl.ANY)
        return pl.pallas_call(
            functools.partial(context_kernel, block),
            in_specs=smem(1) + vmem(2) + [anywhere] * (2 + len(held)),
            out_specs=anywhere,
            out_shape=shape(rows, columns, BF16),
            scratch_shapes=[pltpu.VMEM((BLK, columns), BF16)] * 2 + [pltpu.SemaphoreType.DMA((heads // 2,))] * 2,
            input_output_aliases={5: 0} if held else {},
            compiler_params=PARAMS,
            cost_estimate=pl.CostEstimate(flops=2 * BLK * columns * BLK, bytes_accessed=14 * BLK * columns, transcendentals=0),
            name="finish",
        )(where, acc, weights, *far_vals, *held)

    near_keys = near(keys)
    lats = [latent_call(where, doc_starts, queries, latent_keys, latent_values, 0, 1)]
    lats, late_vals, late_queries = lax.optimization_barrier((lats, values, queries))
    near_vals = [near(part(late_vals, 0))]
    state = own_call(late_queries, keys, values)
    near_keys, state = lax.optimization_barrier((near_keys, state))
    far_keys = onward(near_keys)
    near_vals[0], late_vals, late_queries = lax.optimization_barrier((near_vals[0], late_vals, late_queries))
    lats.append(latent_call(where, doc_starts, late_queries, latent_keys, latent_values, 1))
    lat = jnp.concatenate(lats, axis=1)
    near_vals.append(near(part(late_vals, 1)))
    acc, top, total, *near_weights = weigh_near(near_keys, state)
    far_keys, lat, top = lax.optimization_barrier((far_keys, lat, top))
    weighed = weigh_far(far_keys, top, total)
    near_vals[0], weighed = lax.optimization_barrier((near_vals[0], weighed))
    scale, far_weights, sums = weighed
    sums = move(sums, [(s, s ^ 2) for s in range(4)])
    far_vals = [onward(near_vals[0])]
    parts = pl.pallas_call(
        part_kernel,
        grid=(heads // step,),
        in_specs=smem(2) + [spec(2 * PIECES, step * BLK), spec(rows, wide)],
        out_specs=spec(2 * PIECES, wide),
        out_shape=shape(2 * PIECES, columns),
        compiler_params=PARAMS,
        cost_estimate=pl.CostEstimate(flops=64 * rows * columns * 32, bytes_accessed=3 * rows * columns, transcendentals=0),
        name="part",
    )(where, doc_starts, sums, values)
    mixed = [mix(0, acc, scale, near_weights, near_vals[0], lat)]
    near_vals[1], parts, mixed[0] = lax.optimization_barrier((near_vals[1], parts, mixed[0]))
    far_vals.append(onward(near_vals[1]))
    mixed.append(mix(1, acc, scale, near_weights, near_vals[1], lat))
    context = finish(0, mixed[0][0], far_weights, far_vals[0], None)
    sent = pl.pallas_call(
        route_kernel,
        in_specs=smem(2) + vmem(3),
        out_specs=pl.BlockSpec(memory_space=pltpu.VMEM),
        out_shape=jax.ShapeDtypeStruct((4, 4, columns), BF16),
        compiler_params=PARAMS,
        name="route",
    )(where, doc_owner, parts, *[m[1] for m in mixed])
    sent, context = lax.optimization_barrier((sent, context))
    got = lax.all_to_all(sent, "seq", split_axis=0, concat_axis=0, tiled=True)
    context = finish(1, mixed[1][0], far_weights, far_vals[1], context)
    got, context = lax.optimization_barrier((got, context))
    pooled = pl.pallas_call(
        pool_kernel,
        in_specs=vmem(1),
        out_specs=pl.BlockSpec(memory_space=pltpu.VMEM),
        out_shape=jax.ShapeDtypeStruct((1, 4, 2, columns), BF16),
        compiler_params=PARAMS,
        name="pool",
    )(got)
    return context, pooled


def body(queries, keys, values, latent_keys, latent_values, pattern, doc_starts, doc_owner):
    rows, columns = queries.shape
    heads = columns // HD
    shards = lax.axis_size("seq")
    seq_index = lax.axis_index("seq")
    where = seq_index.astype(jnp.int32).reshape(1)
    levels = [j for j in range(LEVELS) if 2**j < shards]
    last = levels[-1]
    merged = 2 * 2**last >= shards
    rotate = shards <= 4

    def both_ways(value, distance):
        behind = lax.ppermute(value, "seq", [(s, s + distance) for s in range(shards - distance)])
        ahead = lax.ppermute(value, "seq", [(s, s - distance) for s in range(distance, shards)])
        return [behind, ahead]

    def far(value, near):
        if last != 1:
            return both_ways(value, 2**last)
        behind = lax.ppermute(near[0], "seq", [(s, s + 1) for s in range(1, shards - 1)])
        ahead = lax.ppermute(near[1], "seq", [(s, s - 1) for s in range(1, shards - 1)])
        return [behind, ahead]

    if shards == 4:
        return four_shards(queries, keys, values, latent_keys, latent_values, pattern, doc_starts, doc_owner)
    near_keys = both_ways(keys, 1)
    near_vals = both_ways(values, 1)
    state_shapes = (shape(rows, columns),) * 3
    lat = latent_call(where, doc_starts, queries, latent_keys, latent_values)
    state = own_call(queries, keys, values)
    near_keys, state = lax.optimization_barrier((near_keys, state))

    for level in levels[:-1]:
        if level == 0:
            got = near_keys + near_vals
        else:
            got = both_ways(keys, 2**level) + both_ways(values, 2**level)
        state = pl.pallas_call(
            functools.partial(near_kernel, shards, level),
            grid=(heads,),
            in_specs=smem(2) + [spec(rows)] * 8,
            out_specs=[spec(rows)] * 3,
            out_shape=state_shapes,
            input_output_aliases={7 + i: i for i in range(3)},
            compiler_params=PARAMS,
            cost_estimate=pl.CostEstimate(
                flops=8 * rows * columns * BLK, bytes_accessed=20 * rows * columns * 2, transcendentals=2 * heads * rows * BLK
            ),
            name="near",
        )(where, pattern, queries, *got, *state)

    far_keys = far(keys, near_keys)
    far_vals = far(values, near_vals)
    sources = 1 if merged else 2
    acc, *weights = pl.pallas_call(
        functools.partial(far_kernel, shards, last, merged),
        grid=(heads,),
        in_specs=smem(2) + [spec(rows)] * 6,
        out_specs=[spec(rows)] + [spec(rows, BLK)] * sources,
        out_shape=(shape(rows, columns),) + (shape(rows, heads * BLK, BF16),) * sources,
        input_output_aliases={5: 0},
        compiler_params=PARAMS,
        cost_estimate=pl.CostEstimate(
            flops=2 * sources * rows * columns * BLK,
            bytes_accessed=(10 + 3 * sources) * rows * columns * 2,
            transcendentals=sources * heads * rows * BLK,
        ),
        name="far",
    )(where, pattern, queries, *far_keys, *state)

    if rotate:
        sent = (shape(2, columns, BF16),) * shards
    else:
        sent = (jax.ShapeDtypeStruct((shards, 2, columns), BF16),)
    context, *means = pl.pallas_call(
        functools.partial(finish_kernel, shards, last, merged),
        in_specs=smem(3) + vmem(4 + sources),
        out_specs=vmem(1 + len(sent)),
        out_shape=(shape(rows, columns, BF16),) + sent,
        compiler_params=PARAMS,
        cost_estimate=pl.CostEstimate(
            flops=2 * sources * rows * columns * BLK, bytes_accessed=(3 + 3 * sources) * rows * columns * 2, transcendentals=0
        ),
        name="finish",
    )(where, doc_starts, doc_owner, acc, lat, *weights, *far_vals)

    if not rotate:
        return context, lax.all_to_all(means[0], "seq", split_axis=0, concat_axis=0, tiled=True)[None]
    got = [means[0]]
    for r in range(1, shards):
        got.append(lax.ppermute(means[r], "seq", [(s, (s + r) % shards) for s in range(shards)]))
    pooled = []
    for s in range(shards):
        back = lax.rem(seq_index - s + shards, shards)
        row = got[0]
        for r in range(1, shards):
            row = jnp.where(back == r, got[r], row)
        pooled.append(row)
    return context, jnp.stack(pooled)[None]


def solution(mesh):
    in_specs = (
        P(("groups", "seq"), ("head", "sub")),
        P(("groups", "seq"), ("head", "sub")),
        P(("groups", "seq"), ("head", "sub")),
        P("groups", ("head", "sub")),
        P("groups", ("head", "sub")),
        P(("groups", "seq"), None),
        P("groups"),
        P("groups"),
    )
    out_specs = (
        P(("groups", "seq"), ("head", "sub")),
        P(("groups", "seq"), None, None, ("head", "sub")),
    )
    return jax.shard_map(body, mesh=mesh, in_specs=in_specs, out_specs=out_specs, check_vma=False)
```

```python
import functools
import math

import jax
import jax.numpy as jnp
from jax import lax
from jax.experimental import pallas as pl
from jax.experimental.pallas import tpu as pltpu
from jax.sharding import PartitionSpec as P

HD = 128
LEVELS = 4
BLK = 256
PIECES = 4
SCALE = math.log2(math.e) / math.sqrt(HD)
PARAMS = pltpu.CompilerParams(vmem_limit_bytes=24 * 1024 * 1024)
F32 = jnp.float32
BF16 = jnp.bfloat16


def dot_t(a, b):
    return lax.dot_general(a, b, (((1,), (1,)), ((), ())), preferred_element_type=F32)


def dot(a, b):
    return jnp.dot(a, b, preferred_element_type=F32)


def doc_rows(rows, split):
    place = lax.broadcasted_iota(jnp.int32, rows.shape, 0)
    first = jnp.sum(jnp.where(place < split, rows, 0.0), axis=0, keepdims=True)
    second = jnp.sum(jnp.where(place < split, 0.0, rows), axis=0, keepdims=True)
    return jnp.concatenate((first, second), axis=0)


def own_kernel(q_ref, k_ref, v_ref, acc_ref, top_ref, sum_ref):
    for h in range(q_ref.shape[1] // HD):
        head = slice(h * HD, (h + 1) * HD)
        s = dot_t(q_ref[:, head], k_ref[:, head]) * SCALE
        top = jnp.max(s, axis=1, keepdims=True)
        e = jnp.exp2(s - top)
        acc = dot(e.astype(BF16), v_ref[:, head])
        acc_ref[:, head] = acc
        top_ref[:, head] = jnp.broadcast_to(top, acc.shape)
        sum_ref[:, head] = jnp.broadcast_to(jnp.sum(e, axis=1, keepdims=True), acc.shape)


def latent_kernel(where, starts, q_ref, lk_ref, lv_ref, lat_ref):
    for h in range(q_ref.shape[1] // HD):
        head = slice(h * HD, (h + 1) * HD)
        s = dot_t(q_ref[:, head], lk_ref[:, head]) * SCALE
        e = jnp.exp2(s - jnp.max(s, axis=1, keepdims=True))
        out = dot(e.astype(BF16), lv_ref[:, head]) / jnp.sum(e, axis=1, keepdims=True)
        piece = out.shape[0] // PIECES
        for p in range(PIECES):
            split = split_of(where, starts, p)
            lat_ref[2 * p : 2 * p + 2, head] = doc_rows(out[p * piece : (p + 1) * piece], split)


def split_of(where, starts, p, shard=None):
    first = 2 * (PIECES * (where[0] if shard is None else shard) + p)
    return starts[first + 1] - starts[first]


def slot_live(where, pattern, shards, level, side, block):
    partner = where[0] + (2 * side - 1) * 2**level
    return (pattern[block, 2 * level + side] == 1) & (partner >= 0) & (partner < shards)


def live_scores(live, q, k):
    return jnp.where(live, dot_t(q, k) * SCALE, -jnp.inf)


def near_kernel(shards, level, where, pattern, q_ref, kb_ref, ka_ref, vb_ref, va_ref, *refs):
    acc_in, top_in, sum_in, acc_ref, top_ref, sum_ref = refs
    for block in range(q_ref.shape[0] // BLK):
        rows = pl.ds(block * BLK, BLK)
        q = q_ref[rows, :]
        scores = [
            live_scores(slot_live(where, pattern, shards, level, side, block), q, k_ref[rows, :])
            for side, k_ref in enumerate((kb_ref, ka_ref))
        ]
        old = top_in[rows, :1]
        top = old
        for s in scores:
            top = jnp.maximum(top, jnp.max(s, axis=1, keepdims=True))
        shrink = jnp.exp2(old - top)
        total = sum_in[rows, :1] * shrink
        acc = acc_in[rows, :] * shrink
        for s, v_ref in zip(scores, (vb_ref, va_ref)):
            e = jnp.exp2(s - top)
            total = total + jnp.sum(e, axis=1, keepdims=True)
            acc = acc + dot(e.astype(BF16), v_ref[rows, :])
        acc_ref[rows, :] = acc
        top_ref[rows, :] = jnp.broadcast_to(top, acc.shape)
        sum_ref[rows, :] = jnp.broadcast_to(total, acc.shape)


def far_kernel(shards, level, merged, where, pattern, q_ref, kb_ref, ka_ref, acc_in, top_in, sum_in, acc_ref, *outs):
    behind = where[0] >= 2**level
    for block in range(q_ref.shape[0] // BLK):
        rows = pl.ds(block * BLK, BLK)
        q = q_ref[rows, :]
        live = [slot_live(where, pattern, shards, level, side, block) for side in range(2)]
        pair = [k_ref[rows, :] for k_ref in (kb_ref, ka_ref)]
        if merged:
            live = [(behind & live[0]) | (jnp.logical_not(behind) & live[1])]
            pair = [jnp.where(behind, pair[0], pair[1])]
        scores = [live_scores(on, q, k) for on, k in zip(live, pair)]
        old = top_in[rows, :1]
        top = old
        for s in scores:
            top = jnp.maximum(top, jnp.max(s, axis=1, keepdims=True))
        shrink = jnp.exp2(old - top)
        total = sum_in[rows, :1] * shrink
        exps = []
        for s in scores:
            e = jnp.exp2(s - top)
            total = total + jnp.sum(e, axis=1, keepdims=True)
            exps.append(e)
        inverse = 1.0 / total
        acc_ref[rows, :] = acc_in[rows, :] * (shrink * inverse)
        for e, out in zip(exps, outs):
            out[rows, :] = (e * inverse).astype(BF16)


def finish_kernel(shards, level, merged, where, starts, owners, acc_ref, lat_ref, *refs):
    sources = 1 if merged else 2
    weights, (vb_ref, va_ref) = refs[:sources], refs[sources : sources + 2]
    ctx_ref, outs = refs[sources + 2], refs[sources + 3 :]
    rows_here, columns = acc_ref.shape
    piece = rows_here // PIECES
    splits = [split_of(where, starts, p) for p in range(PIECES)]
    behind = where[0] >= 2**level
    sums = []
    for h in range(columns // HD):
        head = pl.ds(h * HD, HD)
        slots = pl.ds(h * BLK, BLK)
        found = []
        for block in range(rows_here // BLK):
            rows = pl.ds(block * BLK, BLK)
            pair = [v_ref[rows, head] for v_ref in (vb_ref, va_ref)]
            if merged:
                pair = [jnp.where(behind, pair[0], pair[1])]
            acc = acc_ref[rows, head]
            for w_ref, v in zip(weights, pair):
                acc = acc + dot(w_ref[rows, slots], v)
            ctx = acc.astype(BF16)
            ctx_ref[rows, head] = ctx
            ctx = ctx.astype(F32)
            for start in range(0, BLK, piece):
                found.append(doc_rows(ctx[start : start + piece], splits[len(found)]))
        sums.append(found)
    side = lax.broadcasted_iota(jnp.int32, (2, columns), 0)
    means = []
    for p in range(PIECES):
        count = jnp.where(side == 0, splits[p], piece - splits[p]).astype(F32)
        total = jnp.concatenate([found[p] for found in sums], axis=1) + lat_ref[2 * p : 2 * p + 2, :]
        means.append(total / count)
    for r in range(shards):
        if len(outs) == 1:
            target = r
        else:
            target = lax.rem(where[0] + r, shards)
        chosen = jnp.zeros((2, columns), F32)
        for p in range(PIECES):
            chosen = jnp.where(owners[2 * (PIECES * where[0] + p)] == target, means[p], chosen)
        if len(outs) == 1:
            outs[0][r] = chosen.astype(BF16)
        else:
            outs[r][...] = chosen.astype(BF16)


def live_bias(where, pattern, shards, level, side, block):
    return jnp.where(slot_live(where, pattern, shards, level, side, block), 0.0, -jnp.inf)


def halves(s, bias):
    return [s[:, i : i + HD] * SCALE + bias for i in range(0, BLK, HD)]


def near_weigh_kernel(shards, where, pattern, q_ref, nb_ref, na_ref, acc_in, top_in, sum_in, *refs):
    acc_ref, top_ref, sum_ref, wb_ref, wa_ref = refs
    biases = [[live_bias(where, pattern, shards, 0, side, block) for side in range(2)] for block in range(q_ref.shape[0] // BLK)]
    piece = q_ref.shape[0] // PIECES
    for h in range(q_ref.shape[1] // HD):
        head = slice(h * HD, (h + 1) * HD)
        for p in range(PIECES):
            rows = slice(p * piece, (p + 1) * piece)
            block = p * piece // BLK
            held = slice(block * BLK, (block + 1) * BLK)
            q = q_ref[rows, head]
            scores = [halves(dot_t(q, k_ref[held, head]), bias) for k_ref, bias in zip((nb_ref, na_ref), biases[block])]
            old = top_in[rows, head]
            top = jnp.max(functools.reduce(jnp.maximum, scores[0] + scores[1]), axis=1, keepdims=True)
            top = jnp.maximum(top, old)
            shrink = jnp.exp2(old - top)
            exps = [[jnp.exp2(x - top) for x in pair] for pair in scores]
            added = jnp.sum(functools.reduce(jnp.add, exps[0] + exps[1]), axis=1, keepdims=True)
            top_ref[rows, head] = top
            sum_ref[rows, head] = sum_in[rows, head] * shrink + added
            acc_ref[rows, head] = acc_in[rows, head] * shrink
            for pair, out in zip(exps, (wb_ref, wa_ref)):
                for i, e in enumerate(pair):
                    first = h * BLK + i * HD
                    out[rows, first : first + HD] = e.astype(BF16)


def far_weigh_kernel(shards, where, pattern, starts, q_ref, fb_ref, fa_ref, top_in, sum_in, scale_ref, wf_ref, sums_ref):
    behind = where[0] >= 2
    biases = []
    for block in range(q_ref.shape[0] // BLK):
        pair = [live_bias(where, pattern, shards, 1, side, block) for side in range(2)]
        biases.append(jnp.where(behind, pair[0], pair[1]))
    piece = q_ref.shape[0] // PIECES
    place = lax.broadcasted_iota(jnp.int32, (piece, HD), 0)
    firsts = [place < split_of(where, starts, p) for p in range(PIECES)]
    for h in range(q_ref.shape[1] // HD):
        head = slice(h * HD, (h + 1) * HD)
        sums = [[] for _ in range(BLK // HD)]
        for p in range(PIECES):
            rows = slice(p * piece, (p + 1) * piece)
            block = p * piece // BLK
            held = slice(block * BLK, (block + 1) * BLK)
            keys = jnp.where(behind, fb_ref[held, head], fa_ref[held, head])
            scores = halves(dot_t(q_ref[rows, head], keys), biases[block])
            old = top_in[rows, head]
            top = jnp.maximum(jnp.max(functools.reduce(jnp.maximum, scores), axis=1, keepdims=True), old)
            shrink = jnp.exp2(old - top)
            exps = [jnp.exp2(x - top) for x in scores]
            added = jnp.sum(functools.reduce(jnp.add, exps), axis=1, keepdims=True)
            inverse = 1.0 / (sum_in[rows, head] * shrink + added)
            scale_ref[rows, head] = shrink * inverse
            for i, e in enumerate(exps):
                first = h * BLK + i * HD
                w = e * inverse
                wf_ref[rows, first : first + HD] = w.astype(BF16)
                sums[i] += [
                    jnp.sum(jnp.where(firsts[p], w, 0.0), axis=0, keepdims=True),
                    jnp.sum(jnp.where(firsts[p], 0.0, w), axis=0, keepdims=True),
                ]
        for i, found in enumerate(sums):
            first = h * BLK + i * HD
            sums_ref[:, first : first + HD] = jnp.concatenate(found, axis=0).astype(sums_ref.dtype)


def doc_counts(split, piece, columns):
    side = lax.broadcasted_iota(jnp.int32, (2, columns), 0)
    return jnp.where(side == 0, split, piece - split).astype(F32)


def mix_kernel(block, where, starts, acc_in, scale_in, wb_ref, wa_ref, vb_ref, va_ref, lat_ref, acc_ref, mean_ref):
    pieces = mean_ref.shape[0] // 2
    piece = BLK // pieces
    for h in range(acc_in.shape[1] // HD):
        head = slice(h * HD, (h + 1) * HD)
        slots = slice(h * BLK, (h + 1) * BLK)
        acc = acc_in[:, head] + dot(wb_ref[:, slots], vb_ref[:, head]) + dot(wa_ref[:, slots], va_ref[:, head])
        acc = acc * scale_in[:, head]
        acc_ref[:, head] = acc
        for p in range(pieces):
            index = block * pieces + p
            split = split_of(where, starts, index)
            found = doc_rows(acc[p * piece : (p + 1) * piece], split) + lat_ref[2 * index : 2 * index + 2, head]
            mean_ref[2 * p : 2 * p + 2, head] = found / doc_counts(split, piece, HD)


def part_kernel(where, starts, sums_ref, v_ref, part_ref):
    piece = v_ref.shape[0] // PIECES
    per_block = BLK // piece
    partner = lax.rem(where[0] + 2, 4)
    counts = [doc_counts(split_of(where, starts, p, partner), piece, HD) for p in range(PIECES)]
    for h in range(v_ref.shape[1] // HD):
        head = slice(h * HD, (h + 1) * HD)
        sums = sums_ref[:, h * BLK : (h + 1) * BLK]
        found = [dot(sums.astype(BF16), v_ref[block * BLK : (block + 1) * BLK, head]) for block in range(v_ref.shape[0] // BLK)]
        for p in range(PIECES):
            rows = slice(2 * p, 2 * p + 2)
            part_ref[rows, head] = found[p // per_block][rows] / counts[p]


def route_kernel(where, owners, part_ref, *refs):
    mean_refs, out_refs = refs[:-4], refs[-4:]
    here, partner = where[0], lax.rem(where[0] + 2, 4)
    means = jnp.concatenate([mean_ref[...] for mean_ref in mean_refs], axis=0)
    parts = part_ref[...]
    for r, out_ref in enumerate(out_refs):
        target = lax.rem(here + r, 4)
        rows = []
        for group, shard in ((means, here), (parts, partner)):
            chosen = jnp.zeros((2, out_ref.shape[1]), F32)
            for p in range(PIECES):
                chosen = jnp.where(owners[2 * (PIECES * shard + p)] == target, group[2 * p : 2 * p + 2], chosen)
            rows.append(chosen)
        out_ref[...] = jnp.concatenate(rows, axis=0)


def pool_kernel(where, *refs):
    got, out_ref = refs[:4], refs[4]
    for s in range(4):
        rows = []
        for first, shard in ((0, s), (2, s ^ 2)):
            back = lax.rem(where[0] - shard + 4, 4)
            found = got[0][first : first + 2, :]
            for r in range(1, 4):
                found = jnp.where(back == r, got[r][first : first + 2, :], found)
            rows.append(found)
        out_ref[0, s] = (rows[0] + rows[1]).astype(BF16)


def context_kernel(block, where, acc_ref, w_ref, vb_ref, va_ref, *refs):
    out_ref, stage, sem = refs[-3:]
    behind = where[0] >= 2
    copies = []
    for h in range(acc_ref.shape[1] // HD):
        head = pl.ds(h * HD, HD)
        v = jnp.where(behind, vb_ref[:, head], va_ref[:, head])
        stage[:, head] = (acc_ref[:, head] + dot(w_ref[pl.ds(block * BLK, BLK), pl.ds(h * BLK, BLK)], v)).astype(BF16)
        if h % 2:
            pair = pl.ds((h - 1) * HD, 2 * HD)
            copy = pltpu.make_async_copy(stage.at[:, pair], out_ref.at[pl.ds(block * BLK, BLK), pair], sem.at[h // 2])
            copy.start()
            copies.append(copy)
    for copy in copies:
        copy.wait()


def spec(rows, columns=HD):
    return pl.BlockSpec((rows, columns), lambda h: (0, h))


def smem(count):
    return [pl.BlockSpec(memory_space=pltpu.SMEM)] * count


def vmem(count):
    return [pl.BlockSpec(memory_space=pltpu.VMEM)] * count


def shape(rows, columns, kind=F32):
    return jax.ShapeDtypeStruct((rows, columns), kind)


def step_of(heads):
    return 2 if heads % 2 == 0 else 1


def own_call(queries, keys, values):
    rows, columns = queries.shape
    heads = columns // HD
    wide = step_of(heads) * HD
    return pl.pallas_call(
        own_kernel,
        grid=(columns // wide,),
        in_specs=[spec(rows, wide)] * 3,
        out_specs=[spec(rows, wide)] * 3,
        out_shape=(shape(rows, columns),) * 3,
        compiler_params=PARAMS,
        cost_estimate=pl.CostEstimate(
            flops=4 * rows * columns * rows, bytes_accessed=18 * rows * columns, transcendentals=heads * rows * rows
        ),
        name="own",
    )(queries, keys, values)


def latent_call(where, doc_starts, queries, latent_keys, latent_values, first=0, last=None):
    rows, columns = queries.shape
    latents = latent_keys.shape[0]
    wide = step_of(columns // HD) * HD
    steps = (last or columns // wide) - first
    return pl.pallas_call(
        latent_kernel,
        grid=(steps,),
        in_specs=smem(2) + [pl.BlockSpec((size, wide), lambda h: (0, h + first)) for size in (rows, latents, latents)],
        out_specs=spec(2 * PIECES, wide),
        out_shape=shape(2 * PIECES, steps * wide),
        compiler_params=PARAMS,
        cost_estimate=pl.CostEstimate(
            flops=4 * rows * steps * wide * latents * (1 if first == 0 else 10),
            bytes_accessed=6 * rows * steps * wide,
            transcendentals=steps * wide // HD * rows * latents,
        ),
        name="latent",
    )(where, doc_starts, queries, latent_keys, latent_values)


def four_shards(queries, keys, values, latent_keys, latent_values, pattern, doc_starts, doc_owner):
    rows, columns = queries.shape
    heads = columns // HD
    step = step_of(heads)
    wide = step * HD
    slots = heads * BLK
    blocks = rows // BLK
    docs = 2 * PIECES // blocks
    where = lax.axis_index("seq").astype(jnp.int32).reshape(1)
    right, left = [(0, 1), (1, 2), (2, 3)], [(1, 0), (2, 1), (3, 2)]

    def move(value, pairs):
        return lax.ppermute(value, "seq", pairs)

    def near(value):
        return [move(value, right), move(value, left)]

    def onward(pair):
        return [move(pair[0], right[1:]), move(pair[1], left[:-1])]

    def part(array, block):
        return array[block * BLK : (block + 1) * BLK]

    def row_spec(block, width=wide):
        return pl.BlockSpec((BLK, width), lambda h: (block, h))

    def weigh_near(near_keys, state):
        return pl.pallas_call(
            functools.partial(near_weigh_kernel, 4),
            grid=(heads // step,),
            in_specs=smem(2) + [spec(rows, wide)] * 6,
            out_specs=[spec(rows, wide)] * 3 + [spec(rows, step * BLK)] * 2,
            out_shape=(shape(rows, columns),) * 3 + (shape(rows, slots, BF16),) * 2,
            input_output_aliases={5: 0, 6: 1, 7: 2},
            compiler_params=PARAMS,
            cost_estimate=pl.CostEstimate(
                flops=4 * rows * columns * BLK, bytes_accessed=20 * rows * columns, transcendentals=2 * heads * rows * BLK
            ),
            name="weigh_near",
        )(where, pattern, queries, *near_keys, *state)

    def weigh_far(far_keys, top, total):
        return pl.pallas_call(
            functools.partial(far_weigh_kernel, 4),
            grid=(heads // step,),
            in_specs=smem(3) + [spec(rows, wide)] * 5,
            out_specs=[spec(rows, wide), spec(rows, step * BLK), spec(2 * PIECES, step * BLK)],
            out_shape=(shape(rows, columns), shape(rows, slots, BF16), shape(2 * PIECES, slots, BF16)),
            compiler_params=PARAMS,
            cost_estimate=pl.CostEstimate(
                flops=2 * rows * columns * BLK, bytes_accessed=22 * rows * columns, transcendentals=heads * rows * BLK
            ),
            name="weigh_far",
        )(where, pattern, doc_starts, queries, *far_keys, top, total)

    def mix(block, acc, scale, weights, near_vals, lat):
        return pl.pallas_call(
            functools.partial(mix_kernel, block),
            grid=(heads // step,),
            in_specs=smem(2)
            + [row_spec(block)] * 2
            + [row_spec(block, step * BLK)] * 2
            + [row_spec(0)] * 2
            + [spec(2 * PIECES, wide)],
            out_specs=[row_spec(0), spec(docs, wide)],
            out_shape=(shape(BLK, columns), shape(docs, columns)),
            compiler_params=PARAMS,
            cost_estimate=pl.CostEstimate(flops=4 * BLK * columns * BLK, bytes_accessed=20 * BLK * columns, transcendentals=0),
            name="mix",
        )(where, doc_starts, acc, scale, *weights, *near_vals, lat)

    def finish(block, acc, weights, far_vals, context):
        held = [] if context is None else [context]
        anywhere = pl.BlockSpec(memory_space=pl.ANY)
        return pl.pallas_call(
            functools.partial(context_kernel, block),
            in_specs=smem(1) + vmem(4) + [anywhere] * len(held),
            out_specs=anywhere,
            out_shape=shape(rows, columns, BF16),
            scratch_shapes=[pltpu.VMEM((BLK, columns), BF16), pltpu.SemaphoreType.DMA((heads // 2,))],
            input_output_aliases={5: 0} if held else {},
            compiler_params=PARAMS,
            cost_estimate=pl.CostEstimate(flops=2 * BLK * columns * BLK, bytes_accessed=14 * BLK * columns, transcendentals=0),
            name="finish",
        )(where, acc, weights, *far_vals, *held)

    near_keys = near(keys)
    lats = [latent_call(where, doc_starts, queries, latent_keys, latent_values, 0, 1)]
    lats, late_vals, late_queries = lax.optimization_barrier((lats, values, queries))
    near_vals = [near(part(late_vals, 0))]
    state = own_call(late_queries, keys, values)
    near_keys, state = lax.optimization_barrier((near_keys, state))
    far_keys = onward(near_keys)
    near_vals[0], late_vals, late_queries = lax.optimization_barrier((near_vals[0], late_vals, late_queries))
    lats.append(latent_call(where, doc_starts, late_queries, latent_keys, latent_values, 1))
    lat = jnp.concatenate(lats, axis=1)
    near_vals.append(near(part(late_vals, 1)))
    acc, top, total, *near_weights = weigh_near(near_keys, state)
    far_keys, lat, top = lax.optimization_barrier((far_keys, lat, top))
    weighed = weigh_far(far_keys, top, total)
    near_vals[0], weighed = lax.optimization_barrier((near_vals[0], weighed))
    scale, far_weights, sums = weighed
    sums = move(sums, [(s, s ^ 2) for s in range(4)])
    far_vals = [onward(near_vals[0])]
    parts = pl.pallas_call(
        part_kernel,
        grid=(heads // step,),
        in_specs=smem(2) + [spec(2 * PIECES, step * BLK), spec(rows, wide)],
        out_specs=spec(2 * PIECES, wide),
        out_shape=shape(2 * PIECES, columns),
        compiler_params=PARAMS,
        cost_estimate=pl.CostEstimate(flops=64 * rows * columns * 32, bytes_accessed=3 * rows * columns, transcendentals=0),
        name="part",
    )(where, doc_starts, sums, values)
    mixed = [mix(0, acc, scale, near_weights, near_vals[0], lat)]
    near_vals[1], parts, mixed[0] = lax.optimization_barrier((near_vals[1], parts, mixed[0]))
    far_vals.append(onward(near_vals[1]))
    mixed.append(mix(1, acc, scale, near_weights, near_vals[1], lat))
    context = finish(0, mixed[0][0], far_weights, far_vals[0], None)
    sent = pl.pallas_call(
        route_kernel,
        in_specs=smem(2) + vmem(3),
        out_specs=vmem(4),
        out_shape=(shape(4, columns),) * 4,
        compiler_params=PARAMS,
        name="route",
    )(where, doc_owner, parts, *[m[1] for m in mixed])
    sent, context = lax.optimization_barrier((sent, context))
    got = [sent[0]] + [move(sent[r], [(s, (s + r) % 4) for s in range(4)]) for r in range(1, 4)]
    context = finish(1, mixed[1][0], far_weights, far_vals[1], context)
    got, context = lax.optimization_barrier((got, context))
    pooled = pl.pallas_call(
        pool_kernel,
        in_specs=smem(1) + vmem(4),
        out_specs=pl.BlockSpec(memory_space=pltpu.VMEM),
        out_shape=jax.ShapeDtypeStruct((1, 4, 2, columns), BF16),
        compiler_params=PARAMS,
        name="pool",
    )(where, *got)
    return context, pooled


def body(queries, keys, values, latent_keys, latent_values, pattern, doc_starts, doc_owner):
    rows, columns = queries.shape
    heads = columns // HD
    shards = lax.axis_size("seq")
    seq_index = lax.axis_index("seq")
    where = seq_index.astype(jnp.int32).reshape(1)
    levels = [j for j in range(LEVELS) if 2**j < shards]
    last = levels[-1]
    merged = 2 * 2**last >= shards
    rotate = shards <= 4

    def both_ways(value, distance):
        behind = lax.ppermute(value, "seq", [(s, s + distance) for s in range(shards - distance)])
        ahead = lax.ppermute(value, "seq", [(s, s - distance) for s in range(distance, shards)])
        return [behind, ahead]

    def far(value, near):
        if last != 1:
            return both_ways(value, 2**last)
        behind = lax.ppermute(near[0], "seq", [(s, s + 1) for s in range(1, shards - 1)])
        ahead = lax.ppermute(near[1], "seq", [(s, s - 1) for s in range(1, shards - 1)])
        return [behind, ahead]

    if shards == 4:
        return four_shards(queries, keys, values, latent_keys, latent_values, pattern, doc_starts, doc_owner)
    near_keys = both_ways(keys, 1)
    near_vals = both_ways(values, 1)
    state_shapes = (shape(rows, columns),) * 3
    lat = latent_call(where, doc_starts, queries, latent_keys, latent_values)
    state = own_call(queries, keys, values)
    near_keys, state = lax.optimization_barrier((near_keys, state))

    for level in levels[:-1]:
        if level == 0:
            got = near_keys + near_vals
        else:
            got = both_ways(keys, 2**level) + both_ways(values, 2**level)
        state = pl.pallas_call(
            functools.partial(near_kernel, shards, level),
            grid=(heads,),
            in_specs=smem(2) + [spec(rows)] * 8,
            out_specs=[spec(rows)] * 3,
            out_shape=state_shapes,
            input_output_aliases={7 + i: i for i in range(3)},
            compiler_params=PARAMS,
            cost_estimate=pl.CostEstimate(
                flops=8 * rows * columns * BLK, bytes_accessed=20 * rows * columns * 2, transcendentals=2 * heads * rows * BLK
            ),
            name="near",
        )(where, pattern, queries, *got, *state)

    far_keys = far(keys, near_keys)
    far_vals = far(values, near_vals)
    sources = 1 if merged else 2
    acc, *weights = pl.pallas_call(
        functools.partial(far_kernel, shards, last, merged),
        grid=(heads,),
        in_specs=smem(2) + [spec(rows)] * 6,
        out_specs=[spec(rows)] + [spec(rows, BLK)] * sources,
        out_shape=(shape(rows, columns),) + (shape(rows, heads * BLK, BF16),) * sources,
        input_output_aliases={5: 0},
        compiler_params=PARAMS,
        cost_estimate=pl.CostEstimate(
            flops=2 * sources * rows * columns * BLK,
            bytes_accessed=(10 + 3 * sources) * rows * columns * 2,
            transcendentals=sources * heads * rows * BLK,
        ),
        name="far",
    )(where, pattern, queries, *far_keys, *state)

    if rotate:
        sent = (shape(2, columns, BF16),) * shards
    else:
        sent = (jax.ShapeDtypeStruct((shards, 2, columns), BF16),)
    context, *means = pl.pallas_call(
        functools.partial(finish_kernel, shards, last, merged),
        in_specs=smem(3) + vmem(4 + sources),
        out_specs=vmem(1 + len(sent)),
        out_shape=(shape(rows, columns, BF16),) + sent,
        compiler_params=PARAMS,
        cost_estimate=pl.CostEstimate(
            flops=2 * sources * rows * columns * BLK, bytes_accessed=(3 + 3 * sources) * rows * columns * 2, transcendentals=0
        ),
        name="finish",
    )(where, doc_starts, doc_owner, acc, lat, *weights, *far_vals)

    if not rotate:
        return context, lax.all_to_all(means[0], "seq", split_axis=0, concat_axis=0, tiled=True)[None]
    got = [means[0]]
    for r in range(1, shards):
        got.append(lax.ppermute(means[r], "seq", [(s, (s + r) % shards) for s in range(shards)]))
    pooled = []
    for s in range(shards):
        back = lax.rem(seq_index - s + shards, shards)
        row = got[0]
        for r in range(1, shards):
            row = jnp.where(back == r, got[r], row)
        pooled.append(row)
    return context, jnp.stack(pooled)[None]


def solution(mesh):
    in_specs = (
        P(("groups", "seq"), ("head", "sub")),
        P(("groups", "seq"), ("head", "sub")),
        P(("groups", "seq"), ("head", "sub")),
        P("groups", ("head", "sub")),
        P("groups", ("head", "sub")),
        P(("groups", "seq"), None),
        P("groups"),
        P("groups"),
    )
    out_specs = (
        P(("groups", "seq"), ("head", "sub")),
        P(("groups", "seq"), None, None, ("head", "sub")),
    )
    return jax.shard_map(body, mesh=mesh, in_specs=in_specs, out_specs=out_specs, check_vma=False)
```

```python
import functools
import math

import jax
import jax.numpy as jnp
from jax import lax
from jax.experimental import pallas as pl
from jax.experimental.pallas import tpu as pltpu
from jax.sharding import PartitionSpec as P

HD = 128
LEVELS = 4
BLK = 256
PIECES = 4
SCALE = math.log2(math.e) / math.sqrt(HD)
PARAMS = pltpu.CompilerParams(vmem_limit_bytes=24 * 1024 * 1024)
F32 = jnp.float32
BF16 = jnp.bfloat16


def dot_t(a, b):
    return lax.dot_general(a, b, (((1,), (1,)), ((), ())), preferred_element_type=F32)


def dot(a, b):
    return jnp.dot(a, b, preferred_element_type=F32)


def doc_rows(rows, split):
    place = lax.broadcasted_iota(jnp.int32, rows.shape, 0)
    first = jnp.sum(jnp.where(place < split, rows, 0.0), axis=0, keepdims=True)
    second = jnp.sum(jnp.where(place < split, 0.0, rows), axis=0, keepdims=True)
    return jnp.concatenate((first, second), axis=0)


def own_kernel(q_ref, k_ref, v_ref, acc_ref, top_ref, sum_ref):
    for h in range(q_ref.shape[1] // HD):
        head = slice(h * HD, (h + 1) * HD)
        s = dot_t(q_ref[:, head], k_ref[:, head]) * SCALE
        top = jnp.max(s, axis=1, keepdims=True)
        e = jnp.exp2(s - top)
        acc = dot(e.astype(BF16), v_ref[:, head])
        acc_ref[:, head] = acc
        top_ref[:, head] = jnp.broadcast_to(top, acc.shape)
        sum_ref[:, head] = jnp.broadcast_to(jnp.sum(e, axis=1, keepdims=True), acc.shape)


def latent_kernel(where, starts, q_ref, lk_ref, lv_ref, lat_ref):
    for h in range(q_ref.shape[1] // HD):
        head = slice(h * HD, (h + 1) * HD)
        s = dot_t(q_ref[:, head], lk_ref[:, head]) * SCALE
        e = jnp.exp2(s - jnp.max(s, axis=1, keepdims=True))
        out = dot(e.astype(BF16), lv_ref[:, head]) / jnp.sum(e, axis=1, keepdims=True)
        piece = out.shape[0] // PIECES
        for p in range(PIECES):
            split = split_of(where, starts, p)
            lat_ref[2 * p : 2 * p + 2, head] = doc_rows(out[p * piece : (p + 1) * piece], split)


def split_of(where, starts, p, shard=None):
    first = 2 * (PIECES * (where[0] if shard is None else shard) + p)
    return starts[first + 1] - starts[first]


def slot_live(where, pattern, shards, level, side, block):
    partner = where[0] + (2 * side - 1) * 2**level
    return (pattern[block, 2 * level + side] == 1) & (partner >= 0) & (partner < shards)


def live_scores(live, q, k):
    return jnp.where(live, dot_t(q, k) * SCALE, -jnp.inf)


def near_kernel(shards, level, where, pattern, q_ref, kb_ref, ka_ref, vb_ref, va_ref, *refs):
    acc_in, top_in, sum_in, acc_ref, top_ref, sum_ref = refs
    for block in range(q_ref.shape[0] // BLK):
        rows = pl.ds(block * BLK, BLK)
        q = q_ref[rows, :]
        scores = [
            live_scores(slot_live(where, pattern, shards, level, side, block), q, k_ref[rows, :])
            for side, k_ref in enumerate((kb_ref, ka_ref))
        ]
        old = top_in[rows, :1]
        top = old
        for s in scores:
            top = jnp.maximum(top, jnp.max(s, axis=1, keepdims=True))
        shrink = jnp.exp2(old - top)
        total = sum_in[rows, :1] * shrink
        acc = acc_in[rows, :] * shrink
        for s, v_ref in zip(scores, (vb_ref, va_ref)):
            e = jnp.exp2(s - top)
            total = total + jnp.sum(e, axis=1, keepdims=True)
            acc = acc + dot(e.astype(BF16), v_ref[rows, :])
        acc_ref[rows, :] = acc
        top_ref[rows, :] = jnp.broadcast_to(top, acc.shape)
        sum_ref[rows, :] = jnp.broadcast_to(total, acc.shape)


def far_kernel(shards, level, merged, where, pattern, q_ref, kb_ref, ka_ref, acc_in, top_in, sum_in, acc_ref, *outs):
    behind = where[0] >= 2**level
    for block in range(q_ref.shape[0] // BLK):
        rows = pl.ds(block * BLK, BLK)
        q = q_ref[rows, :]
        live = [slot_live(where, pattern, shards, level, side, block) for side in range(2)]
        pair = [k_ref[rows, :] for k_ref in (kb_ref, ka_ref)]
        if merged:
            live = [(behind & live[0]) | (jnp.logical_not(behind) & live[1])]
            pair = [jnp.where(behind, pair[0], pair[1])]
        scores = [live_scores(on, q, k) for on, k in zip(live, pair)]
        old = top_in[rows, :1]
        top = old
        for s in scores:
            top = jnp.maximum(top, jnp.max(s, axis=1, keepdims=True))
        shrink = jnp.exp2(old - top)
        total = sum_in[rows, :1] * shrink
        exps = []
        for s in scores:
            e = jnp.exp2(s - top)
            total = total + jnp.sum(e, axis=1, keepdims=True)
            exps.append(e)
        inverse = 1.0 / total
        acc_ref[rows, :] = acc_in[rows, :] * (shrink * inverse)
        for e, out in zip(exps, outs):
            out[rows, :] = (e * inverse).astype(BF16)


def finish_kernel(shards, level, merged, where, starts, owners, acc_ref, lat_ref, *refs):
    sources = 1 if merged else 2
    weights, (vb_ref, va_ref) = refs[:sources], refs[sources : sources + 2]
    ctx_ref, outs = refs[sources + 2], refs[sources + 3 :]
    rows_here, columns = acc_ref.shape
    piece = rows_here // PIECES
    splits = [split_of(where, starts, p) for p in range(PIECES)]
    behind = where[0] >= 2**level
    sums = []
    for h in range(columns // HD):
        head = pl.ds(h * HD, HD)
        slots = pl.ds(h * BLK, BLK)
        found = []
        for block in range(rows_here // BLK):
            rows = pl.ds(block * BLK, BLK)
            pair = [v_ref[rows, head] for v_ref in (vb_ref, va_ref)]
            if merged:
                pair = [jnp.where(behind, pair[0], pair[1])]
            acc = acc_ref[rows, head]
            for w_ref, v in zip(weights, pair):
                acc = acc + dot(w_ref[rows, slots], v)
            ctx = acc.astype(BF16)
            ctx_ref[rows, head] = ctx
            ctx = ctx.astype(F32)
            for start in range(0, BLK, piece):
                found.append(doc_rows(ctx[start : start + piece], splits[len(found)]))
        sums.append(found)
    side = lax.broadcasted_iota(jnp.int32, (2, columns), 0)
    means = []
    for p in range(PIECES):
        count = jnp.where(side == 0, splits[p], piece - splits[p]).astype(F32)
        total = jnp.concatenate([found[p] for found in sums], axis=1) + lat_ref[2 * p : 2 * p + 2, :]
        means.append(total / count)
    for r in range(shards):
        if len(outs) == 1:
            target = r
        else:
            target = lax.rem(where[0] + r, shards)
        chosen = jnp.zeros((2, columns), F32)
        for p in range(PIECES):
            chosen = jnp.where(owners[2 * (PIECES * where[0] + p)] == target, means[p], chosen)
        if len(outs) == 1:
            outs[0][r] = chosen.astype(BF16)
        else:
            outs[r][...] = chosen.astype(BF16)


def live_bias(where, pattern, shards, level, side, block):
    return jnp.where(slot_live(where, pattern, shards, level, side, block), 0.0, -jnp.inf)


def halves(s, bias):
    return [s[:, i : i + HD] * SCALE + bias for i in range(0, BLK, HD)]


def near_weigh_kernel(shards, where, pattern, q_ref, nb_ref, na_ref, acc_in, top_in, sum_in, *refs):
    acc_ref, top_ref, sum_ref, wb_ref, wa_ref = refs
    biases = [[live_bias(where, pattern, shards, 0, side, block) for side in range(2)] for block in range(q_ref.shape[0] // BLK)]
    piece = q_ref.shape[0] // PIECES
    for h in range(q_ref.shape[1] // HD):
        head = slice(h * HD, (h + 1) * HD)
        for p in range(PIECES):
            rows = slice(p * piece, (p + 1) * piece)
            block = p * piece // BLK
            held = slice(block * BLK, (block + 1) * BLK)
            q = q_ref[rows, head]
            scores = [halves(dot_t(q, k_ref[held, head]), bias) for k_ref, bias in zip((nb_ref, na_ref), biases[block])]
            old = top_in[rows, head]
            top = jnp.max(functools.reduce(jnp.maximum, scores[0] + scores[1]), axis=1, keepdims=True)
            top = jnp.maximum(top, old)
            shrink = jnp.exp2(old - top)
            exps = [[jnp.exp2(x - top) for x in pair] for pair in scores]
            added = jnp.sum(functools.reduce(jnp.add, exps[0] + exps[1]), axis=1, keepdims=True)
            top_ref[rows, head] = top
            sum_ref[rows, head] = sum_in[rows, head] * shrink + added
            acc_ref[rows, head] = acc_in[rows, head] * shrink
            for pair, out in zip(exps, (wb_ref, wa_ref)):
                for i, e in enumerate(pair):
                    first = h * BLK + i * HD
                    out[rows, first : first + HD] = e.astype(BF16)


def far_weigh_kernel(shards, where, pattern, starts, q_ref, fb_ref, fa_ref, top_in, sum_in, scale_ref, wf_ref, sums_ref):
    behind = where[0] >= 2
    biases = []
    for block in range(q_ref.shape[0] // BLK):
        pair = [live_bias(where, pattern, shards, 1, side, block) for side in range(2)]
        biases.append(jnp.where(behind, pair[0], pair[1]))
    piece = q_ref.shape[0] // PIECES
    place = lax.broadcasted_iota(jnp.int32, (piece, HD), 0)
    firsts = [place < split_of(where, starts, p) for p in range(PIECES)]
    for h in range(q_ref.shape[1] // HD):
        head = slice(h * HD, (h + 1) * HD)
        sums = [[] for _ in range(BLK // HD)]
        for p in range(PIECES):
            rows = slice(p * piece, (p + 1) * piece)
            block = p * piece // BLK
            held = slice(block * BLK, (block + 1) * BLK)
            keys = jnp.where(behind, fb_ref[held, head], fa_ref[held, head])
            scores = halves(dot_t(q_ref[rows, head], keys), biases[block])
            old = top_in[rows, head]
            top = jnp.maximum(jnp.max(functools.reduce(jnp.maximum, scores), axis=1, keepdims=True), old)
            shrink = jnp.exp2(old - top)
            exps = [jnp.exp2(x - top) for x in scores]
            added = jnp.sum(functools.reduce(jnp.add, exps), axis=1, keepdims=True)
            inverse = 1.0 / (sum_in[rows, head] * shrink + added)
            scale_ref[rows, head] = shrink * inverse
            for i, e in enumerate(exps):
                first = h * BLK + i * HD
                w = e * inverse
                wf_ref[rows, first : first + HD] = w.astype(BF16)
                sums[i] += [
                    jnp.sum(jnp.where(firsts[p], w, 0.0), axis=0, keepdims=True),
                    jnp.sum(jnp.where(firsts[p], 0.0, w), axis=0, keepdims=True),
                ]
        for i, found in enumerate(sums):
            first = h * BLK + i * HD
            sums_ref[:, first : first + HD] = jnp.concatenate(found, axis=0).astype(sums_ref.dtype)


def doc_counts(split, piece, columns):
    side = lax.broadcasted_iota(jnp.int32, (2, columns), 0)
    return jnp.where(side == 0, split, piece - split).astype(F32)


def mix_kernel(block, where, starts, acc_in, scale_in, wb_ref, wa_ref, vb_ref, va_ref, lat_ref, acc_ref, mean_ref):
    pieces = mean_ref.shape[0] // 2
    piece = BLK // pieces
    for h in range(acc_in.shape[1] // HD):
        head = slice(h * HD, (h + 1) * HD)
        slots = slice(h * BLK, (h + 1) * BLK)
        acc = acc_in[:, head] + dot(wb_ref[:, slots], vb_ref[:, head]) + dot(wa_ref[:, slots], va_ref[:, head])
        acc = acc * scale_in[:, head]
        acc_ref[:, head] = acc
        for p in range(pieces):
            index = block * pieces + p
            split = split_of(where, starts, index)
            found = doc_rows(acc[p * piece : (p + 1) * piece], split) + lat_ref[2 * index : 2 * index + 2, head]
            mean_ref[2 * p : 2 * p + 2, head] = found / doc_counts(split, piece, HD)


def part_kernel(where, starts, sums_ref, v_ref, part_ref):
    piece = v_ref.shape[0] // PIECES
    per_block = BLK // piece
    partner = lax.rem(where[0] + 2, 4)
    counts = [doc_counts(split_of(where, starts, p, partner), piece, HD) for p in range(PIECES)]
    for h in range(v_ref.shape[1] // HD):
        head = slice(h * HD, (h + 1) * HD)
        sums = sums_ref[:, h * BLK : (h + 1) * BLK]
        found = [dot(sums.astype(BF16), v_ref[block * BLK : (block + 1) * BLK, head]) for block in range(v_ref.shape[0] // BLK)]
        for p in range(PIECES):
            rows = slice(2 * p, 2 * p + 2)
            part_ref[rows, head] = found[p // per_block][rows] / counts[p]


def route_kernel(where, owners, part_ref, *refs):
    mean_refs, out_refs = refs[:-4], refs[-4:]
    here, partner = where[0], lax.rem(where[0] + 2, 4)
    means = jnp.concatenate([mean_ref[...] for mean_ref in mean_refs], axis=0)
    parts = part_ref[...]
    for r, out_ref in enumerate(out_refs):
        target = lax.rem(here + r, 4)
        rows = []
        for group, shard in ((means, here), (parts, partner)):
            chosen = jnp.zeros((2, out_ref.shape[1]), F32)
            for p in range(PIECES):
                chosen = jnp.where(owners[2 * (PIECES * shard + p)] == target, group[2 * p : 2 * p + 2], chosen)
            rows.append(chosen)
        out_ref[...] = jnp.concatenate(rows, axis=0).astype(BF16)


def pool_kernel(where, *refs):
    got, out_ref = [ref[...].astype(F32) for ref in refs[:4]], refs[4]
    for s in range(4):
        rows = []
        for first, shard in ((0, s), (2, s ^ 2)):
            back = lax.rem(where[0] - shard + 4, 4)
            found = got[0][first : first + 2]
            for r in range(1, 4):
                found = jnp.where(back == r, got[r][first : first + 2], found)
            rows.append(found)
        out_ref[0, s] = (rows[0] + rows[1]).astype(BF16)


def context_kernel(block, where, acc_ref, w_ref, vb_ref, va_ref, *refs):
    out_ref, stage, sem = refs[-3:]
    behind = where[0] >= 2
    copies = []
    for h in range(acc_ref.shape[1] // HD):
        head = pl.ds(h * HD, HD)
        v = jnp.where(behind, vb_ref[:, head], va_ref[:, head])
        stage[:, head] = (acc_ref[:, head] + dot(w_ref[pl.ds(block * BLK, BLK), pl.ds(h * BLK, BLK)], v)).astype(BF16)
        if h % 2:
            pair = pl.ds((h - 1) * HD, 2 * HD)
            copy = pltpu.make_async_copy(stage.at[:, pair], out_ref.at[pl.ds(block * BLK, BLK), pair], sem.at[h // 2])
            copy.start()
            copies.append(copy)
    for copy in copies:
        copy.wait()


def spec(rows, columns=HD):
    return pl.BlockSpec((rows, columns), lambda h: (0, h))


def smem(count):
    return [pl.BlockSpec(memory_space=pltpu.SMEM)] * count


def vmem(count):
    return [pl.BlockSpec(memory_space=pltpu.VMEM)] * count


def shape(rows, columns, kind=F32):
    return jax.ShapeDtypeStruct((rows, columns), kind)


def step_of(heads):
    return 2 if heads % 2 == 0 else 1


def own_call(queries, keys, values):
    rows, columns = queries.shape
    heads = columns // HD
    wide = step_of(heads) * HD
    return pl.pallas_call(
        own_kernel,
        grid=(columns // wide,),
        in_specs=[spec(rows, wide)] * 3,
        out_specs=[spec(rows, wide)] * 3,
        out_shape=(shape(rows, columns),) * 3,
        compiler_params=PARAMS,
        cost_estimate=pl.CostEstimate(
            flops=4 * rows * columns * rows, bytes_accessed=18 * rows * columns, transcendentals=heads * rows * rows
        ),
        name="own",
    )(queries, keys, values)


def latent_call(where, doc_starts, queries, latent_keys, latent_values, first=0, last=None):
    rows, columns = queries.shape
    latents = latent_keys.shape[0]
    wide = step_of(columns // HD) * HD
    steps = (last or columns // wide) - first
    return pl.pallas_call(
        latent_kernel,
        grid=(steps,),
        in_specs=smem(2) + [pl.BlockSpec((size, wide), lambda h: (0, h + first)) for size in (rows, latents, latents)],
        out_specs=spec(2 * PIECES, wide),
        out_shape=shape(2 * PIECES, steps * wide),
        compiler_params=PARAMS,
        cost_estimate=pl.CostEstimate(
            flops=4 * rows * steps * wide * latents * (1 if first == 0 else 10),
            bytes_accessed=6 * rows * steps * wide,
            transcendentals=steps * wide // HD * rows * latents,
        ),
        name="latent",
    )(where, doc_starts, queries, latent_keys, latent_values)


def four_shards(queries, keys, values, latent_keys, latent_values, pattern, doc_starts, doc_owner):
    rows, columns = queries.shape
    heads = columns // HD
    step = step_of(heads)
    wide = step * HD
    slots = heads * BLK
    blocks = rows // BLK
    docs = 2 * PIECES // blocks
    where = lax.axis_index("seq").astype(jnp.int32).reshape(1)
    right, left = [(0, 1), (1, 2), (2, 3)], [(1, 0), (2, 1), (3, 2)]

    def move(value, pairs):
        return lax.ppermute(value, "seq", pairs)

    def near(value):
        return [move(value, right), move(value, left)]

    def onward(pair):
        return [move(pair[0], right[1:]), move(pair[1], left[:-1])]

    def part(array, block):
        return array[block * BLK : (block + 1) * BLK]

    def row_spec(block, width=wide):
        return pl.BlockSpec((BLK, width), lambda h: (block, h))

    def weigh_near(near_keys, state):
        return pl.pallas_call(
            functools.partial(near_weigh_kernel, 4),
            grid=(heads // step,),
            in_specs=smem(2) + [spec(rows, wide)] * 6,
            out_specs=[spec(rows, wide)] * 3 + [spec(rows, step * BLK)] * 2,
            out_shape=(shape(rows, columns),) * 3 + (shape(rows, slots, BF16),) * 2,
            input_output_aliases={5: 0, 6: 1, 7: 2},
            compiler_params=PARAMS,
            cost_estimate=pl.CostEstimate(
                flops=4 * rows * columns * BLK, bytes_accessed=20 * rows * columns, transcendentals=2 * heads * rows * BLK
            ),
            name="weigh_near",
        )(where, pattern, queries, *near_keys, *state)

    def weigh_far(far_keys, top, total):
        return pl.pallas_call(
            functools.partial(far_weigh_kernel, 4),
            grid=(heads // step,),
            in_specs=smem(3) + [spec(rows, wide)] * 5,
            out_specs=[spec(rows, wide), spec(rows, step * BLK), spec(2 * PIECES, step * BLK)],
            out_shape=(shape(rows, columns), shape(rows, slots, BF16), shape(2 * PIECES, slots, BF16)),
            compiler_params=PARAMS,
            cost_estimate=pl.CostEstimate(
                flops=2 * rows * columns * BLK, bytes_accessed=22 * rows * columns, transcendentals=heads * rows * BLK
            ),
            name="weigh_far",
        )(where, pattern, doc_starts, queries, *far_keys, top, total)

    def mix(block, acc, scale, weights, near_vals, lat):
        return pl.pallas_call(
            functools.partial(mix_kernel, block),
            grid=(heads // step,),
            in_specs=smem(2)
            + [row_spec(block)] * 2
            + [row_spec(block, step * BLK)] * 2
            + [row_spec(0)] * 2
            + [spec(2 * PIECES, wide)],
            out_specs=[row_spec(0), spec(docs, wide)],
            out_shape=(shape(BLK, columns), shape(docs, columns)),
            compiler_params=PARAMS,
            cost_estimate=pl.CostEstimate(flops=4 * BLK * columns * BLK, bytes_accessed=20 * BLK * columns, transcendentals=0),
            name="mix",
        )(where, doc_starts, acc, scale, *weights, *near_vals, lat)

    def finish(block, acc, weights, far_vals, context):
        held = [] if context is None else [context]
        anywhere = pl.BlockSpec(memory_space=pl.ANY)
        return pl.pallas_call(
            functools.partial(context_kernel, block),
            in_specs=smem(1) + vmem(4) + [anywhere] * len(held),
            out_specs=anywhere,
            out_shape=shape(rows, columns, BF16),
            scratch_shapes=[pltpu.VMEM((BLK, columns), BF16), pltpu.SemaphoreType.DMA((heads // 2,))],
            input_output_aliases={5: 0} if held else {},
            compiler_params=PARAMS,
            cost_estimate=pl.CostEstimate(flops=2 * BLK * columns * BLK, bytes_accessed=14 * BLK * columns, transcendentals=0),
            name="finish",
        )(where, acc, weights, *far_vals, *held)

    near_keys = near(keys)
    lats = [latent_call(where, doc_starts, queries, latent_keys, latent_values, 0, 1)]
    lats, late_vals, late_queries = lax.optimization_barrier((lats, values, queries))
    near_vals = [near(part(late_vals, 0))]
    state = own_call(late_queries, keys, values)
    near_keys, state = lax.optimization_barrier((near_keys, state))
    far_keys = onward(near_keys)
    near_vals[0], late_vals, late_queries = lax.optimization_barrier((near_vals[0], late_vals, late_queries))
    lats.append(latent_call(where, doc_starts, late_queries, latent_keys, latent_values, 1))
    lat = jnp.concatenate(lats, axis=1)
    near_vals.append(near(part(late_vals, 1)))
    acc, top, total, *near_weights = weigh_near(near_keys, state)
    far_keys, lat, top = lax.optimization_barrier((far_keys, lat, top))
    weighed = weigh_far(far_keys, top, total)
    near_vals[0], weighed = lax.optimization_barrier((near_vals[0], weighed))
    scale, far_weights, sums = weighed
    sums = move(sums, [(s, s ^ 2) for s in range(4)])
    far_vals = [onward(near_vals[0])]
    parts = pl.pallas_call(
        part_kernel,
        grid=(heads // step,),
        in_specs=smem(2) + [spec(2 * PIECES, step * BLK), spec(rows, wide)],
        out_specs=spec(2 * PIECES, wide),
        out_shape=shape(2 * PIECES, columns),
        compiler_params=PARAMS,
        cost_estimate=pl.CostEstimate(flops=64 * rows * columns * 32, bytes_accessed=3 * rows * columns, transcendentals=0),
        name="part",
    )(where, doc_starts, sums, values)
    mixed = [mix(0, acc, scale, near_weights, near_vals[0], lat)]
    near_vals[1], parts, mixed[0] = lax.optimization_barrier((near_vals[1], parts, mixed[0]))
    far_vals.append(onward(near_vals[1]))
    mixed.append(mix(1, acc, scale, near_weights, near_vals[1], lat))
    context = finish(0, mixed[0][0], far_weights, far_vals[0], None)
    sent = pl.pallas_call(
        route_kernel,
        in_specs=smem(2) + vmem(3),
        out_specs=vmem(4),
        out_shape=(shape(4, columns, BF16),) * 4,
        compiler_params=PARAMS,
        name="route",
    )(where, doc_owner, parts, *[m[1] for m in mixed])
    sent, context = lax.optimization_barrier((sent, context))
    got = [sent[0]] + [move(sent[r], [(s, (s + r) % 4) for s in range(4)]) for r in range(1, 4)]
    context = finish(1, mixed[1][0], far_weights, far_vals[1], context)
    got, context = lax.optimization_barrier((got, context))
    pooled = pl.pallas_call(
        pool_kernel,
        in_specs=smem(1) + vmem(4),
        out_specs=pl.BlockSpec(memory_space=pltpu.VMEM),
        out_shape=jax.ShapeDtypeStruct((1, 4, 2, columns), BF16),
        compiler_params=PARAMS,
        name="pool",
    )(where, *got)
    return context, pooled


def body(queries, keys, values, latent_keys, latent_values, pattern, doc_starts, doc_owner):
    rows, columns = queries.shape
    heads = columns // HD
    shards = lax.axis_size("seq")
    seq_index = lax.axis_index("seq")
    where = seq_index.astype(jnp.int32).reshape(1)
    levels = [j for j in range(LEVELS) if 2**j < shards]
    last = levels[-1]
    merged = 2 * 2**last >= shards
    rotate = shards <= 4

    def both_ways(value, distance):
        behind = lax.ppermute(value, "seq", [(s, s + distance) for s in range(shards - distance)])
        ahead = lax.ppermute(value, "seq", [(s, s - distance) for s in range(distance, shards)])
        return [behind, ahead]

    def far(value, near):
        if last != 1:
            return both_ways(value, 2**last)
        behind = lax.ppermute(near[0], "seq", [(s, s + 1) for s in range(1, shards - 1)])
        ahead = lax.ppermute(near[1], "seq", [(s, s - 1) for s in range(1, shards - 1)])
        return [behind, ahead]

    if shards == 4:
        return four_shards(queries, keys, values, latent_keys, latent_values, pattern, doc_starts, doc_owner)
    near_keys = both_ways(keys, 1)
    near_vals = both_ways(values, 1)
    state_shapes = (shape(rows, columns),) * 3
    lat = latent_call(where, doc_starts, queries, latent_keys, latent_values)
    state = own_call(queries, keys, values)
    near_keys, state = lax.optimization_barrier((near_keys, state))

    for level in levels[:-1]:
        if level == 0:
            got = near_keys + near_vals
        else:
            got = both_ways(keys, 2**level) + both_ways(values, 2**level)
        state = pl.pallas_call(
            functools.partial(near_kernel, shards, level),
            grid=(heads,),
            in_specs=smem(2) + [spec(rows)] * 8,
            out_specs=[spec(rows)] * 3,
            out_shape=state_shapes,
            input_output_aliases={7 + i: i for i in range(3)},
            compiler_params=PARAMS,
            cost_estimate=pl.CostEstimate(
                flops=8 * rows * columns * BLK, bytes_accessed=20 * rows * columns * 2, transcendentals=2 * heads * rows * BLK
            ),
            name="near",
        )(where, pattern, queries, *got, *state)

    far_keys = far(keys, near_keys)
    far_vals = far(values, near_vals)
    sources = 1 if merged else 2
    acc, *weights = pl.pallas_call(
        functools.partial(far_kernel, shards, last, merged),
        grid=(heads,),
        in_specs=smem(2) + [spec(rows)] * 6,
        out_specs=[spec(rows)] + [spec(rows, BLK)] * sources,
        out_shape=(shape(rows, columns),) + (shape(rows, heads * BLK, BF16),) * sources,
        input_output_aliases={5: 0},
        compiler_params=PARAMS,
        cost_estimate=pl.CostEstimate(
            flops=2 * sources * rows * columns * BLK,
            bytes_accessed=(10 + 3 * sources) * rows * columns * 2,
            transcendentals=sources * heads * rows * BLK,
        ),
        name="far",
    )(where, pattern, queries, *far_keys, *state)

    if rotate:
        sent = (shape(2, columns, BF16),) * shards
    else:
        sent = (jax.ShapeDtypeStruct((shards, 2, columns), BF16),)
    context, *means = pl.pallas_call(
        functools.partial(finish_kernel, shards, last, merged),
        in_specs=smem(3) + vmem(4 + sources),
        out_specs=vmem(1 + len(sent)),
        out_shape=(shape(rows, columns, BF16),) + sent,
        compiler_params=PARAMS,
        cost_estimate=pl.CostEstimate(
            flops=2 * sources * rows * columns * BLK, bytes_accessed=(3 + 3 * sources) * rows * columns * 2, transcendentals=0
        ),
        name="finish",
    )(where, doc_starts, doc_owner, acc, lat, *weights, *far_vals)

    if not rotate:
        return context, lax.all_to_all(means[0], "seq", split_axis=0, concat_axis=0, tiled=True)[None]
    got = [means[0]]
    for r in range(1, shards):
        got.append(lax.ppermute(means[r], "seq", [(s, (s + r) % shards) for s in range(shards)]))
    pooled = []
    for s in range(shards):
        back = lax.rem(seq_index - s + shards, shards)
        row = got[0]
        for r in range(1, shards):
            row = jnp.where(back == r, got[r], row)
        pooled.append(row)
    return context, jnp.stack(pooled)[None]


def solution(mesh):
    in_specs = (
        P(("groups", "seq"), ("head", "sub")),
        P(("groups", "seq"), ("head", "sub")),
        P(("groups", "seq"), ("head", "sub")),
        P("groups", ("head", "sub")),
        P("groups", ("head", "sub")),
        P(("groups", "seq"), None),
        P("groups"),
        P("groups"),
    )
    out_specs = (
        P(("groups", "seq"), ("head", "sub")),
        P(("groups", "seq"), None, None, ("head", "sub")),
    )
    return jax.shard_map(body, mesh=mesh, in_specs=in_specs, out_specs=out_specs, check_vma=False)
```

```python
import functools
import math

import jax
import jax.numpy as jnp
from jax import lax
from jax.experimental import pallas as pl
from jax.experimental.pallas import tpu as pltpu
from jax.sharding import PartitionSpec as P

HD = 128
LEVELS = 4
BLK = 256
PIECES = 4
SCALE = math.log2(math.e) / math.sqrt(HD)
PARAMS = pltpu.CompilerParams(vmem_limit_bytes=24 * 1024 * 1024)
F32 = jnp.float32
BF16 = jnp.bfloat16


def dot_t(a, b):
    return lax.dot_general(a, b, (((1,), (1,)), ((), ())), preferred_element_type=F32)


def dot(a, b):
    return jnp.dot(a, b, preferred_element_type=F32)


def doc_rows(rows, split):
    place = lax.broadcasted_iota(jnp.int32, rows.shape, 0)
    first = jnp.sum(jnp.where(place < split, rows, 0.0), axis=0, keepdims=True)
    second = jnp.sum(jnp.where(place < split, 0.0, rows), axis=0, keepdims=True)
    return jnp.concatenate((first, second), axis=0)


def own_kernel(q_ref, k_ref, v_ref, acc_ref, top_ref, sum_ref):
    for h in range(q_ref.shape[1] // HD):
        head = slice(h * HD, (h + 1) * HD)
        s = dot_t(q_ref[:, head], k_ref[:, head]) * SCALE
        top = jnp.max(s, axis=1, keepdims=True)
        e = jnp.exp2(s - top)
        acc = dot(e.astype(BF16), v_ref[:, head])
        acc_ref[:, head] = acc
        top_ref[:, head] = jnp.broadcast_to(top, acc.shape)
        sum_ref[:, head] = jnp.broadcast_to(jnp.sum(e, axis=1, keepdims=True), acc.shape)


def latent_kernel(where, starts, q_ref, lk_ref, lv_ref, lat_ref):
    for h in range(q_ref.shape[1] // HD):
        head = slice(h * HD, (h + 1) * HD)
        s = dot_t(q_ref[:, head], lk_ref[:, head]) * SCALE
        e = jnp.exp2(s - jnp.max(s, axis=1, keepdims=True))
        out = dot(e.astype(BF16), lv_ref[:, head]) / jnp.sum(e, axis=1, keepdims=True)
        piece = out.shape[0] // PIECES
        for p in range(PIECES):
            split = split_of(where, starts, p)
            lat_ref[2 * p : 2 * p + 2, head] = doc_rows(out[p * piece : (p + 1) * piece], split)


def split_of(where, starts, p, shard=None):
    first = 2 * (PIECES * (where[0] if shard is None else shard) + p)
    return starts[first + 1] - starts[first]


def slot_live(where, pattern, shards, level, side, block):
    partner = where[0] + (2 * side - 1) * 2**level
    return (pattern[block, 2 * level + side] == 1) & (partner >= 0) & (partner < shards)


def live_scores(live, q, k):
    return jnp.where(live, dot_t(q, k) * SCALE, -jnp.inf)


def near_kernel(shards, level, where, pattern, q_ref, kb_ref, ka_ref, vb_ref, va_ref, *refs):
    acc_in, top_in, sum_in, acc_ref, top_ref, sum_ref = refs
    for block in range(q_ref.shape[0] // BLK):
        rows = pl.ds(block * BLK, BLK)
        q = q_ref[rows, :]
        scores = [
            live_scores(slot_live(where, pattern, shards, level, side, block), q, k_ref[rows, :])
            for side, k_ref in enumerate((kb_ref, ka_ref))
        ]
        old = top_in[rows, :1]
        top = old
        for s in scores:
            top = jnp.maximum(top, jnp.max(s, axis=1, keepdims=True))
        shrink = jnp.exp2(old - top)
        total = sum_in[rows, :1] * shrink
        acc = acc_in[rows, :] * shrink
        for s, v_ref in zip(scores, (vb_ref, va_ref)):
            e = jnp.exp2(s - top)
            total = total + jnp.sum(e, axis=1, keepdims=True)
            acc = acc + dot(e.astype(BF16), v_ref[rows, :])
        acc_ref[rows, :] = acc
        top_ref[rows, :] = jnp.broadcast_to(top, acc.shape)
        sum_ref[rows, :] = jnp.broadcast_to(total, acc.shape)


def far_kernel(shards, level, merged, where, pattern, q_ref, kb_ref, ka_ref, acc_in, top_in, sum_in, acc_ref, *outs):
    behind = where[0] >= 2**level
    for block in range(q_ref.shape[0] // BLK):
        rows = pl.ds(block * BLK, BLK)
        q = q_ref[rows, :]
        live = [slot_live(where, pattern, shards, level, side, block) for side in range(2)]
        pair = [k_ref[rows, :] for k_ref in (kb_ref, ka_ref)]
        if merged:
            live = [(behind & live[0]) | (jnp.logical_not(behind) & live[1])]
            pair = [jnp.where(behind, pair[0], pair[1])]
        scores = [live_scores(on, q, k) for on, k in zip(live, pair)]
        old = top_in[rows, :1]
        top = old
        for s in scores:
            top = jnp.maximum(top, jnp.max(s, axis=1, keepdims=True))
        shrink = jnp.exp2(old - top)
        total = sum_in[rows, :1] * shrink
        exps = []
        for s in scores:
            e = jnp.exp2(s - top)
            total = total + jnp.sum(e, axis=1, keepdims=True)
            exps.append(e)
        inverse = 1.0 / total
        acc_ref[rows, :] = acc_in[rows, :] * (shrink * inverse)
        for e, out in zip(exps, outs):
            out[rows, :] = (e * inverse).astype(BF16)


def finish_kernel(shards, level, merged, where, starts, owners, acc_ref, lat_ref, *refs):
    sources = 1 if merged else 2
    weights, (vb_ref, va_ref) = refs[:sources], refs[sources : sources + 2]
    ctx_ref, outs = refs[sources + 2], refs[sources + 3 :]
    rows_here, columns = acc_ref.shape
    piece = rows_here // PIECES
    splits = [split_of(where, starts, p) for p in range(PIECES)]
    behind = where[0] >= 2**level
    sums = []
    for h in range(columns // HD):
        head = pl.ds(h * HD, HD)
        slots = pl.ds(h * BLK, BLK)
        found = []
        for block in range(rows_here // BLK):
            rows = pl.ds(block * BLK, BLK)
            pair = [v_ref[rows, head] for v_ref in (vb_ref, va_ref)]
            if merged:
                pair = [jnp.where(behind, pair[0], pair[1])]
            acc = acc_ref[rows, head]
            for w_ref, v in zip(weights, pair):
                acc = acc + dot(w_ref[rows, slots], v)
            ctx = acc.astype(BF16)
            ctx_ref[rows, head] = ctx
            ctx = ctx.astype(F32)
            for start in range(0, BLK, piece):
                found.append(doc_rows(ctx[start : start + piece], splits[len(found)]))
        sums.append(found)
    side = lax.broadcasted_iota(jnp.int32, (2, columns), 0)
    means = []
    for p in range(PIECES):
        count = jnp.where(side == 0, splits[p], piece - splits[p]).astype(F32)
        total = jnp.concatenate([found[p] for found in sums], axis=1) + lat_ref[2 * p : 2 * p + 2, :]
        means.append(total / count)
    for r in range(shards):
        if len(outs) == 1:
            target = r
        else:
            target = lax.rem(where[0] + r, shards)
        chosen = jnp.zeros((2, columns), F32)
        for p in range(PIECES):
            chosen = jnp.where(owners[2 * (PIECES * where[0] + p)] == target, means[p], chosen)
        if len(outs) == 1:
            outs[0][r] = chosen.astype(BF16)
        else:
            outs[r][...] = chosen.astype(BF16)


def live_bias(where, pattern, shards, level, side, block):
    return jnp.where(slot_live(where, pattern, shards, level, side, block), 0.0, -jnp.inf)


def halves(s, bias):
    return [s[:, i : i + HD] * SCALE + bias for i in range(0, BLK, HD)]


def near_weigh_kernel(shards, where, pattern, q_ref, nb_ref, na_ref, acc_in, top_in, sum_in, *refs):
    acc_ref, top_ref, sum_ref, wb_ref, wa_ref = refs
    biases = [[live_bias(where, pattern, shards, 0, side, block) for side in range(2)] for block in range(q_ref.shape[0] // BLK)]
    piece = q_ref.shape[0] // PIECES
    for h in range(q_ref.shape[1] // HD):
        head = slice(h * HD, (h + 1) * HD)
        for p in range(PIECES):
            rows = slice(p * piece, (p + 1) * piece)
            block = p * piece // BLK
            held = slice(block * BLK, (block + 1) * BLK)
            q = q_ref[rows, head]
            scores = [halves(dot_t(q, k_ref[held, head]), bias) for k_ref, bias in zip((nb_ref, na_ref), biases[block])]
            old = top_in[rows, head]
            top = jnp.max(functools.reduce(jnp.maximum, scores[0] + scores[1]), axis=1, keepdims=True)
            top = jnp.maximum(top, old)
            shrink = jnp.exp2(old - top)
            exps = [[jnp.exp2(x - top) for x in pair] for pair in scores]
            added = jnp.sum(functools.reduce(jnp.add, exps[0] + exps[1]), axis=1, keepdims=True)
            top_ref[rows, head] = top
            sum_ref[rows, head] = sum_in[rows, head] * shrink + added
            acc_ref[rows, head] = acc_in[rows, head] * shrink
            for pair, out in zip(exps, (wb_ref, wa_ref)):
                for i, e in enumerate(pair):
                    first = h * BLK + i * HD
                    out[rows, first : first + HD] = e.astype(BF16)


def far_weigh_kernel(shards, where, pattern, starts, q_ref, fb_ref, fa_ref, top_in, sum_in, scale_ref, wf_ref, sums_ref):
    behind = where[0] >= 2
    biases = []
    for block in range(q_ref.shape[0] // BLK):
        pair = [live_bias(where, pattern, shards, 1, side, block) for side in range(2)]
        biases.append(jnp.where(behind, pair[0], pair[1]))
    piece = q_ref.shape[0] // PIECES
    place = lax.broadcasted_iota(jnp.int32, (piece, HD), 0)
    firsts = [place < split_of(where, starts, p) for p in range(PIECES)]
    for h in range(q_ref.shape[1] // HD):
        head = slice(h * HD, (h + 1) * HD)
        sums = [[] for _ in range(BLK // HD)]
        for p in range(PIECES):
            rows = slice(p * piece, (p + 1) * piece)
            block = p * piece // BLK
            held = slice(block * BLK, (block + 1) * BLK)
            keys = jnp.where(behind, fb_ref[held, head], fa_ref[held, head])
            scores = halves(dot_t(q_ref[rows, head], keys), biases[block])
            old = top_in[rows, head]
            top = jnp.maximum(jnp.max(functools.reduce(jnp.maximum, scores), axis=1, keepdims=True), old)
            shrink = jnp.exp2(old - top)
            exps = [jnp.exp2(x - top) for x in scores]
            added = jnp.sum(functools.reduce(jnp.add, exps), axis=1, keepdims=True)
            inverse = 1.0 / (sum_in[rows, head] * shrink + added)
            scale_ref[rows, head] = shrink * inverse
            for i, e in enumerate(exps):
                first = h * BLK + i * HD
                w = e * inverse
                wf_ref[rows, first : first + HD] = w.astype(BF16)
                sums[i] += [
                    jnp.sum(jnp.where(firsts[p], w, 0.0), axis=0, keepdims=True),
                    jnp.sum(jnp.where(firsts[p], 0.0, w), axis=0, keepdims=True),
                ]
        for i, found in enumerate(sums):
            first = h * BLK + i * HD
            sums_ref[:, first : first + HD] = jnp.concatenate(found, axis=0).astype(sums_ref.dtype)


def doc_counts(split, piece, columns):
    side = lax.broadcasted_iota(jnp.int32, (2, columns), 0)
    return jnp.where(side == 0, split, piece - split).astype(F32)


def mix_kernel(block, where, starts, acc_in, scale_in, wb_ref, wa_ref, vb_ref, va_ref, lat_ref, acc_ref, mean_ref):
    pieces = mean_ref.shape[0] // 2
    piece = BLK // pieces
    for h in range(acc_in.shape[1] // HD):
        head = slice(h * HD, (h + 1) * HD)
        slots = slice(h * BLK, (h + 1) * BLK)
        acc = acc_in[:, head] + dot(wb_ref[:, slots], vb_ref[:, head]) + dot(wa_ref[:, slots], va_ref[:, head])
        acc = acc * scale_in[:, head]
        acc_ref[:, head] = acc
        for p in range(pieces):
            index = block * pieces + p
            split = split_of(where, starts, index)
            found = doc_rows(acc[p * piece : (p + 1) * piece], split) + lat_ref[2 * index : 2 * index + 2, head]
            mean_ref[2 * p : 2 * p + 2, head] = found / doc_counts(split, piece, HD)


def part_kernel(where, starts, sums_ref, v_ref, part_ref):
    rows_here = v_ref.shape[0]
    piece = rows_here // PIECES
    pieces = part_ref.shape[0] // 2
    partner = lax.rem(where[0] + 2, 4)
    counts = [doc_counts(split_of(where, starts, PIECES - pieces + p, partner), piece, HD) for p in range(pieces)]
    for h in range(v_ref.shape[1] // HD):
        head = slice(h * HD, (h + 1) * HD)
        found = dot(sums_ref[:, h * BLK : (h + 1) * BLK], v_ref[rows_here - BLK :, head])
        for p in range(pieces):
            rows = slice(2 * p, 2 * p + 2)
            part_ref[rows, head] = found[rows] / counts[p]


def route_kernel(where, owners, part_ref, *refs):
    mean_refs, out_refs = refs[:-4], refs[-4:]
    here, partner = where[0], lax.rem(where[0] + 2, 4)
    means = jnp.concatenate([mean_ref[...] for mean_ref in mean_refs], axis=0)
    parts = part_ref[...]
    for r, out_ref in enumerate(out_refs):
        target = lax.rem(here + r, 4)
        rows = []
        for group, shard in ((means, here), (parts, partner)):
            chosen = jnp.zeros((2, out_ref.shape[1]), F32)
            count = group.shape[0] // 2
            for p in range(count):
                mine = owners[2 * (PIECES * shard + PIECES - count + p)] == target
                chosen = jnp.where(mine, group[2 * p : 2 * p + 2], chosen)
            rows.append(chosen)
        out_ref[...] = jnp.concatenate(rows, axis=0).astype(BF16)


def pool_kernel(where, *refs):
    got, out_ref = [ref[...].astype(F32) for ref in refs[:4]], refs[4]
    for s in range(4):
        rows = []
        for first, shard in ((0, s), (2, s ^ 2)):
            back = lax.rem(where[0] - shard + 4, 4)
            found = got[0][first : first + 2]
            for r in range(1, 4):
                found = jnp.where(back == r, got[r][first : first + 2], found)
            rows.append(found)
        out_ref[0, s] = (rows[0] + rows[1]).astype(BF16)


def context_kernel(block, where, starts, acc_ref, w_ref, vb_ref, va_ref, *refs):
    if block == 0:
        mean_in, out_ref, mean_ref, stage, sem = refs
    else:
        _, out_ref, stage, sem = refs
    behind = where[0] >= 2
    copies = []
    for h in range(acc_ref.shape[1] // HD):
        head = pl.ds(h * HD, HD)
        v = jnp.where(behind, vb_ref[:, head], va_ref[:, head])
        found = dot(w_ref[pl.ds(block * BLK, BLK), pl.ds(h * BLK, BLK)], v)
        stage[:, head] = (acc_ref[:, head] + found).astype(BF16)
        if block == 0:
            pieces = mean_ref.shape[0] // 2
            piece = BLK // pieces
            for p in range(pieces):
                split = split_of(where, starts, p)
                far = doc_rows(found[p * piece : (p + 1) * piece], split) / doc_counts(split, piece, HD)
                mean_ref[2 * p : 2 * p + 2, head] = mean_in[2 * p : 2 * p + 2, head] + far
        if h % 2:
            pair = pl.ds((h - 1) * HD, 2 * HD)
            copy = pltpu.make_async_copy(stage.at[:, pair], out_ref.at[pl.ds(block * BLK, BLK), pair], sem.at[h // 2])
            copy.start()
            copies.append(copy)
    for copy in copies:
        copy.wait()


def spec(rows, columns=HD):
    return pl.BlockSpec((rows, columns), lambda h: (0, h))


def smem(count):
    return [pl.BlockSpec(memory_space=pltpu.SMEM)] * count


def vmem(count):
    return [pl.BlockSpec(memory_space=pltpu.VMEM)] * count


def shape(rows, columns, kind=F32):
    return jax.ShapeDtypeStruct((rows, columns), kind)


def step_of(heads):
    return 2 if heads % 2 == 0 else 1


def own_call(queries, keys, values):
    rows, columns = queries.shape
    heads = columns // HD
    wide = step_of(heads) * HD
    return pl.pallas_call(
        own_kernel,
        grid=(columns // wide,),
        in_specs=[spec(rows, wide)] * 3,
        out_specs=[spec(rows, wide)] * 3,
        out_shape=(shape(rows, columns),) * 3,
        compiler_params=PARAMS,
        cost_estimate=pl.CostEstimate(
            flops=4 * rows * columns * rows, bytes_accessed=18 * rows * columns, transcendentals=heads * rows * rows
        ),
        name="own",
    )(queries, keys, values)


def latent_call(where, doc_starts, queries, latent_keys, latent_values, first=0, last=None):
    rows, columns = queries.shape
    latents = latent_keys.shape[0]
    wide = step_of(columns // HD) * HD
    steps = (last or columns // wide) - first
    return pl.pallas_call(
        latent_kernel,
        grid=(steps,),
        in_specs=smem(2) + [pl.BlockSpec((size, wide), lambda h: (0, h + first)) for size in (rows, latents, latents)],
        out_specs=spec(2 * PIECES, wide),
        out_shape=shape(2 * PIECES, steps * wide),
        compiler_params=PARAMS,
        cost_estimate=pl.CostEstimate(
            flops=4 * rows * steps * wide * latents * (1 if first == 0 else 10),
            bytes_accessed=6 * rows * steps * wide,
            transcendentals=steps * wide // HD * rows * latents,
        ),
        name="latent",
    )(where, doc_starts, queries, latent_keys, latent_values)


def four_shards(queries, keys, values, latent_keys, latent_values, pattern, doc_starts, doc_owner):
    rows, columns = queries.shape
    heads = columns // HD
    step = step_of(heads)
    wide = step * HD
    slots = heads * BLK
    blocks = rows // BLK
    docs = 2 * PIECES // blocks
    where = lax.axis_index("seq").astype(jnp.int32).reshape(1)
    right, left = [(0, 1), (1, 2), (2, 3)], [(1, 0), (2, 1), (3, 2)]

    def move(value, pairs):
        return lax.ppermute(value, "seq", pairs)

    def near(value):
        return [move(value, right), move(value, left)]

    def onward(pair):
        return [move(pair[0], right[1:]), move(pair[1], left[:-1])]

    def part(array, block):
        return array[block * BLK : (block + 1) * BLK]

    def row_spec(block, width=wide):
        return pl.BlockSpec((BLK, width), lambda h: (block, h))

    def weigh_near(near_keys, state):
        return pl.pallas_call(
            functools.partial(near_weigh_kernel, 4),
            grid=(heads // step,),
            in_specs=smem(2) + [spec(rows, wide)] * 6,
            out_specs=[spec(rows, wide)] * 3 + [spec(rows, step * BLK)] * 2,
            out_shape=(shape(rows, columns),) * 3 + (shape(rows, slots, BF16),) * 2,
            input_output_aliases={5: 0, 6: 1, 7: 2},
            compiler_params=PARAMS,
            cost_estimate=pl.CostEstimate(
                flops=4 * rows * columns * BLK, bytes_accessed=20 * rows * columns, transcendentals=2 * heads * rows * BLK
            ),
            name="weigh_near",
        )(where, pattern, queries, *near_keys, *state)

    def weigh_far(far_keys, top, total):
        return pl.pallas_call(
            functools.partial(far_weigh_kernel, 4),
            grid=(heads // step,),
            in_specs=smem(3) + [spec(rows, wide)] * 5,
            out_specs=[spec(rows, wide), spec(rows, step * BLK), spec(2 * PIECES, step * BLK)],
            out_shape=(shape(rows, columns), shape(rows, slots, BF16), shape(2 * PIECES, slots, BF16)),
            compiler_params=PARAMS,
            cost_estimate=pl.CostEstimate(
                flops=2 * rows * columns * BLK, bytes_accessed=22 * rows * columns, transcendentals=heads * rows * BLK
            ),
            name="weigh_far",
        )(where, pattern, doc_starts, queries, *far_keys, top, total)

    def mix(block, acc, scale, weights, near_vals, lat):
        return pl.pallas_call(
            functools.partial(mix_kernel, block),
            grid=(heads // step,),
            in_specs=smem(2)
            + [row_spec(block)] * 2
            + [row_spec(block, step * BLK)] * 2
            + [row_spec(0)] * 2
            + [spec(2 * PIECES, wide)],
            out_specs=[row_spec(0), spec(docs, wide)],
            out_shape=(shape(BLK, columns), shape(docs, columns)),
            compiler_params=PARAMS,
            cost_estimate=pl.CostEstimate(flops=4 * BLK * columns * BLK, bytes_accessed=20 * BLK * columns, transcendentals=0),
            name="mix",
        )(where, doc_starts, acc, scale, *weights, *near_vals, lat)

    def finish(block, acc, weights, far_vals, held):
        first = block == 0
        anywhere = pl.BlockSpec(memory_space=pl.ANY)
        context = shape(rows, columns, BF16)
        return pl.pallas_call(
            functools.partial(context_kernel, block),
            in_specs=smem(2) + vmem(4) + (vmem(1) if first else [anywhere]),
            out_specs=[anywhere] + vmem(1) if first else anywhere,
            out_shape=(context, shape(docs, columns)) if first else context,
            scratch_shapes=[pltpu.VMEM((BLK, columns), BF16), pltpu.SemaphoreType.DMA((heads // 2,))],
            input_output_aliases={} if first else {6: 0},
            compiler_params=PARAMS,
            cost_estimate=pl.CostEstimate(flops=2 * BLK * columns * BLK, bytes_accessed=14 * BLK * columns, transcendentals=0),
            name="finish",
        )(where, doc_starts, acc, weights, *far_vals, held)

    near_keys = near(keys)
    lats = [latent_call(where, doc_starts, queries, latent_keys, latent_values, 0, 1)]
    lats, late_vals, late_queries = lax.optimization_barrier((lats, values, queries))
    near_vals = [near(part(late_vals, 0))]
    state = own_call(late_queries, keys, values)
    near_keys, state = lax.optimization_barrier((near_keys, state))
    far_keys = onward(near_keys)
    near_vals[0], late_vals, late_queries = lax.optimization_barrier((near_vals[0], late_vals, late_queries))
    lats.append(latent_call(where, doc_starts, late_queries, latent_keys, latent_values, 1))
    lat = jnp.concatenate(lats, axis=1)
    near_vals.append(near(part(late_vals, 1)))
    acc, top, total, *near_weights = weigh_near(near_keys, state)
    far_keys, lat, top = lax.optimization_barrier((far_keys, lat, top))
    weighed = weigh_far(far_keys, top, total)
    near_vals[0], weighed = lax.optimization_barrier((near_vals[0], weighed))
    scale, far_weights, sums = weighed
    sums = move(sums[docs:], [(s, s ^ 2) for s in range(4)])
    far_vals = [onward(near_vals[0])]
    parts = pl.pallas_call(
        part_kernel,
        grid=(heads // step,),
        in_specs=smem(2) + [spec(docs, step * BLK), spec(rows, wide)],
        out_specs=spec(docs, wide),
        out_shape=shape(docs, columns),
        compiler_params=PARAMS,
        cost_estimate=pl.CostEstimate(flops=64 * rows * columns * 32, bytes_accessed=3 * rows * columns, transcendentals=0),
        name="part",
    )(where, doc_starts, sums, values)
    mixed = [mix(0, acc, scale, near_weights, near_vals[0], lat)]
    near_vals[1], parts, mixed[0] = lax.optimization_barrier((near_vals[1], parts, mixed[0]))
    far_vals.append(onward(near_vals[1]))
    mixed.append(mix(1, acc, scale, near_weights, near_vals[1], lat))
    context, mean = finish(0, mixed[0][0], far_weights, far_vals[0], mixed[0][1])
    sent = pl.pallas_call(
        route_kernel,
        in_specs=smem(2) + vmem(3),
        out_specs=vmem(4),
        out_shape=(shape(4, columns, BF16),) * 4,
        compiler_params=PARAMS,
        name="route",
    )(where, doc_owner, parts, mean, mixed[1][1])
    sent, context = lax.optimization_barrier((sent, context))
    got = [sent[0]] + [move(sent[r], [(s, (s + r) % 4) for s in range(4)]) for r in range(1, 4)]
    context = finish(1, mixed[1][0], far_weights, far_vals[1], context)
    got, context = lax.optimization_barrier((got, context))
    pooled = pl.pallas_call(
        pool_kernel,
        in_specs=smem(1) + vmem(4),
        out_specs=pl.BlockSpec(memory_space=pltpu.VMEM),
        out_shape=jax.ShapeDtypeStruct((1, 4, 2, columns), BF16),
        compiler_params=PARAMS,
        name="pool",
    )(where, *got)
    return context, pooled


def body(queries, keys, values, latent_keys, latent_values, pattern, doc_starts, doc_owner):
    rows, columns = queries.shape
    heads = columns // HD
    shards = lax.axis_size("seq")
    seq_index = lax.axis_index("seq")
    where = seq_index.astype(jnp.int32).reshape(1)
    levels = [j for j in range(LEVELS) if 2**j < shards]
    last = levels[-1]
    merged = 2 * 2**last >= shards
    rotate = shards <= 4

    def both_ways(value, distance):
        behind = lax.ppermute(value, "seq", [(s, s + distance) for s in range(shards - distance)])
        ahead = lax.ppermute(value, "seq", [(s, s - distance) for s in range(distance, shards)])
        return [behind, ahead]

    def far(value, near):
        if last != 1:
            return both_ways(value, 2**last)
        behind = lax.ppermute(near[0], "seq", [(s, s + 1) for s in range(1, shards - 1)])
        ahead = lax.ppermute(near[1], "seq", [(s, s - 1) for s in range(1, shards - 1)])
        return [behind, ahead]

    if shards == 4:
        return four_shards(queries, keys, values, latent_keys, latent_values, pattern, doc_starts, doc_owner)
    near_keys = both_ways(keys, 1)
    near_vals = both_ways(values, 1)
    state_shapes = (shape(rows, columns),) * 3
    lat = latent_call(where, doc_starts, queries, latent_keys, latent_values)
    state = own_call(queries, keys, values)
    near_keys, state = lax.optimization_barrier((near_keys, state))

    for level in levels[:-1]:
        if level == 0:
            got = near_keys + near_vals
        else:
            got = both_ways(keys, 2**level) + both_ways(values, 2**level)
        state = pl.pallas_call(
            functools.partial(near_kernel, shards, level),
            grid=(heads,),
            in_specs=smem(2) + [spec(rows)] * 8,
            out_specs=[spec(rows)] * 3,
            out_shape=state_shapes,
            input_output_aliases={7 + i: i for i in range(3)},
            compiler_params=PARAMS,
            cost_estimate=pl.CostEstimate(
                flops=8 * rows * columns * BLK, bytes_accessed=20 * rows * columns * 2, transcendentals=2 * heads * rows * BLK
            ),
            name="near",
        )(where, pattern, queries, *got, *state)

    far_keys = far(keys, near_keys)
    far_vals = far(values, near_vals)
    sources = 1 if merged else 2
    acc, *weights = pl.pallas_call(
        functools.partial(far_kernel, shards, last, merged),
        grid=(heads,),
        in_specs=smem(2) + [spec(rows)] * 6,
        out_specs=[spec(rows)] + [spec(rows, BLK)] * sources,
        out_shape=(shape(rows, columns),) + (shape(rows, heads * BLK, BF16),) * sources,
        input_output_aliases={5: 0},
        compiler_params=PARAMS,
        cost_estimate=pl.CostEstimate(
            flops=2 * sources * rows * columns * BLK,
            bytes_accessed=(10 + 3 * sources) * rows * columns * 2,
            transcendentals=sources * heads * rows * BLK,
        ),
        name="far",
    )(where, pattern, queries, *far_keys, *state)

    if rotate:
        sent = (shape(2, columns, BF16),) * shards
    else:
        sent = (jax.ShapeDtypeStruct((shards, 2, columns), BF16),)
    context, *means = pl.pallas_call(
        functools.partial(finish_kernel, shards, last, merged),
        in_specs=smem(3) + vmem(4 + sources),
        out_specs=vmem(1 + len(sent)),
        out_shape=(shape(rows, columns, BF16),) + sent,
        compiler_params=PARAMS,
        cost_estimate=pl.CostEstimate(
            flops=2 * sources * rows * columns * BLK, bytes_accessed=(3 + 3 * sources) * rows * columns * 2, transcendentals=0
        ),
        name="finish",
    )(where, doc_starts, doc_owner, acc, lat, *weights, *far_vals)

    if not rotate:
        return context, lax.all_to_all(means[0], "seq", split_axis=0, concat_axis=0, tiled=True)[None]
    got = [means[0]]
    for r in range(1, shards):
        got.append(lax.ppermute(means[r], "seq", [(s, (s + r) % shards) for s in range(shards)]))
    pooled = []
    for s in range(shards):
        back = lax.rem(seq_index - s + shards, shards)
        row = got[0]
        for r in range(1, shards):
            row = jnp.where(back == r, got[r], row)
        pooled.append(row)
    return context, jnp.stack(pooled)[None]


def solution(mesh):
    in_specs = (
        P(("groups", "seq"), ("head", "sub")),
        P(("groups", "seq"), ("head", "sub")),
        P(("groups", "seq"), ("head", "sub")),
        P("groups", ("head", "sub")),
        P("groups", ("head", "sub")),
        P(("groups", "seq"), None),
        P("groups"),
        P("groups"),
    )
    out_specs = (
        P(("groups", "seq"), ("head", "sub")),
        P(("groups", "seq"), None, None, ("head", "sub")),
    )
    return jax.shard_map(body, mesh=mesh, in_specs=in_specs, out_specs=out_specs, check_vma=False)
```
